32 devices in a mesh: dp: 8 (over z, x), tensor: 4 (over y, core).
Axes of the slice: x: 2, y: 2, z: 4, core: 2. Of those that a mesh axis runs over, the one named last changes fastest.
Arguments:
- tokens: bfloat16 [8, 2048, 768], P('dp', 'tensor'), may hold values from -6 to 6
- segment_ids: int32 [8, 2048], P('dp'), may hold values from -1 to 5, as said below
- query_weight: bfloat16 [768, 768], P(None, 'tensor'), may hold values from -0.21875 to 0.21875
- key_weight: bfloat16 [768, 768], P(None, 'tensor'), may hold values from -0.21875 to 0.21875
- value_weight: bfloat16 [768, 768], P(None, 'tensor'), may hold values from -0.21875 to 0.21875
- output_weight: bfloat16 [768, 768], P('tensor'), may hold values from -3.5 to 3.5
- attn_gain: float32 [768], replicated, may hold values from 0.5 to 1.5
- attn_shift: float32 [768], replicated, may hold values from -3 to 3
- gate_weight: bfloat16 [768, 3072], P(None, 'tensor'), may hold values from -0.21875 to 0.21875
- up_weight: bfloat16 [768, 3072], P(None, 'tensor'), may hold values from -0.21875 to 0.21875
- down_weight: bfloat16 [3072, 768], P('tensor'), may hold values from -0.109375 to 0.109375
- mlp_gain: float32 [768], replicated, may hold values from 0.5 to 1.5
- mlp_shift: float32 [768], replicated, may hold values from -3 to 3
- cotangent: bfloat16 [8, 2048, 768], P('dp', 'tensor'), may hold values from -6 to 6
Outputs:
- encoded: bfloat16 [8, 2048, 768], P('dp', 'tensor')
- grad_tokens: float32 [8, 2048, 768], P('dp', 'tensor')
- grad_query: float32 [768, 768], P(None, 'tensor')
- grad_key: float32 [768, 768], P(None, 'tensor')
- grad_value: float32 [768, 768], P(None, 'tensor')
- grad_output: float32 [768, 768], P('tensor')
- grad_attn_gain: float32 [768], replicated
- grad_attn_shift: float32 [768], replicated
- grad_gate: float32 [768, 3072], P(None, 'tensor')
- grad_up: float32 [768, 3072], P(None, 'tensor')
- grad_down: float32 [3072, 768], P('tensor')
- grad_mlp_gain: float32 [768], replicated
- grad_mlp_shift: float32 [768], replicated
The draws below stay inside these ranges and needn't reach their ends.
Inputs may be any that keep to these rules, and one draw needn't show every extreme that they name: `segment_ids`: each packed row holds documents 0 to 5 in this order, each one or more positions long, followed by one or more padding positions marked -1.
All inputs are finite; a program needn't handle non-finite values.
Results may differ from the reference program's by a relative error of at most 0.019.
Values may be sent and summed in bfloat16 or wider, within the bound.
No kernel may reach another device: no remote copies, remote signals or barrier semaphores. Data moves between devices by JAX's collectives and lax.ppermute only.
A program may use at most 128 MiB of HBM per device.

```python
import math
import jax
import jax.numpy as jnp
from jax import lax

D = 768
HEADS = 12
HEAD_DIM = 64
FF = 3072
ROW_LEN = 2048
NSEG = 6
BATCH = 8


def draw_segment_ids(key, part):
    key = jax.random.fold_in(key, 7)
    first_key, second_key = jax.random.split(key)
    slot_width = ROW_LEN // 32
    longest = jax.random.randint(first_key, (BATCH, 1), 0, 3)
    jitter = jax.random.randint(second_key, (BATCH, NSEG), 0, slot_width // 2)
    cut_number = jnp.arange(1, NSEG + 1, dtype=jnp.int32)[None, :]
    early_cuts = cut_number * slot_width - jitter
    late_cuts = ROW_LEN - (NSEG + 1 - cut_number) * slot_width + jitter
    cuts = jnp.where(cut_number <= longest, early_cuts, late_cuts)
    places = jnp.arange(ROW_LEN, dtype=jnp.int32)
    passed = jnp.sum((cuts[:, :, None] <= places[None, None, :]).astype(jnp.int32), axis=1)
    return jnp.where(passed == NSEG, -1, passed).astype(jnp.int32)


def levels(key, dims, pieces, smallest, high):
    def one(axis_at, blocks):
        heights = jax.random.uniform(jax.random.fold_in(jax.random.fold_in(key, 6), axis_at), (blocks,), jnp.float32, smallest / len(pieces), high / len(pieces))
        return jnp.repeat(jnp.exp(heights), dims[axis_at] // blocks).reshape((-1,) + (1,) * (len(dims) - axis_at - 1))

    loudness = one(*pieces[0])
    for cut in pieces[1:]:
        loudness = loudness * one(*cut)
    return loudness


def noise(own_key, extent, spread, bound, cuts=(), held_as=jnp.bfloat16):
    array = spread * jax.random.normal(own_key, extent, jnp.float32)
    if cuts:
        array = array * levels(own_key, extent, cuts, -0.22, 0.18)
    return jnp.clip(array, -bound, bound).astype(held_as)


def setup_inputs(seed: int = 0) -> dict:
    streams_of = jax.random.split(jax.random.key(seed), 15)
    tokens = noise(streams_of[0], (BATCH, ROW_LEN, D), 1.0, 6.0, ((0, 8), (1, 4)))
    segment_ids = draw_segment_ids(jax.random.fold_in(streams_of[14], 71), 0)
    query_weight = noise(streams_of[2], (D, D), D ** -0.5, 0.21875, ((1, 4),))
    key_weight = noise(streams_of[3], (D, D), D ** -0.5, 0.21875, ((1, 4),))
    value_weight = noise(streams_of[4], (D, D), D ** -0.5, 0.21875, ((1, 4),))
    output_weight = noise(streams_of[5], (D, D), (max(1, D * 8 // ROW_LEN)) ** -0.5, 3.5, ((0, 4),))
    attn_gain = jnp.clip(1.0 + 0.1 * jax.random.normal(streams_of[6], (D,), jnp.float32), 0.5, 1.5)
    attn_shift = noise(streams_of[7], (D,), 0.5, 3.0, (), jnp.float32)
    gate_weight = noise(streams_of[8], (D, FF), D ** -0.5, 0.21875, ((1, 4),))
    up_weight = noise(streams_of[9], (D, FF), D ** -0.5, 0.21875, ((1, 4),))
    down_weight = noise(streams_of[10], (FF, D), FF ** -0.5, 0.109375, ((0, 4),))
    mlp_gain = jnp.clip(1.0 + 0.1 * jax.random.normal(streams_of[11], (D,), jnp.float32), 0.5, 1.5)
    mlp_shift = noise(streams_of[12], (D,), 0.5, 3.0, (), jnp.float32)
    cotangent = noise(streams_of[13], (BATCH, ROW_LEN, D), 1.0, 6.0, ((0, 8), (1, 4)))
    return dict(tokens=tokens, segment_ids=segment_ids, query_weight=query_weight, key_weight=key_weight, value_weight=value_weight, output_weight=output_weight, attn_gain=attn_gain, attn_shift=attn_shift, gate_weight=gate_weight, up_weight=up_weight, down_weight=down_weight, mlp_gain=mlp_gain, mlp_shift=mlp_shift, cotangent=cotangent)


@jax.custom_vjp
def low(v):
    return lax.optimization_barrier(v.astype(jnp.bfloat16)).astype(jnp.float32)

@jax.custom_vjp
def low_back(v):
    return v

def low_keep(v):
    return (low(v), None)

def low_pass(kept, grad):
    return (grad,)

def back_keep(v):
    return (v, None)

def back_low(kept, grad):
    return (low(grad),)
low.defvjp(low_keep, low_pass)
low_back.defvjp(back_keep, back_low)
EPSILON = 1e-05
ROPE_BASE = 1000.0
MASKED = -1000000000.0
query_block = 512

def positions(segments):
    places = jnp.arange(segments.shape[0], dtype=jnp.int32)
    before = jnp.concatenate([segments[:1] - 1, segments[:-1]])
    starts = lax.cummax(jnp.where(segments != before, places, 0), axis=0)
    return (places - starts).astype(jnp.float32)

def rotary_tables(segments):
    half_dim = HEAD_DIM // 2
    angle_rate = ROPE_BASE ** (-(jnp.arange(half_dim, dtype=jnp.float32) * 2.0 / HEAD_DIM))
    angles = positions(segments)[:, None] * angle_rate[None, :]
    return (jnp.cos(angles), jnp.sin(angles))

def rotate(tensor, cosine_table, sine_table):
    half_dim = tensor.shape[-1] // 2
    first_half = tensor[..., :half_dim]
    second_half = tensor[..., half_dim:]
    cosine_part = cosine_table[:, None, :]
    sine_part = sine_table[:, None, :]
    return jnp.concatenate([first_half * cosine_part - second_half * sine_part, second_half * cosine_part + first_half * sine_part], axis=-1)

def layer_norm(row_values, norm_gain, norm_shift):
    centred = row_values - lax.optimization_barrier(jnp.mean(row_values, axis=-1, keepdims=True))
    variance = lax.optimization_barrier(jnp.mean(centred * centred, axis=-1, keepdims=True))
    return centred * lax.rsqrt(variance + EPSILON) * norm_gain + norm_shift

def row_forward(params, row_tokens, segments):
    query_weight, key_weight, value_weight, output_weight, attn_gain, attn_shift, gate_weight, up_weight, down_weight, mlp_gain, mlp_shift = params
    highest = lax.Precision.HIGHEST
    length = row_tokens.shape[0]
    cosine_table, sine_table = rotary_tables(segments)
    joint_weight = jnp.concatenate([query_weight, key_weight, value_weight], axis=1)
    projected = low_back(jnp.dot(row_tokens, joint_weight, precision=highest))
    shaped = projected.reshape(length, 3, HEADS, HEAD_DIM)
    queries = low(rotate(shaped[:, 0], cosine_table, sine_table))
    key_rows = low(rotate(shaped[:, 1], cosine_table, sine_table))
    value_rows = low(shaped[:, 2])
    block_rows = min(query_block, length)
    block_count = length // block_rows
    score_scale = 1.0 / math.sqrt(HEAD_DIM)

    def attend(block_pair):
        query_part, segment_part = block_pair
        scores = low_back(jnp.einsum('qhd,khd->hqk', query_part, key_rows, precision=highest) * score_scale)
        allowed = (segment_part[:, None] == segments[None, :])[None]
        scores = jnp.where(allowed, scores, MASKED)
        row_peak = lax.optimization_barrier(jnp.max(scores, axis=-1, keepdims=True))
        shifted = jnp.exp(scores - row_peak)
        soft_weights = shifted / lax.optimization_barrier(jnp.sum(shifted, axis=-1, keepdims=True))
        return jnp.einsum('hqk,khd->qhd', low(soft_weights), value_rows, precision=highest)
    context = lax.map(jax.checkpoint(attend), (queries.reshape(block_count, block_rows, HEADS, HEAD_DIM), segments.reshape(block_count, block_rows)))
    context = low_back(low(context.reshape(length, HEADS * HEAD_DIM)))
    attended = low_back(jnp.dot(context, output_weight, precision=highest))
    normed = layer_norm(row_tokens + attended, attn_gain, attn_shift)
    normed_low = low(normed)
    gate_pre = low_back(jnp.dot(normed_low, gate_weight, precision=highest))
    up_pre = low_back(jnp.dot(normed_low, up_weight, precision=highest))
    hidden = low(jax.nn.silu(gate_pre) * up_pre)
    mlp_rows = low_back(jnp.dot(hidden, down_weight, precision=highest))
    return layer_norm(normed + mlp_rows, mlp_gain, mlp_shift)

def reference(tokens, segment_ids, query_weight, key_weight, value_weight, output_weight, attn_gain, attn_shift, gate_weight, up_weight, down_weight, mlp_gain, mlp_shift, cotangent):
    params = tuple((weight_array.astype(jnp.float32) for weight_array in (query_weight, key_weight, value_weight, output_weight, attn_gain, attn_shift, gate_weight, up_weight, down_weight, mlp_gain, mlp_shift)))
    token_rows = tokens.astype(jnp.float32)
    checked_row = jax.checkpoint(row_forward)

    def forward(all_rows, weights):

        def scan_step(carried, row_pair):
            return (carried, checked_row(weights, row_pair[0], row_pair[1]))
        carry_out, outputs = lax.scan(scan_step, None, (all_rows, segment_ids))
        return outputs
    encoded, pullback = jax.vjp(forward, token_rows, params)
    grad_tokens, grads = pullback(cotangent.astype(jnp.float32))
    return (encoded.astype(jnp.bfloat16), grad_tokens, grads[0], grads[1], grads[2], grads[3], grads[4], grads[5], grads[6], grads[7], grads[8], grads[9], grads[10])
```

```python
import functools
import math

import jax
import jax.numpy as jnp
from jax import lax
from jax.experimental import pallas as pl
from jax.experimental.pallas import tpu as pltpu
from jax.sharding import PartitionSpec as P

HEAD_DIM = 64
EPSILON = 1e-05
ROPE_BASE = 1000.0
APART = -(2.0**30)
WIDE = 128
SEG_AT = HEAD_DIM
ROW_AT = HEAD_DIM + 8
VMEM = 48 * 2**20
bf16 = jnp.bfloat16
f32 = jnp.float32
NT = (((1,), (1,)), ((), ()))
TN = (((0,), (0,)), ((), ()))


def dot(a, b):
    return jnp.dot(a, b, preferred_element_type=f32)


def dot_nt(a, b):
    return lax.dot_general(a, b, NT, preferred_element_type=f32)


def dot_tn(a, b):
    return lax.dot_general(a, b, TN, preferred_element_type=f32)


def swap(value, axis, bit):
    size = lax.axis_size(axis)
    return lax.ppermute(value, axis, [(i, i ^ bit) for i in range(size)])


def gather_rows(block, axis):
    size = lax.axis_size(axis)
    held = {0: block}
    step = size // 2
    while step:
        keys = sorted(held)
        sent = held[keys[0]] if len(keys) == 1 else jnp.concatenate([held[k] for k in keys], axis=0)
        got = swap(sent, axis, step)
        rows = block.shape[0]
        for n, k in enumerate(keys):
            held[k ^ step] = got[n * rows : (n + 1) * rows]
        step //= 2
    return jnp.concatenate([held[k] for k in range(size)], axis=0)


def scatter_sum(blocks, axis):
    step = lax.axis_size(axis) // 2
    while step:
        got = swap(jnp.concatenate([b.astype(bf16) for b in blocks[step:]], axis=0), axis, step)
        rows = blocks[0].shape[0]
        blocks = [
            blocks[n].astype(f32) + got[n * rows : (n + 1) * rows].astype(f32) for n in range(step)
        ]
        step //= 2
    return blocks[0]


def exchange(blocks, axis):
    return [b if j == 0 else swap(b, axis, j) for j, b in enumerate(blocks)]


def sum_over(value, axis, order):
    me = lax.axis_index(axis)
    for bit in order:
        half = value.shape[0] // 2
        side = (me >> bit) & 1
        mine = lax.dynamic_slice_in_dim(value, side * half, half, 0)
        other = lax.dynamic_slice_in_dim(value, (1 - side) * half, half, 0)
        value = (mine.astype(f32) + swap(other, axis, 1 << bit).astype(f32)).astype(value.dtype)
    for bit in reversed(order):
        side = (me >> bit) & 1
        got = swap(value, axis, 1 << bit)
        value = jnp.where(
            side == 0, jnp.concatenate([value, got], 0), jnp.concatenate([got, value], 0)
        )
    return value


def small_sum(value, axis):
    step = lax.axis_size(axis) // 2
    while step:
        value = value + swap(value, axis, step)
        step //= 2
    return value


def project_kernel(heads, x_ref, w_ref, cos_ref, sin_ref, qf_ref, kf_ref, qa_ref, ka_ref, va_ref):
    proj = dot(x_ref[...], w_ref[...])
    cosine, sine = cos_ref[...], sin_ref[...]
    lane = lax.broadcasted_iota(jnp.int32, (proj.shape[0], WIDE), 1)
    first = lane < HEAD_DIM
    qf, kf = qf_ref[...], kf_ref[...]
    ones = jnp.where((lane >= HEAD_DIM) & (lane < HEAD_DIM + 3), 1.0, 0.0)
    for h in range(heads):
        at = [(part * heads + h) * WIDE for part in range(3)]
        q = proj[:, at[0] : at[0] + WIDE]
        k = proj[:, at[1] : at[1] + WIDE]
        v = proj[:, at[2] : at[2] + WIDE]
        q = q * cosine + pltpu.roll(q, HEAD_DIM, 1) * sine
        k = k * cosine + pltpu.roll(k, HEAD_DIM, 1) * sine
        qa_ref[h] = jnp.where(first, q * (1.0 / math.sqrt(HEAD_DIM)), qf).astype(bf16)
        ka_ref[h] = jnp.where(first, k, kf).astype(bf16)
        va_ref[h] = jnp.where(first, v, ones).astype(bf16)


def project(x, w, cosine, sine, qf, kf, heads, block=512):
    length, width = x.shape
    wide = jax.ShapeDtypeStruct((heads, length, WIDE), bf16)
    rows = lambda n: pl.BlockSpec((block, n), lambda i: (i, 0))
    out = pl.BlockSpec((heads, block, WIDE), lambda i: (0, i, 0))
    return pl.pallas_call(
        functools.partial(project_kernel, heads),
        grid=(length // block,),
        in_specs=[rows(width), pl.BlockSpec(w.shape, lambda i: (0, 0))] + [rows(WIDE)] * 4,
        out_specs=[out] * 3,
        out_shape=[wide] * 3,
        compiler_params=pltpu.CompilerParams(vmem_limit_bytes=VMEM),
        cost_estimate=pl.CostEstimate(
            flops=2 * length * width * w.shape[1], bytes_accessed=8 * 2**20, transcendentals=0
        ),
        name="project",
    )(x, w, cosine, sine, qf, kf)


def split3(value):
    high = value.astype(bf16).astype(f32)
    rest = value - high
    middle = rest.astype(bf16).astype(f32)
    return high, middle, rest - middle


def put_row(wide, at, value):
    lane = lax.broadcasted_iota(jnp.int32, wide.shape, 1)
    for n, part in enumerate(split3(value)):
        wide = jnp.where(lane == at + n, -part, wide)
    return wide


def attend_kernel(heads, qa_ref, ka_ref, va_ref, ctx_ref, qb_ref):
    parts = []
    for h in range(heads):
        qa = qa_ref[h]
        scores = dot_nt(qa, ka_ref[h])
        peak = jnp.max(scores, axis=1, keepdims=True)
        weights = jnp.exp(scores - peak).astype(bf16)
        summed = dot(weights, va_ref[h])
        total = summed[:, HEAD_DIM : HEAD_DIM + 1]
        parts.append(summed[:, :HEAD_DIM] / total)
        qb_ref[h] = put_row(qa.astype(f32), ROW_AT, peak + jnp.log(total)).astype(bf16)
    ctx_ref[...] = jnp.concatenate(parts, axis=1).astype(bf16)


def attend(qa, ka, va, block=256):
    heads, length, _ = qa.shape
    whole = pl.BlockSpec((heads, length, WIDE), lambda i: (0, 0, 0))
    part = pl.BlockSpec((heads, block, WIDE), lambda i: (0, i, 0))
    return pl.pallas_call(
        functools.partial(attend_kernel, heads),
        grid=(length // block,),
        in_specs=[part, whole, whole],
        out_specs=[pl.BlockSpec((block, heads * HEAD_DIM), lambda i: (i, 0)), part],
        out_shape=[
            jax.ShapeDtypeStruct((length, heads * HEAD_DIM), bf16),
            jax.ShapeDtypeStruct((heads, length, WIDE), bf16),
        ],
        compiler_params=pltpu.CompilerParams(vmem_limit_bytes=VMEM),
        cost_estimate=pl.CostEstimate(
            flops=4 * heads * length * length * 256,
            bytes_accessed=8 * 2**20,
            transcendentals=heads * length * length,
        ),
        name="attend",
    )(qa, ka, va)


def swap_halves(value, lane):
    half = HEAD_DIM // 2
    return jnp.where(
        lane < half, pltpu.roll(value, WIDE - half, 1), pltpu.roll(value, half, 1)
    )


def attend_back_kernel(
    head, block, qb_ref, ka_ref, va_ref, go_ref, ctx_ref, cos_ref, sin_ref, dq_ref, dkv_ref, doa, dqt
):
    j = pl.program_id(0)
    length = qb_ref.shape[1]
    cols = pl.ds(head * HEAD_DIM, HEAD_DIM)

    @pl.when(j == 0)
    def _():
        dqt[...] = jnp.zeros_like(dqt)
        for i in range(length // block):
            at = pl.ds(i * block, block)
            go = go_ref[at, cols].astype(f32)
            delta = jnp.sum(go * ctx_ref[at, cols].astype(f32), axis=1, keepdims=True)
            wide = jnp.concatenate([go, jnp.zeros_like(go)], axis=1)
            doa[at, :] = put_row(wide, HEAD_DIM, delta).astype(bf16)

    ka, va = ka_ref[0], va_ref[0]
    kt = ka.astype(f32).T[:HEAD_DIM].astype(bf16)
    dk = dv = None
    for i in range(length // block):
        at = pl.ds(i * block, block)
        qb, do = qb_ref[0, at, :], doa[at, :]
        weights = jnp.exp(dot_nt(ka, qb))
        grads = (weights * dot_nt(va, do)).astype(bf16)
        v_part = dot(weights.astype(bf16), do)
        k_part = dot(grads, qb)
        dk = k_part if i == 0 else dk + k_part
        dv = v_part if i == 0 else dv + v_part
        dqt[:, at] += dot(kt, grads)
    lane = lax.broadcasted_iota(jnp.int32, dk.shape, 1)
    rows = pl.ds(pl.multiple_of(j * ka.shape[0], ka.shape[0]), ka.shape[0])
    dk = dk * cos_ref[rows, :] - swap_halves(dk, lane) * sin_ref[rows, :]
    dkv_ref[...] = jnp.where(
        lane < HEAD_DIM, dk, pltpu.roll(jnp.where(lane < HEAD_DIM, dv, 0.0), HEAD_DIM, 1)
    ).astype(bf16)

    @pl.when(j == pl.num_programs(0) - 1)
    def _():
        for i in range(length // block):
            at = pl.ds(i * block, block)
            part = dqt[:, at]
            dq = jnp.concatenate([part, jnp.zeros_like(part)], axis=0).T
            lanes = lax.broadcasted_iota(jnp.int32, dq.shape, 1)
            dq = dq * cos_ref[at, :] - swap_halves(dq, lanes) * sin_ref[at, :]
            dq_ref[at, :] = (dq[:, :HEAD_DIM] * (1.0 / math.sqrt(HEAD_DIM))).astype(bf16)


def attend_back(head, qb, ka, va, go, ctx, cosine, sine, block_k=512, block_q=512):
    _, length, _ = qb.shape
    at_head = pl.BlockSpec((1, length, WIDE), lambda j: (head, 0, 0))
    part = pl.BlockSpec((1, block_k, WIDE), lambda j: (head, j, 0))
    full = lambda a: pl.BlockSpec(a.shape, lambda j: (0, 0))
    return pl.pallas_call(
        functools.partial(attend_back_kernel, head, block_q),
        grid=(length // block_k,),
        in_specs=[at_head, part, part, full(go), full(ctx), full(cosine), full(sine)],
        out_specs=[
            pl.BlockSpec((length, HEAD_DIM), lambda j: (0, 0)),
            pl.BlockSpec((block_k, WIDE), lambda j: (j, 0)),
        ],
        out_shape=[
            jax.ShapeDtypeStruct((length, HEAD_DIM), bf16),
            jax.ShapeDtypeStruct((length, WIDE), bf16),
        ],
        scratch_shapes=[pltpu.VMEM((length, WIDE), bf16), pltpu.VMEM((HEAD_DIM, length), f32)],
        compiler_params=pltpu.CompilerParams(vmem_limit_bytes=VMEM),
        cost_estimate=pl.CostEstimate(
            flops=10 * length * length * 256,
            bytes_accessed=4 * 2**20,
            transcendentals=length * length,
        ),
        name="attend_back",
    )(qb, ka, va, go, ctx, cosine, sine)


def positions(segments):
    places = jnp.arange(segments.shape[0], dtype=jnp.int32)
    before = jnp.concatenate([segments[:1] - 1, segments[:-1]])
    starts = lax.cummax(jnp.where(segments != before, places, 0), axis=0)
    return (places - starts).astype(f32)


def norm_parts(row_values):
    centred = row_values - jnp.mean(row_values, axis=-1, keepdims=True)
    inverse = lax.rsqrt(jnp.mean(centred * centred, axis=-1, keepdims=True) + EPSILON)
    return (centred * inverse, inverse)


def norm_back(grad_norm, normalized, inverse):
    return inverse * (
        grad_norm
        - jnp.mean(grad_norm, axis=-1, keepdims=True)
        - normalized * jnp.mean(grad_norm * normalized, axis=-1, keepdims=True)
    )


def relative_rows(value, blocks):
    me = lax.axis_index("tensor")
    rows = value.shape[0] // blocks
    return jnp.concatenate(
        [lax.dynamic_slice_in_dim(value, (me ^ j) * rows, rows, 0) for j in range(blocks)], axis=0
    )


def wide_weight(query_weight, key_weight, value_weight, heads):
    width = query_weight.shape[0]
    half = HEAD_DIM // 2

    def turned(weight):
        w = weight.reshape(width, heads, HEAD_DIM)
        swapped = jnp.concatenate([w[..., half:], w[..., :half]], axis=-1)
        return jnp.concatenate([w, swapped], axis=-1).reshape(width, heads * WIDE)

    v = value_weight.reshape(width, heads, HEAD_DIM)
    v = jnp.concatenate([v, jnp.zeros_like(v)], axis=-1).reshape(width, heads * WIDE)
    return jnp.concatenate([turned(query_weight), turned(key_weight), v], axis=1)


def local(
    tokens,
    segment_ids,
    query_weight,
    key_weight,
    value_weight,
    output_weight,
    attn_gain,
    attn_shift,
    gate_weight,
    up_weight,
    down_weight,
    mlp_gain,
    mlp_shift,
    cotangent,
):
    own = tokens[0]
    segments = segment_ids[0]
    head_width = query_weight.shape[1]
    heads = head_width // HEAD_DIM
    ff_local = gate_weight.shape[1]
    group = lax.axis_size("tensor")
    block = own.shape[0]
    bits = list(range(int(math.log2(lax.axis_size("dp")))))
    orders = [bits, bits[1:] + bits[:1]]

    x_full = gather_rows(own, "tensor")
    out_full = gather_rows(output_weight, "tensor")

    angle_rate = ROPE_BASE ** (-(jnp.arange(HEAD_DIM // 2, dtype=f32) * 2.0 / HEAD_DIM))
    angles = positions(segments)[:, None] * angle_rate[None, :]
    cosine, sine = jnp.cos(angles), jnp.sin(angles)
    blank = jnp.zeros((segments.shape[0], HEAD_DIM), f32)
    one_hot = (segments[:, None] + 1 == jnp.arange(8)[None, :]).astype(f32)
    table = jnp.concatenate(
        [cosine, cosine, blank, -sine, sine, blank]
        + [blank, APART * one_hot, blank[:, :56], blank, 1.0 - one_hot, blank[:, :3] + 1.0, blank[:, :53]],
        axis=1,
    )
    table = relative_rows(table, group)
    cos_wide, sin_wide, qf, kf = (table[:, n * WIDE : (n + 1) * WIDE] for n in range(4))

    joint_wide = wide_weight(query_weight, key_weight, value_weight, heads)
    qa, ka, va = project(x_full, joint_wide, cos_wide, sin_wide, qf, kf, heads)
    ctx, qb = attend(qa, ka, va)
    ctx_parts = exchange([ctx[j * block : (j + 1) * block] for j in range(group)], "tensor")
    ctx_own = jnp.concatenate(ctx_parts, axis=1)

    first_norm, first_inverse = norm_parts(own.astype(f32) + dot(ctx_own, out_full))
    normed = first_norm * attn_gain + attn_shift
    normed_full = gather_rows(normed.astype(bf16), "tensor")
    gate_pre = dot(normed_full, gate_weight)
    up_pre = dot(normed_full, up_weight)
    gate_sigmoid = jax.nn.sigmoid(gate_pre)
    activated = gate_pre * gate_sigmoid
    hidden = (activated * up_pre).astype(bf16)
    mlp = dot(hidden, down_weight)
    mlp_rows = scatter_sum([mlp[j * block : (j + 1) * block] for j in range(group)], "tensor")
    second_norm, second_inverse = norm_parts(normed + mlp_rows)
    encoded = (second_norm * mlp_gain + mlp_shift).astype(bf16)
    grad_encoded = cotangent[0].astype(f32)
    grad_second = norm_back(grad_encoded * mlp_gain, second_norm, second_inverse)
    grad_mlp_full = gather_rows(grad_second.astype(bf16), "tensor")

    grad_down = dot_tn(hidden, grad_mlp_full).astype(bf16)
    grad_down = sum_over(grad_down, "dp", orders[0])
    grad_hidden = dot_nt(grad_mlp_full, down_weight)
    grad_gate_low = (
        grad_hidden * up_pre * gate_sigmoid * (1.0 + gate_pre * (1.0 - gate_sigmoid))
    ).astype(bf16)
    grad_up_low = (grad_hidden * activated).astype(bf16)
    back = dot_nt(grad_gate_low, gate_weight) + dot_nt(grad_up_low, up_weight)
    grad_normed = grad_second + scatter_sum(
        [back[j * block : (j + 1) * block] for j in range(group)], "tensor"
    )
    grad_gate = sum_over(dot_tn(normed_full, grad_gate_low).astype(bf16), "dp", orders[1])
    grad_up = sum_over(dot_tn(normed_full, grad_up_low).astype(bf16), "dp", orders[0])

    grad_first = norm_back(grad_normed * attn_gain, first_norm, first_inverse)
    grad_attn_low = grad_first.astype(bf16)
    small = jnp.stack(
        [
            jnp.sum(grad_normed * first_norm, axis=0),
            jnp.sum(grad_normed, axis=0),
            jnp.sum(grad_encoded * second_norm, axis=0),
            jnp.sum(grad_encoded, axis=0),
        ]
    )
    small = small_sum(small_sum(small, "tensor"), "dp")

    grad_ctx_own = dot_nt(grad_attn_low, out_full).astype(bf16)
    grad_ctx = jnp.concatenate(
        exchange([grad_ctx_own[:, j * head_width : (j + 1) * head_width] for j in range(group)], "tensor"),
        axis=0,
    )
    grad_out = dot_tn(ctx_own, grad_attn_low)
    grad_out = scatter_sum(
        [grad_out[j * head_width : (j + 1) * head_width] for j in range(group)], "tensor"
    ).astype(bf16)
    grad_out = sum_over(grad_out, "dp", orders[0])

    grad_heads, parts = [], []
    for h in range(heads):
        dq, dkv = attend_back(h, qb, ka, va, grad_ctx, ctx, cos_wide, sin_wide)
        part = jnp.concatenate([dq, dkv], axis=1)
        parts.append(part)
        grad_heads.append(sum_over(dot_tn(x_full, part).astype(bf16), "dp", orders[h % 2]))
    columns = [
        jnp.concatenate([p[:, n * HEAD_DIM : (n + 1) * HEAD_DIM] for p in parts], axis=1)
        for n in range(3)
    ]
    back = (
        dot_nt(columns[0], query_weight)
        + dot_nt(columns[1], key_weight)
        + dot_nt(columns[2], value_weight)
    )
    grad_tokens = grad_first + scatter_sum(
        [back[j * block : (j + 1) * block] for j in range(group)], "tensor"
    )
    grad_joint = [
        jnp.concatenate([g[:, n * HEAD_DIM : (n + 1) * HEAD_DIM] for g in grad_heads], axis=1).astype(f32)
        for n in range(3)
    ]
    return (
        encoded[None],
        grad_tokens[None],
        *grad_joint,
        grad_out.astype(f32),
        small[0],
        small[1],
        grad_gate.astype(f32),
        grad_up.astype(f32),
        grad_down.astype(f32),
        small[2],
        small[3],
    )


def solution(mesh):
    rows, cols, lead = P("dp", "tensor", None), P(None, "tensor"), P("tensor", None)
    return jax.shard_map(
        local,
        mesh=mesh,
        in_specs=(
            rows, P("dp", None), cols, cols, cols, lead, P(), P(), cols, cols, lead, P(), P(), rows,
        ),
        out_specs=(
            rows, rows, cols, cols, cols, lead, P(), P(), cols, cols, lead, P(), P(),
        ),
        check_vma=False,
    )
```

```python
import functools
import math

import jax
import jax.numpy as jnp
from jax import lax
from jax.experimental import pallas as pl
from jax.experimental.pallas import tpu as pltpu
from jax.sharding import PartitionSpec as P

HEAD_DIM = 64
EPSILON = 1e-05
ROPE_BASE = 1000.0
APART = -(2.0**30)
WIDE = 128
SEG_AT = HEAD_DIM
ROW_AT = HEAD_DIM + 8
VMEM = 48 * 2**20
bf16 = jnp.bfloat16
f32 = jnp.float32
NT = (((1,), (1,)), ((), ()))
TN = (((0,), (0,)), ((), ()))


def dot(a, b):
    return jnp.dot(a, b, preferred_element_type=f32)


def dot_nt(a, b):
    return lax.dot_general(a, b, NT, preferred_element_type=f32)


def dot_tn(a, b):
    return lax.dot_general(a, b, TN, preferred_element_type=f32)


def swap(value, axis, bit):
    size = lax.axis_size(axis)
    return lax.ppermute(value, axis, [(i, i ^ bit) for i in range(size)])


def after(value, *others):
    return lax.optimization_barrier((value, *others))[0]


def all_after(values, *others):
    return list(lax.optimization_barrier((tuple(values), others))[0])


def scatter_sum(blocks, axis):
    held = dict(enumerate(blocks))
    rows = blocks[0].shape[0]
    step = 1
    while step < len(blocks):
        sent = [k for k in held if k & step]
        got = [held.pop(k).astype(bf16) for k in sent]
        got = swap(got[0] if len(got) == 1 else jnp.concatenate(got, axis=0), axis, step)
        for n, k in enumerate(sent):
            held[k ^ step] = held[k ^ step] + got[n * rows : (n + 1) * rows].astype(f32)
        step *= 2
    return held[0]


def exchange(blocks, axis):
    return [b if j == 0 else swap(b, axis, j) for j, b in enumerate(blocks)]


def sum_steps(value, axis, order):
    me = lax.axis_index(axis)
    for bit in order:
        half = value.shape[0] // 2
        side = (me >> bit) & 1
        mine = lax.dynamic_slice_in_dim(value, side * half, half, 0)
        other = lax.dynamic_slice_in_dim(value, (1 - side) * half, half, 0)
        got = swap(other, axis, 1 << bit)
        deps = yield other
        if deps is not None:
            got = after(got, deps)
        value = (mine.astype(f32) + got.astype(f32)).astype(value.dtype)
    for bit in reversed(order):
        side = (me >> bit) & 1
        got = swap(value, axis, 1 << bit)
        deps = yield value
        if deps is not None:
            got = after(got, deps)
        value = jnp.where(
            side == 0, jnp.concatenate([value, got], 0), jnp.concatenate([got, value], 0)
        )
    return value


class Sum:
    def __init__(self, value, order):
        self.steps = sum_steps(value, "dp", order)
        self.result = None
        self.sent = next(self.steps)

    def advance(self, deps=None):
        if self.result is None:
            try:
                self.sent = self.steps.send(deps)
            except StopIteration as end:
                self.result = end.value

    def finish(self):
        while self.result is None:
            self.advance()
        return self.result


def small_sum(value, axis):
    step = lax.axis_size(axis) // 2
    while step:
        value = value + swap(value, axis, step)
        step //= 2
    return value


def project_kernel(heads, count, *refs):
    pieces, refs = refs[:count], refs[count:]
    w_ref, cos_ref, sin_ref, seg_ref = refs[:4]
    x_ref, qa_ref, ka_ref, va_ref = refs[-4:]
    rows = x_ref.shape[0]
    for n, piece in enumerate(pieces):

        @pl.when(pl.program_id(0) == n)
        def _(piece=piece):
            x_ref[...] = piece[...]

    proj = dot(x_ref[...], w_ref[...])
    cosine, sine = cos_ref[...], sin_ref[...]
    lane = lax.broadcasted_iota(jnp.int32, (rows, WIDE), 1)
    first = lane < HEAD_DIM
    same = lane == seg_ref[...] + (SEG_AT + 1)
    qf = jnp.where(same, APART, 0.0)
    kf = jnp.where((lane < ROW_AT + 3) & ~same, 1.0, 0.0)
    ones = jnp.where(lane < HEAD_DIM + 3, 1.0, 0.0)
    for h in range(heads):
        at = [(part * heads + h) * WIDE for part in range(3)]
        q = proj[:, at[0] : at[0] + WIDE]
        k = proj[:, at[1] : at[1] + WIDE]
        v = proj[:, at[2] : at[2] + WIDE]
        q = q * cosine + pltpu.roll(q, HEAD_DIM, 1) * sine
        k = k * cosine + pltpu.roll(k, HEAD_DIM, 1) * sine
        qa_ref[h] = jnp.where(first, q * (1.0 / math.sqrt(HEAD_DIM)), qf).astype(bf16)
        ka_ref[h] = jnp.where(first, k, kf).astype(bf16)
        va_ref[h] = jnp.where(first, v, ones).astype(bf16)


def project(pieces, start, w, cosine, sine, seg, heads, done=()):
    block, width = pieces[0].shape
    length = cosine.shape[0]
    rows = lambda n: pl.BlockSpec((block, n), lambda i: (start + i, 0))
    whole = lambda a: pl.BlockSpec(a.shape, lambda i: (0, 0))
    out = pl.BlockSpec((heads, block, WIDE), lambda i: (0, start + i, 0))
    given = len(pieces) + 4
    return pl.pallas_call(
        functools.partial(project_kernel, heads, len(pieces)),
        grid=(len(pieces),),
        in_specs=[whole(p) for p in pieces]
        + [whole(w), rows(WIDE), rows(WIDE), rows(1)]
        + [pl.BlockSpec(memory_space=pl.ANY)] * len(done),
        out_specs=[rows(width)] + [out] * 3,
        out_shape=[jax.ShapeDtypeStruct((length, width), bf16)]
        + [jax.ShapeDtypeStruct((heads, length, WIDE), bf16)] * 3,
        input_output_aliases={given + n: n for n in range(len(done))},
        compiler_params=pltpu.CompilerParams(vmem_limit_bytes=VMEM),
        cost_estimate=pl.CostEstimate(
            flops=2 * len(pieces) * block * width * w.shape[1], bytes_accessed=4 * 2**20, transcendentals=0
        ),
        name="project",
    )(*pieces, w, cosine, sine, seg, *done)


def split3(value):
    high = value.astype(bf16).astype(f32)
    rest = value - high
    middle = rest.astype(bf16).astype(f32)
    return high, middle, rest - middle


def put_row(wide, at, value):
    lane = lax.broadcasted_iota(jnp.int32, wide.shape, 1)
    for n, part in enumerate(split3(value)):
        wide = jnp.where(lane == at + n, -part, wide)
    return wide


def attend_kernel(heads, qa_ref, ka_ref, va_ref, *refs):
    ctx_ref, qb_ref = refs[-2:]
    parts = []
    for h in range(heads):
        qa = qa_ref[h]
        scores = dot_nt(qa, ka_ref[h])
        peak = jnp.max(scores, axis=1, keepdims=True)
        weights = jnp.exp(scores - peak).astype(bf16)
        summed = dot(weights, va_ref[h])
        total = summed[:, HEAD_DIM : HEAD_DIM + 1]
        parts.append(summed[:, :HEAD_DIM] / total)
        qb_ref[h] = put_row(qa.astype(f32), ROW_AT, peak + jnp.log(total)).astype(bf16)
    ctx_ref[...] = jnp.concatenate(parts, axis=1).astype(bf16)


def attend(qa, ka, va, start, count, done=(), block=256):
    heads, length, _ = qa.shape
    first = start // block
    whole = pl.BlockSpec((heads, length, WIDE), lambda i: (0, 0, 0))
    part = pl.BlockSpec((heads, block, WIDE), lambda i: (0, first + i, 0))
    return pl.pallas_call(
        functools.partial(attend_kernel, heads),
        grid=(count // block,),
        in_specs=[part, whole, whole] + [pl.BlockSpec(memory_space=pl.ANY)] * len(done),
        out_specs=[pl.BlockSpec((block, heads * HEAD_DIM), lambda i: (first + i, 0)), part],
        out_shape=[
            jax.ShapeDtypeStruct((length, heads * HEAD_DIM), bf16),
            jax.ShapeDtypeStruct((heads, length, WIDE), bf16),
        ],
        input_output_aliases={3 + n: n for n in range(len(done))},
        compiler_params=pltpu.CompilerParams(vmem_limit_bytes=VMEM),
        cost_estimate=pl.CostEstimate(
            flops=4 * heads * count * length * 256,
            bytes_accessed=8 * 2**20,
            transcendentals=heads * count * length,
        ),
        name="attend",
    )(qa, ka, va, *done)


def swap_halves(value, lane):
    half = HEAD_DIM // 2
    return jnp.where(
        lane < half, pltpu.roll(value, WIDE - half, 1), pltpu.roll(value, half, 1)
    )


def attend_back_kernel(head, block, qb_ref, ka_ref, va_ref, *refs):
    gos, refs = refs[:4], refs[4:]
    ctx_ref, cos_ref, sin_ref, dq_ref, dkv_ref, doa, dqt = refs
    j = pl.program_id(0)
    length = qb_ref.shape[1]
    cols = pl.ds(head * HEAD_DIM, HEAD_DIM)

    @pl.when(j == 0)
    def _():
        dqt[...] = jnp.zeros_like(dqt)
        for i in range(length // block):
            at = pl.ds(i * block, block)
            go = gos[i][:block, cols].astype(f32)
            delta = jnp.sum(go * ctx_ref[at, cols].astype(f32), axis=1, keepdims=True)
            wide = jnp.concatenate([go, jnp.zeros_like(go)], axis=1)
            doa[at, :] = put_row(wide, HEAD_DIM, delta).astype(bf16)

    ka, va = ka_ref[0], va_ref[0]
    kt = ka.astype(f32).T[:HEAD_DIM].astype(bf16)
    dk = dv = None
    for i in range(length // block):
        at = pl.ds(i * block, block)
        qb, do = qb_ref[0, at, :], doa[at, :]
        weights = jnp.exp(dot_nt(ka, qb))
        grads = (weights * dot_nt(va, do)).astype(bf16)
        v_part = dot(weights.astype(bf16), do)
        k_part = dot(grads, qb)
        dk = k_part if i == 0 else dk + k_part
        dv = v_part if i == 0 else dv + v_part
        dqt[:, at] += dot(kt, grads)
    lane = lax.broadcasted_iota(jnp.int32, dk.shape, 1)
    rows = pl.ds(pl.multiple_of(j * ka.shape[0], ka.shape[0]), ka.shape[0])
    dk = dk * cos_ref[rows, :] - swap_halves(dk, lane) * sin_ref[rows, :]
    dkv_ref[...] = jnp.where(
        lane < HEAD_DIM, dk, pltpu.roll(jnp.where(lane < HEAD_DIM, dv, 0.0), HEAD_DIM, 1)
    ).astype(bf16)

    @pl.when(j == pl.num_programs(0) - 1)
    def _():
        for i in range(length // block):
            at = pl.ds(i * block, block)
            part = dqt[:, at]
            dq = jnp.concatenate([part, jnp.zeros_like(part)], axis=0).T
            lanes = lax.broadcasted_iota(jnp.int32, dq.shape, 1)
            dq = dq * cos_ref[at, :] - swap_halves(dq, lanes) * sin_ref[at, :]
            dq_ref[at, :] = (dq[:, :HEAD_DIM] * (1.0 / math.sqrt(HEAD_DIM))).astype(bf16)


def attend_back(head, qb, ka, va, gos, ctx, cosine, sine, block_k=512):
    _, length, _ = qb.shape
    block_q = length // len(gos)
    at_head = pl.BlockSpec((1, length, WIDE), lambda j: (head, 0, 0))
    part = pl.BlockSpec((1, block_k, WIDE), lambda j: (head, j, 0))
    full = lambda a: pl.BlockSpec(a.shape, lambda j: (0, 0))
    return pl.pallas_call(
        functools.partial(attend_back_kernel, head, block_q),
        grid=(length // block_k,),
        in_specs=[at_head, part, part] + [full(a) for a in (*gos, ctx, cosine, sine)],
        out_specs=[
            pl.BlockSpec((length, HEAD_DIM), lambda j: (0, 0)),
            pl.BlockSpec((block_k, WIDE), lambda j: (j, 0)),
        ],
        out_shape=[
            jax.ShapeDtypeStruct((length, HEAD_DIM), bf16),
            jax.ShapeDtypeStruct((length, WIDE), bf16),
        ],
        scratch_shapes=[pltpu.VMEM((length, WIDE), bf16), pltpu.VMEM((HEAD_DIM, length), f32)],
        compiler_params=pltpu.CompilerParams(vmem_limit_bytes=VMEM),
        cost_estimate=pl.CostEstimate(
            flops=2**20,
            bytes_accessed=2**16,
            transcendentals=0,
        ),
        name="attend_back",
    )(qb, ka, va, *gos, ctx, cosine, sine)


ANY = pl.BlockSpec(memory_space=pl.ANY)
IN_VMEM = pl.BlockSpec(memory_space=pltpu.VMEM)


def start(source, target, sem):
    copy = pltpu.make_async_copy(source, target, sem)
    copy.start()
    return copy


def norm_parts(row_values):
    centred = row_values - jnp.mean(row_values, axis=-1, keepdims=True)
    inverse = lax.rsqrt(jnp.mean(centred * centred, axis=-1, keepdims=True) + EPSILON)
    return (centred * inverse, inverse)


def norm_back(grad_norm, normalized, inverse):
    return inverse * (
        grad_norm
        - jnp.mean(grad_norm, axis=-1, keepdims=True)
        - normalized * jnp.mean(grad_norm * normalized, axis=-1, keepdims=True)
    )


def mix_kernel(own_ref, *refs):
    parts, outs, refs = refs[:4], refs[4:8], refs[8:]
    gain_ref, shift_ref, norm_ref, inverse_ref, low_ref = refs
    total = own_ref[...].astype(f32)
    for part, out in zip(parts, outs):
        total = total + dot(part[...], out[...])
    norm, inverse = norm_parts(total)
    norm_ref[...] = norm
    inverse_ref[...] = jnp.broadcast_to(inverse, inverse_ref.shape)
    low_ref[...] = (norm * gain_ref[...] + shift_ref[...]).astype(bf16)


def mix(own, parts, outs, gain, shift, block=256):
    length, width = own.shape
    rows = lambda a: pl.BlockSpec((block, a.shape[1]), lambda i: (i, 0))
    whole = lambda a: pl.BlockSpec(a.shape, lambda i: (0, 0))
    shapes = [
        jax.ShapeDtypeStruct((length, width), f32),
        jax.ShapeDtypeStruct((length, WIDE), f32),
        jax.ShapeDtypeStruct((length, width), bf16),
    ]
    return pl.pallas_call(
        mix_kernel,
        grid=(length // block,),
        in_specs=[rows(own)] + [rows(p) for p in parts] + [whole(w) for w in outs] + [whole(gain), whole(shift)],
        out_specs=[rows(s) for s in shapes],
        out_shape=shapes,
        compiler_params=pltpu.CompilerParams(vmem_limit_bytes=VMEM),
        cost_estimate=pl.CostEstimate(flops=2 * length * width * width, bytes_accessed=6 * 2**20, transcendentals=0),
        name="mix",
    )(own, *parts, *outs, gain, shift)


def feed(low, gate, up):
    gate_pre, up_pre = dot(low, gate), dot(low, up)
    return gate_pre, up_pre


def hidden_of(gate_pre, up_pre):
    return (gate_pre * jax.nn.sigmoid(gate_pre) * up_pre).astype(bf16)


def feed_back(grad_hidden, gate_pre, up_pre):
    sigmoid = jax.nn.sigmoid(gate_pre)
    grad_gate = grad_hidden * up_pre * sigmoid * (1.0 + gate_pre * (1.0 - sigmoid))
    return grad_gate.astype(bf16), (grad_hidden * gate_pre * sigmoid).astype(bf16)


def shard_copies(n, firsts, shards, buffers, sem):
    refs = list(shards[3 * n : 3 * n + 3])
    hidden = refs[2].shape[0]
    for k in range(2):
        refs[k] = refs[k].at[:, pl.ds(firsts[2 * n + k] * hidden, hidden)]
    return [start(ref, buffer.at[n], sem.at[n, k]) for k, (ref, buffer) in enumerate(zip(refs, buffers))]


def shard_args(shards):
    args = [a for (gate, _), (up, _), down in shards for a in (gate, up, down)]
    return args, [first for (_, g), (_, u), _ in shards for first in (g, u)]


HALVES = 2


def halves(length):
    return [pl.ds(n * (length // HALVES), length // HALVES) for n in range(HALVES)]


def forward_kernel(firsts, last, low_ref, *refs):
    count = len(firsts) // 2
    shards, refs = refs[: 3 * count], refs[3 * count :]
    if last:
        before_ref, norm_ref, cot_ref, gain_ref, shift_ref, gain2_ref, shift2_ref = refs[:7]
        gates_ref, ups_ref, encoded_ref, second_ref, low2_ref, small_ref = refs[7:13]
        gate, up, down, gates, ups, sem, out_sem, total, before, norm1, cot_in, more_sem = refs[13:]
    else:
        gates_ref, ups_ref, total, gate, up, down, gates, ups, sem, out_sem = refs
    buffers = (gate, up, down)
    coming = [shard_copies(0, firsts, shards, buffers, sem)]
    if last:
        extra = [
            start(ref, buffer, more_sem.at[n])
            for n, (ref, buffer) in enumerate([(before_ref, before), (norm_ref, norm1), (cot_ref, cot_in)])
        ]
    going = []
    hidden = down.shape[1]
    for n in range(count):
        if n + 1 < count:
            coming.append(shard_copies(n + 1, firsts, shards, buffers, sem))
        for copy in coming[n]:
            copy.wait()
        for at in halves(low_ref.shape[0]):
            gate_pre, up_pre = feed(low_ref[at, :], gate[n], up[n])
            gates[n, at, :] = gate_pre.astype(bf16)
            ups[n, at, :] = up_pre.astype(bf16)
            part = dot(hidden_of(gate_pre, up_pre), down[n])
            total[at, :] = part if n == 0 else total[at, :] + part
        cols = pl.ds(n * hidden, hidden)
        going.append(start(gates.at[n], gates_ref.at[:, cols], out_sem.at[n, 0]))
        going.append(start(ups.at[n], ups_ref.at[:, cols], out_sem.at[n, 1]))
    if last:
        for copy in extra:
            copy.wait()
        normed = norm1[...] * gain_ref[...] + shift_ref[...]
        norm, inverse = norm_parts(normed + (before[...] + total[...]))
        cot = cot_in[...].astype(f32)
        encoded_ref[...] = (norm * gain2_ref[...] + shift2_ref[...]).astype(bf16)
        second = norm_back(cot * gain2_ref[...], norm, inverse)
        second_ref[...] = second
        low2_ref[...] = second.astype(bf16)
        small_ref[...] = jnp.concatenate(
            [jnp.sum(cot * norm, axis=0, keepdims=True), jnp.sum(cot, axis=0, keepdims=True)], axis=0
        )
    for copy in going:
        copy.wait()


def forward(low, shards, last=()):
    length, width = low.shape
    count, hidden = len(shards), shards[0][2].shape[0]
    args, firsts = shard_args(shards)
    shapes = [jax.ShapeDtypeStruct((length, hidden * count), bf16)] * 2
    out_specs = [ANY, ANY]
    scratch = [
        pltpu.VMEM((count, width, hidden), bf16),
        pltpu.VMEM((count, width, hidden), bf16),
        pltpu.VMEM((count, hidden, width), bf16),
        pltpu.VMEM((count, length, hidden), bf16),
        pltpu.VMEM((count, length, hidden), bf16),
        pltpu.SemaphoreType.DMA((count, 3)),
        pltpu.SemaphoreType.DMA((count, 2)),
    ]
    if last:
        shapes += [
            jax.ShapeDtypeStruct((length, width), bf16),
            jax.ShapeDtypeStruct((length, width), f32),
            jax.ShapeDtypeStruct((length, width), bf16),
            jax.ShapeDtypeStruct((2, width), f32),
        ]
        out_specs += [IN_VMEM] * 4
        wide = pltpu.VMEM((length, width), f32)
        scratch += [wide, wide, wide, pltpu.VMEM((length, width), bf16), pltpu.SemaphoreType.DMA((3,))]
    else:
        shapes.append(jax.ShapeDtypeStruct((length, width), f32))
        out_specs.append(IN_VMEM)
    return pl.pallas_call(
        functools.partial(forward_kernel, firsts, bool(last)),
        in_specs=[IN_VMEM] + [ANY] * len(args) + [ANY] * len(last[:3]) + [IN_VMEM] * len(last[3:]),
        out_specs=out_specs,
        out_shape=shapes,
        scratch_shapes=scratch,
        compiler_params=pltpu.CompilerParams(vmem_limit_bytes=VMEM),
        cost_estimate=pl.CostEstimate(
            flops=6 * length * width * hidden * count,
            bytes_accessed=12 * 2**20,
            transcendentals=length * hidden * count,
        ),
        name="feed_forward",
    )(low, *args, *last)


def backward_kernel(firsts, low2_ref, *refs):
    count = len(firsts) // 2
    shards, refs = refs[: 3 * count], refs[3 * count :]
    saved, refs = refs[:4], refs[4:]
    late_refs, refs = refs[:7], refs[7:]
    gain_ref, small_in_ref, first_ref, low_ref, ctx_ref = refs[:5]
    gate, up, down, gates, ups, total, second, norm1, inverse, outs, sem, saved_sem, late_sem = refs[5:]
    buffers = (gate, up, down)
    hidden = down.shape[1]

    def fetch(n):
        part, cols = n * 2 // count, pl.ds(n % (count // 2) * hidden, hidden)
        return shard_copies(n, firsts, shards, buffers, sem) + [
            start(ref.at[:, cols], buffer.at[n], saved_sem.at[n, k])
            for k, (ref, buffer) in enumerate(zip(saved[2 * part : 2 * part + 2], (gates, ups)))
        ]

    coming = [fetch(0)]
    late = []
    for n in range(count):
        if n + 1 < count:
            coming.append(fetch(n + 1))
        else:
            targets = [second, norm1, inverse] + [outs.at[k] for k in range(4)]
            late = [start(ref, target, late_sem.at[k]) for k, (ref, target) in enumerate(zip(late_refs, targets))]
        for copy in coming[n]:
            copy.wait()
        for at in halves(low2_ref.shape[0]):
            grad_hidden = dot_nt(low2_ref[at, :], down[n])
            grad_gate, grad_up = feed_back(grad_hidden, gates[n, at, :].astype(f32), ups[n, at, :].astype(f32))
            part = dot_nt(grad_gate, gate[n]) + dot_nt(grad_up, up[n])
            total[at, :] = part if n == 0 else total[at, :] + part
    for copy in late:
        copy.wait()
    normed_grad, norm = second[...] + total[...], norm1[...]
    first = norm_back(normed_grad * gain_ref[...], norm, inverse[:, :1])
    first_ref[...] = first
    low = first.astype(bf16)
    low_ref[...] = low
    small = jnp.concatenate(
        [
            jnp.sum(normed_grad * norm, axis=0, keepdims=True),
            jnp.sum(normed_grad, axis=0, keepdims=True),
            small_in_ref[...],
        ],
        axis=0,
    )
    width = outs.shape[1]
    small = jnp.concatenate([small[:, k * width : (k + 1) * width] for k in range(4)], axis=0)
    high = small.astype(bf16)
    small = jnp.concatenate([high, (small - high.astype(f32)).astype(bf16)], axis=0)
    length = low.shape[0]
    for k in range(4):
        ctx_ref[k, :length, :] = dot_nt(low, outs[k]).astype(bf16)
        ctx_ref[k, length:, :] = small


SMALL = 32


def backward(low2, shards, saved, second, norm, inverse, outs, gain, small):
    length, width = low2.shape
    count, hidden = len(shards), shards[0][2].shape[0]
    args, firsts = shard_args(shards)
    late = [second, norm, inverse, *outs]
    wide = pltpu.VMEM((length, width), f32)
    return pl.pallas_call(
        functools.partial(backward_kernel, firsts),
        in_specs=[IN_VMEM] + [ANY] * (len(args) + len(saved) + len(late)) + [IN_VMEM] * 2,
        out_specs=[IN_VMEM] * 3,
        out_shape=[
            jax.ShapeDtypeStruct((length, width), f32),
            jax.ShapeDtypeStruct((length, width), bf16),
            jax.ShapeDtypeStruct((4, length + SMALL, outs[0].shape[0]), bf16),
        ],
        scratch_shapes=[
            pltpu.VMEM((count, width, hidden), bf16),
            pltpu.VMEM((count, width, hidden), bf16),
            pltpu.VMEM((count, hidden, width), bf16),
            pltpu.VMEM((count, length, hidden), bf16),
            pltpu.VMEM((count, length, hidden), bf16),
            wide,
            wide,
            wide,
            pltpu.VMEM(inverse.shape, f32),
            pltpu.VMEM((4, *outs[0].shape), bf16),
            pltpu.SemaphoreType.DMA((count, 3)),
            pltpu.SemaphoreType.DMA((count, 2)),
            pltpu.SemaphoreType.DMA((len(late),)),
        ],
        compiler_params=pltpu.CompilerParams(vmem_limit_bytes=VMEM),
        cost_estimate=pl.CostEstimate(
            flops=6 * length * width * hidden * count,
            bytes_accessed=24 * 2**20,
            transcendentals=length * hidden * count,
        ),
        name="feed_back",
    )(low2, *args, *saved, *late, gain, small)


def weights_kernel(*refs):
    rows, grads, weights, refs = refs[:4], refs[4:8], refs[8:11], refs[11:]
    targets, refs = refs[:3], refs[3:]
    gate, up, down, low, low_t, low2, dgate, dup, hidden_t, result, sem, out_sem = refs
    block = rows[0].shape[0]
    at = [pl.ds(n * block, block) for n in range(4)]

    def fetch(n):
        return [
            start(rows[n], low.at[at[n], :], sem.at[n, 0]),
            start(grads[n], low2.at[at[n], :], sem.at[n, 1]),
        ]

    coming = [fetch(0)]
    own = [start(w, buffer, sem.at[4 + k, 0]) for k, (w, buffer) in enumerate(zip(weights, (gate, up, down)))]
    coming.append(fetch(1))
    for copy in own:
        copy.wait()
    for n in range(4):
        if n + 2 < 4:
            coming.append(fetch(n + 2))
        for copy in coming[n]:
            copy.wait()
        here = low[at[n], :]
        low_t[:, at[n]] = here.T
        gate_pre, up_pre = feed(here, gate[...], up[...])
        grad_hidden = dot_nt(low2[at[n], :], down[...])
        dgate[at[n], :], dup[at[n], :] = feed_back(grad_hidden, gate_pre, up_pre)
        hidden_t[:, at[n]] = hidden_of(gate_pre, up_pre).T
    going = []
    for k, (left, right) in enumerate([(low_t, dgate), (low_t, dup), (hidden_t, low2)]):
        result[k] = dot(left[...], right[...]).astype(bf16)
        going.append(start(result.at[k], targets[k], out_sem.at[k]))
    for copy in going:
        copy.wait()


def weight_grads(rows, grads, gate, up, down):
    block, width = rows[0].shape
    length, hidden = 4 * block, gate.shape[1]
    return pl.pallas_call(
        weights_kernel,
        in_specs=[ANY] * 11,
        out_specs=[ANY] * 3,
        out_shape=[
            jax.ShapeDtypeStruct((width, hidden), bf16),
            jax.ShapeDtypeStruct((width, hidden), bf16),
            jax.ShapeDtypeStruct((hidden, width), bf16),
        ],
        scratch_shapes=[
            pltpu.VMEM((width, hidden), bf16),
            pltpu.VMEM((width, hidden), bf16),
            pltpu.VMEM((hidden, width), bf16),
            pltpu.VMEM((length, width), bf16),
            pltpu.VMEM((width, length), bf16),
            pltpu.VMEM((length, width), bf16),
            pltpu.VMEM((length, hidden), bf16),
            pltpu.VMEM((length, hidden), bf16),
            pltpu.VMEM((hidden, length), bf16),
            pltpu.VMEM((3, width, hidden), bf16),
            pltpu.SemaphoreType.DMA((7, 2)),
            pltpu.SemaphoreType.DMA((3,)),
        ],
        compiler_params=pltpu.CompilerParams(vmem_limit_bytes=VMEM),
        cost_estimate=pl.CostEstimate(
            flops=12 * length * width * hidden, bytes_accessed=16 * 2**20, transcendentals=length * hidden
        ),
        name="feed_weights",
    )(*rows, *grads, gate, up, down)


def positions(segments):
    places = jnp.arange(segments.shape[0], dtype=jnp.int32)
    before = jnp.concatenate([segments[:1] - 1, segments[:-1]])
    starts = lax.cummax(jnp.where(segments != before, places, 0), axis=0)
    return (places - starts).astype(f32)


def relative_rows(value, blocks):
    me = lax.axis_index("tensor")
    rows = value.shape[0] // blocks
    return jnp.concatenate(
        [lax.dynamic_slice_in_dim(value, (me ^ j) * rows, rows, 0) for j in range(blocks)], axis=0
    )


def wide_weight(query_weight, key_weight, value_weight, heads):
    width = query_weight.shape[0]
    half = HEAD_DIM // 2

    def turned(weight):
        w = weight.reshape(width, heads, HEAD_DIM)
        swapped = jnp.concatenate([w[..., half:], w[..., :half]], axis=-1)
        return jnp.concatenate([w, swapped], axis=-1).reshape(width, heads * WIDE)

    v = value_weight.reshape(width, heads, HEAD_DIM)
    v = jnp.concatenate([v, jnp.zeros_like(v)], axis=-1).reshape(width, heads * WIDE)
    return jnp.concatenate([turned(query_weight), turned(key_weight), v], axis=1)


def local(
    tokens,
    segment_ids,
    query_weight,
    key_weight,
    value_weight,
    output_weight,
    attn_gain,
    attn_shift,
    gate_weight,
    up_weight,
    down_weight,
    mlp_gain,
    mlp_shift,
    cotangent,
):
    own = tokens[0]
    segments = segment_ids[0]
    head_width = query_weight.shape[1]
    heads = head_width // HEAD_DIM
    group = lax.axis_size("tensor")
    block = own.shape[0]
    dp = lax.axis_size("dp")
    bits = list(range(int(math.log2(dp))))
    orders = [bits, bits[1:] + bits[:1]]

    near = lambda a: swap(a, "tensor", 1)
    far = lambda a: swap(a, "tensor", 2)

    share = gate_weight.shape[0] // dp
    at = lax.axis_index("dp") * share
    mine = jnp.concatenate(
        [lax.dynamic_slice_in_dim(w, at, share, 0) for w in (gate_weight, up_weight)], axis=1
    )
    far_own = far(after(own, mine))
    mine = far(mine)
    near_own = near(own)
    near_weights = [near(w) for w in (gate_weight, up_weight, down_weight, output_weight)]

    angle_rate = ROPE_BASE ** (-(jnp.arange(HEAD_DIM // 2, dtype=f32) * 2.0 / HEAD_DIM))
    rates = jnp.concatenate([angle_rate, angle_rate, jnp.zeros(HEAD_DIM, f32)])
    signs = jnp.concatenate([-jnp.ones(HEAD_DIM // 2, f32), jnp.ones(HEAD_DIM // 2, f32), jnp.zeros(HEAD_DIM, f32)])
    angles = relative_rows(positions(segments), group)[:, None] * rates[None, :]
    cos_wide, sin_wide = jnp.cos(angles), jnp.sin(angles) * signs[None, :]
    seg = relative_rows(segments, group)[:, None]

    joint_wide = wide_weight(query_weight, key_weight, value_weight, heads)
    mine = after(mine, cos_wide)
    far_mixed = lax.all_gather(mine, "dp", axis=0, tiled=True)
    near_gate, near_up, near_down, near_out = all_after(near_weights, mine)
    tables = (joint_wide, cos_wide, sin_wide, seg, heads)
    near_half = project([after(own, near_gate, near_up, near_down, near_out), near_own], 0, *tables)
    far_own, _ = all_after([far_own, near_half[0]])
    both_own = near(far_own)
    far_out = far(after(output_weight, far_own))
    far_down = far(after(down_weight, far_own))
    x_full, qa, ka, va = project([far_own, both_own], 2, *tables, done=near_half)

    def send(value, j):
        return swap(value[j * block : (j + 1) * block], "tensor", j)

    half = attend(qa, ka, va, 2 * block, 2 * block)
    slices = [half[0][j * block : (j + 1) * block] for j in (2, 3)]
    far_out = after(far_out, half[0])
    ctx_far = [swap(c, "tensor", j) for c, j in zip(slices, (2, 3))]
    both_out = near(far_out)
    ctx, qb = attend(after(qa, far_out, *slices), ka, va, 0, 2 * block, done=half)
    far_mixed, far_down, both_out, *ctx_far = all_after([far_mixed, far_down, both_out, *ctx_far], ctx)
    ctx_parts = [ctx[:block], send(ctx, 1), *ctx_far]
    both_mixed, both_down = near(far_mixed), near(far_down)
    outs = [output_weight, near_out, far_out, both_out]
    sides = lambda a: ((a, 0), (a, 1))
    row = lambda a: a[None, :]

    first_norm, inverse, normed_low = mix(own, ctx_parts, outs, row(attn_gain), row(attn_shift))
    near_rows, far_rows = near(normed_low), far(normed_low)
    first_shards = [
        ((gate_weight, 0), (up_weight, 0), down_weight),
        ((near_gate, 0), (near_up, 0), near_down),
    ]
    gates_a, ups_a, half_way = forward(normed_low, first_shards)
    both_mixed, both_down = all_after([both_mixed, both_down], half_way)
    shards = first_shards + [(*sides(far_mixed), far_down), (*sides(both_mixed), both_down)]
    gates_b, ups_b, encoded, grad_second, grad_low, small = forward(
        normed_low,
        shards[2:],
        (half_way, first_norm, cotangent[0], row(attn_gain), row(attn_shift), row(mlp_gain), row(mlp_shift)),
    )
    near_rows, far_rows = all_after([near_rows, far_rows], grad_low)
    both_rows = near(far_rows)
    near_grads, far_grads = near(grad_low), far(grad_low)
    grad_first, grad_attn_low, grad_ctx = backward(
        after(grad_low, far_rows),
        shards,
        (gates_a, ups_a, gates_b, ups_b),
        grad_second,
        first_norm,
        inverse,
        outs,
        row(attn_gain),
        small,
    )
    near_grads, far_grads, both_rows = all_after([near_grads, far_grads, both_rows], grad_first)
    both_grads = near(far_grads)
    own_ctx, *sent_ctx = [grad_ctx[j] for j in range(group)]
    got_ctx = [swap(g, "tensor", j + 1) for j, g in enumerate(sent_ctx)]
    grad_out = [dot_tn(c, grad_attn_low) for c in ctx_parts]
    both_grads, *grad_out = all_after([both_grads, *grad_out])

    grad_gate, grad_up, grad_down = weight_grads(
        [after(normed_low, *sent_ctx), near_rows, far_rows, both_rows],
        [grad_low, near_grads, far_grads, both_grads],
        gate_weight,
        up_weight,
        down_weight,
    )
    grad_ctx = [own_ctx, *all_after(got_ctx, grad_down)]
    grad_gate = lax.psum(grad_gate, "dp")
    sums = [Sum(grad_up, orders[0]), Sum(grad_down, orders[1])]

    parts, grad_heads = [], []
    for h in range(heads):
        tied = all_after(grad_ctx, *[s.sent for s in sums])
        dq, dkv = attend_back(h, qb, ka, va, tied, ctx, cos_wide, sin_wide)
        part = jnp.concatenate([dq, dkv], axis=1)
        parts.append(part)
        for s in sums:
            s.advance(dq)
        grad_heads.append(dot_tn(part, x_full).astype(bf16))
        if h == 0:
            grad_out = scatter_sum(all_after(grad_out, dq), "tensor").astype(bf16)
            small = sum(g[block:].astype(f32) for g in all_after(grad_ctx, dq))
            small = (small[: SMALL // 2] + small[SMALL // 2 :]).reshape(4, 4, head_width)
            small = small.transpose(1, 0, 2).reshape(4, -1).astype(bf16)
        if h == heads - 2:
            most = jnp.concatenate([grad_out, *grad_heads, small], axis=0)
            sums.append(Sum(jnp.pad(most, ((0, -len(most) % (16 * dp)), (0, 0))), orders[0]))
    sums.append(Sum(grad_heads[-1], orders[1]))
    weights = [query_weight, key_weight, value_weight]
    columns = [
        jnp.concatenate([p[:, n * HEAD_DIM : (n + 1) * HEAD_DIM] for p in parts], axis=1)
        for n in range(3)
    ]
    back = [
        sum(dot_nt(c[j * block : (j + 1) * block], w) for c, w in zip(columns, weights))
        for j in range(group)
    ]
    grad_tokens = grad_first + scatter_sum(back, "tensor")
    while any(s.result is None for s in sums):
        for s in sums:
            s.advance()
    grad_up, grad_down, most, final = (s.result.astype(f32) for s in sums)
    grad_out, small = most[:head_width], most[heads * head_width : heads * head_width + 4]
    joint = jnp.concatenate([most[head_width : heads * head_width], final], axis=0)
    joint = joint.reshape(heads, 3, HEAD_DIM, -1)
    grad_joint = [joint[:, n].reshape(head_width, -1).T for n in range(3)]
    return (
        encoded[None],
        grad_tokens[None],
        *grad_joint,
        grad_out,
        small[0],
        small[1],
        grad_gate.astype(f32),
        grad_up,
        grad_down,
        small[2],
        small[3],
    )


def solution(mesh):
    rows, cols, lead = P("dp", "tensor", None), P(None, "tensor"), P("tensor", None)
    return jax.shard_map(
        local,
        mesh=mesh,
        in_specs=(
            rows, P("dp", None), cols, cols, cols, lead, P(), P(), cols, cols, lead, P(), P(), rows,
        ),
        out_specs=(
            rows, rows, cols, cols, cols, lead, P(), P(), cols, cols, lead, P(), P(),
        ),
        check_vma=False,
    )
```

```python
import functools
import math

import jax
import jax.numpy as jnp
from jax import lax
from jax.experimental import pallas as pl
from jax.experimental.pallas import tpu as pltpu
from jax.sharding import PartitionSpec as P

HEAD_DIM = 64
EPSILON = 1e-05
ROPE_BASE = 1000.0
APART = -(2.0**30)
WIDE = 128
SEGMENTS = 7
SEG_AT = HEAD_DIM
ROW_AT = HEAD_DIM + 8
VMEM = 60 * 2**20
VMEM_LESS = 44 * 2**20
SMALL_COST = pl.CostEstimate(flops=2**20, bytes_accessed=2**16, transcendentals=0)
bf16 = jnp.bfloat16
f32 = jnp.float32
NT = (((1,), (1,)), ((), ()))
TN = (((0,), (0,)), ((), ()))


def dot(a, b):
    return jnp.dot(a, b, preferred_element_type=f32)


def dot_nt(a, b):
    return lax.dot_general(a, b, NT, preferred_element_type=f32)


def dot_tn(a, b):
    return lax.dot_general(a, b, TN, preferred_element_type=f32)


def swap(value, axis, bit):
    size = lax.axis_size(axis)
    return lax.ppermute(value, axis, [(i, i ^ bit) for i in range(size)])


def after(value, *others):
    return lax.optimization_barrier((value, *others))[0]


def all_after(values, *others):
    return list(lax.optimization_barrier((tuple(values), others))[0])


def scatter_sum(blocks, axis):
    held = dict(enumerate(blocks))
    rows = blocks[0].shape[0]
    step = 1
    while step < len(blocks):
        sent = [k for k in held if k & step]
        got = [held.pop(k).astype(bf16) for k in sent]
        got = swap(got[0] if len(got) == 1 else jnp.concatenate(got, axis=0), axis, step)
        for n, k in enumerate(sent):
            held[k ^ step] = held[k ^ step] + got[n * rows : (n + 1) * rows].astype(f32)
        step *= 2
    return held[0]


def peers(axis, bits):
    me = lax.axis_index(axis)
    mine = sum(((me >> bit) & 1) << n for n, bit in enumerate(bits))
    far = [sum(((j >> n) & 1) << bit for n, bit in enumerate(bits)) for j in range(1 << len(bits))]
    return mine, far


def split_rows(value, axis, bits):
    mine, far = peers(axis, bits)
    rows = value.shape[0] // len(far)
    return [lax.dynamic_slice_in_dim(value, (mine ^ j) * rows, rows, 0) for j in range(len(far))]


def join_rows(parts, axis, bits):
    mine, _ = peers(axis, bits)

    def pick(p):
        value = parts[-1]
        for j in reversed(range(len(parts) - 1)):
            value = jnp.where(mine == p ^ j, parts[j], value)
        return value

    return jnp.concatenate([pick(p) for p in range(len(parts))], axis=0)


def sum_steps(parts, axis, groups):
    for n, bits in enumerate(groups):
        if n:
            parts = split_rows(value, axis, bits)
        _, far = peers(axis, bits)
        got = yield parts[1:], [swap(part, axis, step) for part, step in zip(parts[1:], far[1:])]
        value = sum((g.astype(f32) for g in got), parts[0].astype(f32)).astype(bf16)
    for bits in reversed(groups):
        _, far = peers(axis, bits)
        got = yield [value], [swap(value, axis, step) for step in far[1:]]
        value = join_rows([value, *got], axis, bits)
    return value


class Sum:
    def __init__(self, parts, groups):
        self.steps = sum_steps(parts, "dp", groups)
        self.result = None
        self.sent, self.got = next(self.steps)

    def take(self, got):
        if self.result is None:
            try:
                self.sent, self.got = self.steps.send(got)
            except StopIteration as end:
                self.result, self.sent, self.got = end.value, [], []


def take_round(sums, *others):
    got, others = lax.optimization_barrier(([s.got for s in sums], others))
    for s, g in zip(sums, got):
        s.take(g)
    return list(others)


def swap_halves(value, lane):
    half = HEAD_DIM // 2
    return jnp.where(
        lane < half, pltpu.roll(value, WIDE - half, 1), pltpu.roll(value, half, 1)
    )


def project_kernel(heads, start, count, me_ref, *refs):
    pieces, refs = refs[:count], refs[count:]
    weights, (seg_ref, rate_ref) = refs[:3], refs[3:5]
    x_ref, qa_ref, ka_ref, va_ref, cos_ref, sin_ref = refs[-6:]
    rows = x_ref.shape[0]
    step = pl.program_id(0)
    for n, piece in enumerate(pieces):

        @pl.when(step == n)
        def _(piece=piece):
            x_ref[...] = piece[...]

    x = x_ref[...]
    query, key, value = (dot_nt(x, w[...]) for w in weights)

    segs = seg_ref[...]
    order = jnp.where(segs < 0, SEGMENTS - 1, segs)
    first_place = jnp.zeros_like(order)
    for s in range(1, SEGMENTS):
        before = jnp.sum((order < s).astype(jnp.int32), axis=1, keepdims=True)
        first_place = jnp.where(order == s, before, first_place)
    places = lax.broadcasted_iota(jnp.int32, segs.shape, 1) - first_place

    def column(values):
        mine = me_ref[0] ^ (start + step)
        block = values[:, -rows:]
        for n in range(values.shape[1] // rows - 1):
            block = jnp.where(mine == n, values[:, n * rows : (n + 1) * rows], block)
        return jnp.broadcast_to(block.astype(f32), (WIDE, rows)).T

    angles = column(places) * rate_ref[...]
    seg = column(segs).astype(jnp.int32)
    lane = lax.broadcasted_iota(jnp.int32, (rows, WIDE), 1)
    cosine, sine = jnp.cos(angles), jnp.sin(angles)
    sine = jnp.where(lane < HEAD_DIM // 2, -sine, sine)
    cos_ref[...], sin_ref[...] = cosine, sine
    first = lane < HEAD_DIM
    same = lane == seg + (SEG_AT + 1)
    qf = jnp.where(same, APART, 0.0)
    kf = jnp.where((lane < ROW_AT + 3) & ~same, 1.0, 0.0)
    ones = jnp.where(lane < HEAD_DIM + 3, 1.0, 0.0)

    def part(values, h):
        at = h * HEAD_DIM
        if h % 2:
            return pltpu.roll(values[:, at - HEAD_DIM : at + HEAD_DIM], HEAD_DIM, 1)
        if h + 1 < heads:
            return values[:, at : at + WIDE]
        here = values[:, at : at + HEAD_DIM]
        return jnp.concatenate([here, jnp.zeros_like(here)], axis=1)

    for h in range(heads):
        q, k = part(query, h), part(key, h)
        q = q * cosine + swap_halves(q, lane) * sine
        k = k * cosine + swap_halves(k, lane) * sine
        qa_ref[h] = jnp.where(first, q * (1.0 / math.sqrt(HEAD_DIM)), qf).astype(bf16)
        ka_ref[h] = jnp.where(first, k, kf).astype(bf16)
        va_ref[h] = jnp.where(first, part(value, h), ones).astype(bf16)


def project(pieces, start, weights, segments, rates, heads, done=()):
    block, width = pieces[0].shape
    length = segments.shape[1]
    rows = lambda n: pl.BlockSpec((block, n), lambda i: (start + i, 0))
    whole = lambda a: pl.BlockSpec(a.shape, lambda i: (0, 0))
    out = pl.BlockSpec((heads, block, WIDE), lambda i: (0, start + i, 0))
    given = 1 + len(pieces) + 5
    me = lax.axis_index("tensor").astype(jnp.int32)[None]
    return pl.pallas_call(
        functools.partial(project_kernel, heads, start, len(pieces)),
        grid=(len(pieces),),
        in_specs=[pl.BlockSpec(memory_space=pltpu.SMEM)]
        + [whole(p) for p in pieces]
        + [whole(w) for w in weights]
        + [whole(segments), whole(rates)]
        + [pl.BlockSpec(memory_space=pl.ANY)] * len(done),
        out_specs=[rows(width)] + [out] * 3 + [rows(WIDE)] * 2,
        out_shape=[jax.ShapeDtypeStruct((length, width), bf16)]
        + [jax.ShapeDtypeStruct((heads, length, WIDE), bf16)] * 3
        + [jax.ShapeDtypeStruct((length, WIDE), f32)] * 2,
        input_output_aliases={given + n: n for n in range(len(done))},
        compiler_params=pltpu.CompilerParams(vmem_limit_bytes=VMEM),
        cost_estimate=SMALL_COST,
        name="project",
    )(me, *pieces, *weights, segments, rates, *done)


def split3(value):
    high = value.astype(bf16).astype(f32)
    rest = value - high
    middle = rest.astype(bf16).astype(f32)
    return high, middle, rest - middle


def put_row(wide, at, value):
    lane = lax.broadcasted_iota(jnp.int32, wide.shape, 1)
    for n, part in enumerate(split3(value)):
        wide = jnp.where(lane == at + n, -part, wide)
    return wide


def attend_kernel(heads, qa_ref, ka_ref, va_ref, *refs):
    ctx_ref, qb_ref = refs[-2:]
    parts = []
    for h in range(heads):
        qa = qa_ref[h]
        scores = dot_nt(qa, ka_ref[h])
        peak = jnp.max(scores, axis=1, keepdims=True)
        weights = jnp.exp(scores - peak).astype(bf16)
        summed = dot(weights, va_ref[h])
        total = summed[:, HEAD_DIM : HEAD_DIM + 1]
        parts.append(summed[:, :HEAD_DIM] / total)
        qb_ref[h] = put_row(qa.astype(f32), ROW_AT, peak + jnp.log(total)).astype(bf16)
    ctx_ref[...] = jnp.concatenate(parts, axis=1).astype(bf16)


def attend(qa, ka, va, start, count, done=(), block=256):
    heads, length, _ = qa.shape
    first = start // block
    whole = pl.BlockSpec((heads, length, WIDE), lambda i: (0, 0, 0))
    part = pl.BlockSpec((heads, block, WIDE), lambda i: (0, first + i, 0))
    return pl.pallas_call(
        functools.partial(attend_kernel, heads),
        grid=(count // block,),
        in_specs=[part, whole, whole] + [pl.BlockSpec(memory_space=pl.ANY)] * len(done),
        out_specs=[pl.BlockSpec((block, heads * HEAD_DIM), lambda i: (first + i, 0)), part],
        out_shape=[
            jax.ShapeDtypeStruct((length, heads * HEAD_DIM), bf16),
            jax.ShapeDtypeStruct((heads, length, WIDE), bf16),
        ],
        input_output_aliases={3 + n: n for n in range(len(done))},
        compiler_params=pltpu.CompilerParams(vmem_limit_bytes=VMEM_LESS),
        cost_estimate=SMALL_COST,
        name="attend",
    )(qa, ka, va, *done)


def attend_back_kernel(heads, qb_ref, ka_ref, va_ref, *refs):
    gos, refs = refs[:4], refs[4:]
    ctx_ref, cos_ref, sin_ref, dq_ref, dk_ref, dv_ref, doa, dqt = refs
    j, h = pl.program_id(0), pl.program_id(1)
    length = qb_ref.shape[1]
    block = length // 4
    at = [pl.ds(i * block, block) for i in range(4)]

    for head in range(heads):
        cols = pl.ds(head * HEAD_DIM, HEAD_DIM)

        @pl.when((j == 0) & (h == head))
        def _(cols=cols):
            for i in range(4):
                go = gos[i][:block, cols].astype(f32)
                delta = jnp.sum(go * ctx_ref[at[i], cols].astype(f32), axis=1, keepdims=True)
                wide = jnp.concatenate([go, jnp.zeros_like(go)], axis=1)
                doa[h, at[i], :] = put_row(wide, HEAD_DIM, delta).astype(bf16)

    @pl.when(j == 0)
    def _():
        dqt[h] = jnp.zeros(dqt.shape[1:], f32)

    ka, va = ka_ref[h], va_ref[h]
    kt = ka.astype(f32).T[:HEAD_DIM].astype(bf16)
    dk = dv = None
    for i in range(4):
        qb, do = qb_ref[h, at[i], :], doa[h, at[i], :]
        weights = jnp.exp(dot_nt(ka, qb))
        grads = (weights * dot_nt(va, do)).astype(bf16)
        v_part = dot(weights.astype(bf16), do)
        k_part = dot(grads, qb)
        dk = k_part if i == 0 else dk + k_part
        dv = v_part if i == 0 else dv + v_part
        dqt[h, :, at[i]] += dot(kt, grads)
    lane = lax.broadcasted_iota(jnp.int32, dk.shape, 1)
    rows = pl.ds(pl.multiple_of(j * ka.shape[0], ka.shape[0]), ka.shape[0])
    dk = dk * cos_ref[rows, :] - swap_halves(dk, lane) * sin_ref[rows, :]
    for head in range(heads):
        cols = pl.ds(head * HEAD_DIM, HEAD_DIM)

        @pl.when(h == head)
        def _(cols=cols):
            dk_ref[:, cols] = dk[:, :HEAD_DIM].astype(bf16)
            dv_ref[:, cols] = dv[:, :HEAD_DIM].astype(bf16)

        @pl.when((h == head) & (j == pl.num_programs(0) - 1))
        def _(cols=cols):
            for i in range(4):
                part = dqt[h, :, at[i]]
                dq = jnp.concatenate([part, jnp.zeros_like(part)], axis=0).T
                lanes = lax.broadcasted_iota(jnp.int32, dq.shape, 1)
                dq = dq * cos_ref[at[i], :] - swap_halves(dq, lanes) * sin_ref[at[i], :]
                dq_ref[at[i], cols] = (dq[:, :HEAD_DIM] * (1.0 / math.sqrt(HEAD_DIM))).astype(bf16)


def attend_back(qb, ka, va, gos, ctx, cosine, sine, block_k=512):
    heads, length, _ = qb.shape
    part = pl.BlockSpec((heads, block_k, WIDE), lambda j, h: (0, j, 0))
    full = lambda a: pl.BlockSpec(a.shape, lambda j, h, r=len(a.shape): (0,) * r)
    grad = jax.ShapeDtypeStruct((length, heads * HEAD_DIM), bf16)
    rows = pl.BlockSpec((block_k, heads * HEAD_DIM), lambda j, h: (j, 0))
    return pl.pallas_call(
        functools.partial(attend_back_kernel, heads),
        grid=(length // block_k, heads),
        in_specs=[full(qb), part, part] + [full(a) for a in (*gos, ctx, cosine, sine)],
        out_specs=[full(grad), rows, rows],
        out_shape=[grad] * 3,
        scratch_shapes=[pltpu.VMEM((heads, length, WIDE), bf16), pltpu.VMEM((heads, HEAD_DIM, length), f32)],
        compiler_params=pltpu.CompilerParams(vmem_limit_bytes=VMEM),
        cost_estimate=SMALL_COST,
        name="attend_back",
    )(qb, ka, va, *gos, ctx, cosine, sine)


ANY = pl.BlockSpec(memory_space=pl.ANY)
IN_VMEM = pl.BlockSpec(memory_space=pltpu.VMEM)


def start(source, target, sem):
    copy = pltpu.make_async_copy(source, target, sem)
    copy.start()
    return copy


def norm_parts(row_values):
    centred = row_values - jnp.mean(row_values, axis=-1, keepdims=True)
    inverse = lax.rsqrt(jnp.mean(centred * centred, axis=-1, keepdims=True) + EPSILON)
    return (centred * inverse, inverse)


def norm_back(grad_norm, normalized, inverse):
    return inverse * (
        grad_norm
        - jnp.mean(grad_norm, axis=-1, keepdims=True)
        - normalized * jnp.mean(grad_norm * normalized, axis=-1, keepdims=True)
    )


def mix_kernel(own_ref, *refs):
    parts, outs, refs = refs[:4], refs[4:8], refs[8:]
    gain_ref, shift_ref, norm_ref, inverse_ref, low_ref = refs
    total = own_ref[...].astype(f32)
    for part, out in zip(parts, outs):
        total = total + dot(part[...], out[...])
    norm, inverse = norm_parts(total)
    norm_ref[...] = norm
    inverse_ref[...] = jnp.broadcast_to(inverse, inverse_ref.shape)
    low_ref[...] = (norm * gain_ref[...] + shift_ref[...]).astype(bf16)


def mix(own, parts, outs, gain, shift, block=256):
    length, width = own.shape
    rows = lambda a: pl.BlockSpec((block, a.shape[1]), lambda i: (i, 0))
    whole = lambda a: pl.BlockSpec(a.shape, lambda i: (0, 0))
    shapes = [
        jax.ShapeDtypeStruct((length, width), f32),
        jax.ShapeDtypeStruct((length, WIDE), f32),
        jax.ShapeDtypeStruct((length, width), bf16),
    ]
    return pl.pallas_call(
        mix_kernel,
        grid=(length // block,),
        in_specs=[rows(own)] + [rows(p) for p in parts] + [whole(w) for w in outs] + [whole(gain), whole(shift)],
        out_specs=[rows(s) for s in shapes],
        out_shape=shapes,
        compiler_params=pltpu.CompilerParams(vmem_limit_bytes=VMEM),
        cost_estimate=SMALL_COST,
        name="mix",
    )(own, *parts, *outs, gain, shift)


def sigmoid(value):
    return 0.5 * jnp.tanh(0.5 * value) + 0.5


def feed(low, gate, up):
    gate_pre, up_pre = dot(low, gate), dot(low, up)
    return gate_pre, up_pre


def hidden_of(gate_pre, up_pre):
    return (gate_pre * sigmoid(gate_pre) * up_pre).astype(bf16)


def feed_back(grad_hidden, gate_pre, up_pre):
    part = sigmoid(gate_pre)
    active = gate_pre * part
    grad_gate = grad_hidden * up_pre * (part + active * (1.0 - part))
    return grad_gate.astype(bf16), (grad_hidden * active).astype(bf16)


def shard_copies(n, firsts, shards, buffers, sem):
    copies = []
    for k, buffer in enumerate(buffers):
        width = buffer.shape[2]
        source = shards[3 * n + k].at[:, pl.ds(firsts[3 * n + k] * width, width)]
        copies.append(start(source, buffer.at[n], sem.at[n, k]))
    return copies


def shard_args(shards):
    return [a for shard in shards for a, _ in shard], [first for shard in shards for _, first in shard]


HALVES = 2


def halves(length):
    return [pl.ds(n * (length // HALVES), length // HALVES) for n in range(HALVES)]


def forward_kernel(firsts, last, low_ref, *refs):
    count = len(firsts) // 3
    shards, refs = refs[: 3 * count], refs[3 * count :]
    if last:
        first_ref, then_ref, norm_ref, cot_ref, gain_ref, shift_ref, gain2_ref, shift2_ref = refs[:8]
        gates_ref, ups_ref, encoded_ref, second_ref, low2_ref, small_ref = refs[8:14]
        gate, up, down, gates, ups, sem, out_sem, total, before, then, norm1, cot_in, more_sem = refs[14:]
    else:
        gates_ref, ups_ref, total, gate, up, down, gates, ups, sem, out_sem = refs
    buffers = (gate, up, down)
    coming = [shard_copies(0, firsts, shards, buffers, sem)]
    if last:
        extra = [
            start(ref, buffer, more_sem.at[n])
            for n, (ref, buffer) in enumerate(
                [(first_ref, before), (then_ref, then), (norm_ref, norm1), (cot_ref, cot_in)]
            )
        ]
    going = []
    hidden = down.shape[1]
    for n in range(count):
        if n + 1 < count:
            coming.append(shard_copies(n + 1, firsts, shards, buffers, sem))
        for copy in coming[n]:
            copy.wait()
        for at in halves(low_ref.shape[0]):
            gate_pre, up_pre = feed(low_ref[at, :], gate[n], up[n])
            gates[n, at, :] = gate_pre.astype(bf16)
            ups[n, at, :] = up_pre.astype(bf16)
            part = dot(hidden_of(gate_pre, up_pre), down[n])
            total[at, :] = part if n == 0 else total[at, :] + part
        cols = pl.ds(n * hidden, hidden)
        going.append(start(gates.at[n], gates_ref.at[:, cols], out_sem.at[n, 0]))
        going.append(start(ups.at[n], ups_ref.at[:, cols], out_sem.at[n, 1]))
    if last:
        for copy in extra:
            copy.wait()
        normed = norm1[...] * gain_ref[...] + shift_ref[...]
        norm, inverse = norm_parts(normed + (before[...] + then[...] + total[...]))
        cot = cot_in[...].astype(f32)
        encoded_ref[...] = (norm * gain2_ref[...] + shift2_ref[...]).astype(bf16)
        second = norm_back(cot * gain2_ref[...], norm, inverse)
        second_ref[...] = second
        low2_ref[...] = second.astype(bf16)
        small_ref[...] = jnp.concatenate(
            [jnp.sum(cot * norm, axis=0, keepdims=True), jnp.sum(cot, axis=0, keepdims=True)], axis=0
        )
    for copy in going:
        copy.wait()


def forward(low, shards, last=()):
    length, width = low.shape
    count, hidden = len(shards), shards[0][2][0].shape[0]
    args, firsts = shard_args(shards)
    shapes = [jax.ShapeDtypeStruct((length, hidden * count), bf16)] * 2
    out_specs = [ANY, ANY]
    scratch = [
        pltpu.VMEM((count, width, hidden), bf16),
        pltpu.VMEM((count, width, hidden), bf16),
        pltpu.VMEM((count, hidden, width), bf16),
        pltpu.VMEM((count, length, hidden), bf16),
        pltpu.VMEM((count, length, hidden), bf16),
        pltpu.SemaphoreType.DMA((count, 3)),
        pltpu.SemaphoreType.DMA((count, 2)),
    ]
    if last:
        shapes += [
            jax.ShapeDtypeStruct((length, width), bf16),
            jax.ShapeDtypeStruct((length, width), f32),
            jax.ShapeDtypeStruct((length, width), bf16),
            jax.ShapeDtypeStruct((2, width), f32),
        ]
        out_specs += [IN_VMEM] * 4
        wide = pltpu.VMEM((length, width), f32)
        scratch += [wide] * 4 + [pltpu.VMEM((length, width), bf16), pltpu.SemaphoreType.DMA((4,))]
    else:
        shapes.append(jax.ShapeDtypeStruct((length, width), f32))
        out_specs.append(IN_VMEM)
    return pl.pallas_call(
        functools.partial(forward_kernel, firsts, bool(last)),
        in_specs=[IN_VMEM] + [ANY] * len(args) + [ANY] * len(last[:4]) + [IN_VMEM] * len(last[4:]),
        out_specs=out_specs,
        out_shape=shapes,
        scratch_shapes=scratch,
        compiler_params=pltpu.CompilerParams(vmem_limit_bytes=VMEM),
        cost_estimate=SMALL_COST,
        name="feed_forward",
    )(low, *args, *last)


def backward_kernel(firsts, where, low2_ref, *refs):
    count = len(firsts) // 3
    shards, refs = refs[: 3 * count], refs[3 * count :]
    pairs = where[-1][0] + 1
    saved, refs = refs[: 2 * pairs], refs[2 * pairs :]
    late_refs, refs = refs[:7], refs[7:]
    gain_ref, small_in_ref, first_ref, low_ref, *ctx_refs = refs[:8]
    gate, up, down, gates, ups, total, second, norm1, inverse, outs, sem, saved_sem, late_sem = refs[8:]
    buffers = (gate, up, down)
    hidden = down.shape[1]

    def fetch(n):
        part, cols = where[n][0], pl.ds(where[n][1] * hidden, hidden)
        return shard_copies(n, firsts, shards, buffers, sem) + [
            start(ref.at[:, cols], buffer.at[n], saved_sem.at[n, k])
            for k, (ref, buffer) in enumerate(zip(saved[2 * part : 2 * part + 2], (gates, ups)))
        ]

    coming = [fetch(0)]
    late = []
    for n in range(count):
        if n + 1 < count:
            coming.append(fetch(n + 1))
        else:
            targets = [second, norm1, inverse] + [outs.at[k] for k in range(4)]
            late = [start(ref, target, late_sem.at[k]) for k, (ref, target) in enumerate(zip(late_refs, targets))]
        for copy in coming[n]:
            copy.wait()
        for at in halves(low2_ref.shape[0]):
            grad_hidden = dot_nt(low2_ref[at, :], down[n])
            grad_gate, grad_up = feed_back(grad_hidden, gates[n, at, :].astype(f32), ups[n, at, :].astype(f32))
            part = dot_nt(grad_gate, gate[n]) + dot_nt(grad_up, up[n])
            total[at, :] = part if n == 0 else total[at, :] + part
    for copy in late:
        copy.wait()
    normed_grad, norm = second[...] + total[...], norm1[...]
    first = norm_back(normed_grad * gain_ref[...], norm, inverse[:, :1])
    first_ref[...] = first
    low = first.astype(bf16)
    low_ref[...] = low
    small = jnp.concatenate(
        [
            jnp.sum(normed_grad * norm, axis=0, keepdims=True),
            jnp.sum(normed_grad, axis=0, keepdims=True),
            small_in_ref[...],
        ],
        axis=0,
    )
    width = outs.shape[1]
    small = jnp.concatenate([small[:, k * width : (k + 1) * width] for k in range(4)], axis=0)
    high = small.astype(bf16)
    small = jnp.concatenate([high, (small - high.astype(f32)).astype(bf16)], axis=0)
    length = low.shape[0]
    for k in range(4):
        ctx_refs[k][:length, :] = dot_nt(low, outs[k]).astype(bf16)
        ctx_refs[k][length:, :] = small


SMALL = 32


def backward(low2, shards, saved, second, norm, inverse, outs, gain, small):
    length, width = low2.shape
    count, hidden = len(shards), shards[0][2][0].shape[0]
    args, firsts = shard_args(shards)
    where = [(n, k) for n, (gates, _) in enumerate(saved) for k in range(gates.shape[1] // hidden)]
    saved = [a for pair in saved for a in pair]
    late = [second, norm, inverse, *outs]
    wide = pltpu.VMEM((length, width), f32)
    return pl.pallas_call(
        functools.partial(backward_kernel, firsts, where),
        in_specs=[IN_VMEM] + [ANY] * (len(args) + len(saved) + len(late)) + [IN_VMEM] * 2,
        out_specs=[IN_VMEM] * 6,
        out_shape=[
            jax.ShapeDtypeStruct((length, width), f32),
            jax.ShapeDtypeStruct((length, width), bf16),
        ]
        + [jax.ShapeDtypeStruct((length + SMALL, outs[0].shape[0]), bf16)] * 4,
        scratch_shapes=[
            pltpu.VMEM((count, width, hidden), bf16),
            pltpu.VMEM((count, width, hidden), bf16),
            pltpu.VMEM((count, hidden, width), bf16),
            pltpu.VMEM((count, length, hidden), bf16),
            pltpu.VMEM((count, length, hidden), bf16),
            wide,
            wide,
            wide,
            pltpu.VMEM(inverse.shape, f32),
            pltpu.VMEM((4, *outs[0].shape), bf16),
            pltpu.SemaphoreType.DMA((count, 3)),
            pltpu.SemaphoreType.DMA((count, 2)),
            pltpu.SemaphoreType.DMA((len(late),)),
        ],
        compiler_params=pltpu.CompilerParams(vmem_limit_bytes=VMEM),
        cost_estimate=SMALL_COST,
        name="feed_back",
    )(low2, *args, *saved, *late, gain, small)


def weights_kernel(*refs):
    rows, grads, weights, refs = refs[:4], refs[4:8], refs[8:11], refs[11:]
    target, refs = refs[0], refs[1:]
    gate, up, down, low, low_t, low2, dgate, dup, hidden_t, result, sem, out_sem = refs
    block = rows[0].shape[0]
    at = [pl.ds(n * block, block) for n in range(4)]

    def fetch(n):
        return [
            start(rows[n], low.at[at[n], :], sem.at[n, 0]),
            start(grads[n], low2.at[at[n], :], sem.at[n, 1]),
        ]

    coming = [fetch(0)]
    own = [start(w, buffer, sem.at[4 + k, 0]) for k, (w, buffer) in enumerate(zip(weights, (gate, up, down)))]
    coming.append(fetch(1))
    for copy in own:
        copy.wait()
    for n in range(4):
        if n + 2 < 4:
            coming.append(fetch(n + 2))
        for copy in coming[n]:
            copy.wait()
        here = low[at[n], :]
        low_t[:, at[n]] = here.T
        gate_pre, up_pre = feed(here, gate[...], up[...])
        grad_hidden = dot_nt(low2[at[n], :], down[...])
        dgate[at[n], :], dup[at[n], :] = feed_back(grad_hidden, gate_pre, up_pre)
        hidden_t[:, at[n]] = hidden_of(gate_pre, up_pre).T
    going = []
    for k, (left, right) in enumerate([(low_t, dgate), (low_t, dup), (hidden_t, low2)]):
        result[k] = dot(left[...], right[...]).astype(bf16)
        rows_at = pl.ds(k * result.shape[1], result.shape[1])
        going.append(start(result.at[k], target.at[rows_at, :], out_sem.at[k]))
    for copy in going:
        copy.wait()


def weight_grads(rows, grads, gate, up, down):
    block, width = rows[0].shape
    length, hidden = 4 * block, gate.shape[1]
    return pl.pallas_call(
        weights_kernel,
        in_specs=[ANY] * 11,
        out_specs=ANY,
        out_shape=jax.ShapeDtypeStruct((3 * width, hidden), bf16),
        scratch_shapes=[
            pltpu.VMEM((width, hidden), bf16),
            pltpu.VMEM((width, hidden), bf16),
            pltpu.VMEM((hidden, width), bf16),
            pltpu.VMEM((length, width), bf16),
            pltpu.VMEM((width, length), bf16),
            pltpu.VMEM((length, width), bf16),
            pltpu.VMEM((length, hidden), bf16),
            pltpu.VMEM((length, hidden), bf16),
            pltpu.VMEM((hidden, length), bf16),
            pltpu.VMEM((3, width, hidden), bf16),
            pltpu.SemaphoreType.DMA((7, 2)),
            pltpu.SemaphoreType.DMA((3,)),
        ],
        compiler_params=pltpu.CompilerParams(vmem_limit_bytes=VMEM),
        cost_estimate=SMALL_COST,
        name="feed_weights",
    )(*rows, *grads, gate, up, down)


def local(
    tokens,
    segment_ids,
    query_weight,
    key_weight,
    value_weight,
    output_weight,
    attn_gain,
    attn_shift,
    gate_weight,
    up_weight,
    down_weight,
    mlp_gain,
    mlp_shift,
    cotangent,
):
    own = tokens[0]
    head_width = query_weight.shape[1]
    heads = head_width // HEAD_DIM
    group = lax.axis_size("tensor")
    block = own.shape[0]
    dp = lax.axis_size("dp")
    bits = list(range(int(math.log2(dp))))
    groups = [bits[:1]] + [bits[n : n + 2] for n in range(1, len(bits), 2)]

    near = lambda a: swap(a, "tensor", 1)
    far = lambda a: swap(a, "tensor", 2)

    share = gate_weight.shape[0] // dp
    at = lax.axis_index("dp") * share
    mine = jnp.concatenate(
        [lax.dynamic_slice_in_dim(w, at, share, 0) for w in (gate_weight, up_weight)], axis=1
    )
    far_own = far(own)
    near_own = near(own)
    near_weights = [near(w) for w in (gate_weight, up_weight, down_weight, output_weight)]
    angle_rate = ROPE_BASE ** (-(jnp.arange(HEAD_DIM // 2, dtype=f32) * 2.0 / HEAD_DIM))
    rates = jnp.concatenate([angle_rate, angle_rate, jnp.zeros(HEAD_DIM, f32)])[None, :]
    tables = ([w.T for w in (query_weight, key_weight, value_weight)], segment_ids, rates, heads)
    near_half = project([after(own, mine, *near_weights), near_own], 0, *tables)
    near_gate, near_up, near_down, near_out = near_weights
    far_own = after(far_own, near_half[0])
    both_own = near(far_own)
    mine = after(mine, far_own)
    far_mine = far(mine)
    x_full, qa, ka, va, cosine, sine = project([far_own, after(both_own, mine)], 2, *tables, done=near_half)
    far_mine = after(far_mine, qa)
    far_mixed = lax.all_gather(far_mine, "dp", axis=0, tiled=True)
    out_sent = after(output_weight, far_mine)
    far_out = far(out_sent)
    qa = after(qa, out_sent)

    def send(value, j):
        return swap(value[j * block : (j + 1) * block], "tensor", j)

    half = attend(qa, ka, va, 2 * block, 2 * block)
    far_out, *slices = all_after([far_out, *(half[0][j * block : (j + 1) * block] for j in (2, 3))], half[0])
    ctx_far = [swap(c, "tensor", j) for c, j in zip(slices, (2, 3))]
    both_out = near(far_out)
    ctx, qb = attend(after(qa, far_out, *slices), ka, va, 0, 2 * block, done=half)
    both_out, *ctx_far = all_after([both_out, *ctx_far], ctx)
    near_ctx = send(ctx, 1)
    down_sent = after(down_weight, *ctx_far)
    far_down = far(down_sent)
    ctx_parts = [ctx[:block], near_ctx, *ctx_far]
    outs = [output_weight, near_out, far_out, both_out]
    row = lambda a: a[None, :]

    first_norm, inverse, normed_low = mix(
        after(own, down_sent), ctx_parts, outs, row(attn_gain), row(attn_shift)
    )
    near_rows = near(normed_low)
    near_shards = [
        ((gate_weight, 0), (up_weight, 0), (down_weight, 0)),
        ((near_gate, 0), (near_up, 0), (near_down, 0)),
    ]
    *saved_a, half_way = forward(normed_low, near_shards)
    far_mixed, far_down = all_after([far_mixed, far_down], half_way)
    both_mixed, both_down = near(far_mixed), near(far_down)
    rows_sent = after(normed_low, far_down)
    far_rows = far(rows_sent)
    far_shard = [((far_mixed, 0), (far_mixed, 1), (far_down, 0))]
    *saved_b, more_way = forward(after(normed_low, rows_sent, far_mixed), far_shard)
    both_mixed, both_down = all_after([both_mixed, both_down], more_way)
    both_shard = [((both_mixed, 0), (both_mixed, 1), (both_down, 0))]
    shards = near_shards + far_shard + both_shard
    *saved_c, encoded, grad_second, grad_low, small = forward(
        normed_low,
        both_shard,
        (
            half_way,
            more_way,
            first_norm,
            cotangent[0],
            row(attn_gain),
            row(attn_shift),
            row(mlp_gain),
            row(mlp_shift),
        ),
    )
    near_rows, far_rows = all_after([near_rows, far_rows], grad_low)
    both_rows = near(far_rows)
    near_grads, far_grads = near(grad_low), far(grad_low)
    grad_first, grad_attn_low, own_ctx, *sent_ctx = backward(
        after(grad_low, far_rows),
        shards,
        (saved_a, saved_b, saved_c),
        grad_second,
        first_norm,
        inverse,
        outs,
        row(attn_gain),
        small,
    )
    near_grads, far_grads, both_rows = all_after([near_grads, far_grads, both_rows], grad_first)
    both_grads = near(far_grads)
    got_ctx = [swap(g, "tensor", j + 1) for j, g in enumerate(sent_ctx)]
    grad_feed = weight_grads(
        [after(normed_low, *sent_ctx), near_rows, far_rows, both_rows],
        [grad_low, near_grads, far_grads, both_grads],
        gate_weight,
        up_weight,
        down_weight,
    )
    grad_ctx = all_after(got_ctx, grad_feed)
    feed_part = lax.psum_scatter(after(grad_feed, *grad_ctx), "dp", scatter_dimension=0, tiled=True)
    grad_ctx = [own_ctx, *grad_ctx]
    grad_attn_low = after(grad_attn_low, grad_feed)
    sent = jnp.concatenate([dot_tn(ctx_parts[j], grad_attn_low) for j in (1, 3)], axis=0).astype(bf16)
    got = near(sent)
    kept = [dot_tn(ctx_parts[j], after(grad_attn_low, sent)) for j in (0, 2)]
    small = sum(g[block:].astype(f32) for g in grad_ctx)
    small = (small[: SMALL // 2] + small[SMALL // 2 :]).reshape(4, 4, head_width)
    small = small.transpose(1, 0, 2).reshape(4, -1).astype(bf16)
    got, *kept = all_after([got, *kept])
    sent = (kept[1] + got[head_width:].astype(f32)).astype(bf16)
    kept = kept[0] + got[:head_width].astype(f32)
    got = far(sent)

    dq, dk, dv = attend_back(qb, ka, va, all_after(grad_ctx, small, sent, kept), ctx, cosine, sine)
    grad_out = (kept + after(got, dq).astype(f32)).astype(bf16)
    joint = [dot_tn(g, x_full).astype(bf16) for g in (dq, dk, dv)]
    joint = jnp.concatenate([*joint, grad_out, small], axis=0)
    joint = jnp.pad(joint, ((0, -len(joint) % (8 * dp)), (0, 0)))
    sums = [Sum(split_rows(joint, "dp", groups[0]), groups)]
    parts = all_after([dq, dk, dv], *[s.sent for s in sums])
    weights = [query_weight, key_weight, value_weight]

    def token_part(j):
        return sum(dot_nt(g[j * block : (j + 1) * block], w) for g, w in zip(parts, weights))

    sent = jnp.concatenate([token_part(j).astype(bf16) for j in (1, 3)], axis=0)
    got = near(sent)
    parts = all_after(parts, sent)
    mine, far_sent = token_part(0), token_part(2)
    got, mine, far_sent, feed_part = take_round(sums, got, mine, far_sent, feed_part)
    feed_part = after(feed_part, *[s.sent for s in sums])
    grad_feed = lax.all_gather(feed_part, "dp", axis=0, tiled=True)
    far_sent = (far_sent + got[block:].astype(f32)).astype(bf16)
    got_rows = far(far_sent)
    mine = grad_first + mine + got[:block].astype(f32)
    (got_rows,) = take_round(sums, got_rows)
    grad_tokens = mine + got_rows.astype(f32)
    while any(s.result is None for s in sums):
        take_round([s for s in sums if s.result is None])
    joint = sums[0].result.astype(f32)
    grad_gate, grad_up, grad_down = jnp.split(grad_feed.astype(f32), 3, axis=0)
    grad_joint = [joint[n * head_width : (n + 1) * head_width] for n in range(4)]
    grad_out = grad_joint.pop()
    small = joint[4 * head_width : 4 * head_width + 4]
    grad_joint = [g.T for g in grad_joint]
    return (
        encoded[None],
        grad_tokens[None],
        *grad_joint,
        grad_out,
        small[0],
        small[1],
        grad_gate,
        grad_up,
        grad_down,
        small[2],
        small[3],
    )


def solution(mesh):
    rows, cols, lead = P("dp", "tensor", None), P(None, "tensor"), P("tensor", None)
    return jax.shard_map(
        local,
        mesh=mesh,
        in_specs=(
            rows, P("dp", None), cols, cols, cols, lead, P(), P(), cols, cols, lead, P(), P(), rows,
        ),
        out_specs=(
            rows, rows, cols, cols, cols, lead, P(), P(), cols, cols, lead, P(), P(),
        ),
        check_vma=False,
    )
```

```python
import functools
import math

import jax
import jax.numpy as jnp
from jax import lax
from jax.experimental import pallas as pl
from jax.experimental.pallas import tpu as pltpu
from jax.sharding import PartitionSpec as P

HEAD_DIM = 64
EPSILON = 1e-05
ROPE_BASE = 1000.0
APART = -(2.0**30)
WIDE = 128
SEGMENTS = 7
SEG_AT = HEAD_DIM
ROW_AT = HEAD_DIM + 8
VMEM = 60 * 2**20
VMEM_LESS = 44 * 2**20
SMALL_COST = pl.CostEstimate(flops=2**20, bytes_accessed=2**16, transcendentals=0)
bf16 = jnp.bfloat16
f32 = jnp.float32
NT = (((1,), (1,)), ((), ()))
TN = (((0,), (0,)), ((), ()))


def dot(a, b):
    return jnp.dot(a, b, preferred_element_type=f32)


def dot_nt(a, b):
    return lax.dot_general(a, b, NT, preferred_element_type=f32)


def dot_tn(a, b):
    return lax.dot_general(a, b, TN, preferred_element_type=f32)


def swap(value, axis, bit):
    size = lax.axis_size(axis)
    return lax.ppermute(value, axis, [(i, i ^ bit) for i in range(size)])


def after(value, *others):
    return lax.optimization_barrier((value, *others))[0]


def all_after(values, *others):
    return list(lax.optimization_barrier((tuple(values), others))[0])


def scatter_sum(blocks, axis):
    held = dict(enumerate(blocks))
    rows = blocks[0].shape[0]
    step = 1
    while step < len(blocks):
        sent = [k for k in held if k & step]
        got = [held.pop(k).astype(bf16) for k in sent]
        got = swap(got[0] if len(got) == 1 else jnp.concatenate(got, axis=0), axis, step)
        for n, k in enumerate(sent):
            held[k ^ step] = held[k ^ step] + got[n * rows : (n + 1) * rows].astype(f32)
        step *= 2
    return held[0]


def peers(axis, bits):
    me = lax.axis_index(axis)
    mine = sum(((me >> bit) & 1) << n for n, bit in enumerate(bits))
    far = [sum(((j >> n) & 1) << bit for n, bit in enumerate(bits)) for j in range(1 << len(bits))]
    return mine, far


def split_rows(value, axis, bits):
    mine, far = peers(axis, bits)
    rows = value.shape[0] // len(far)
    return [lax.dynamic_slice_in_dim(value, (mine ^ j) * rows, rows, 0) for j in range(len(far))]


def join_rows(parts, axis, bits):
    mine, _ = peers(axis, bits)

    def pick(p):
        value = parts[-1]
        for j in reversed(range(len(parts) - 1)):
            value = jnp.where(mine == p ^ j, parts[j], value)
        return value

    return jnp.concatenate([pick(p) for p in range(len(parts))], axis=0)


def sum_steps(parts, axis, groups):
    for n, bits in enumerate(groups):
        if n:
            parts = split_rows(value, axis, bits)
        _, far = peers(axis, bits)
        got = yield parts[1:], [swap(part, axis, step) for part, step in zip(parts[1:], far[1:])]
        value = sum((g.astype(f32) for g in got), parts[0].astype(f32)).astype(bf16)
    for bits in reversed(groups):
        _, far = peers(axis, bits)
        got = yield [value], [swap(value, axis, step) for step in far[1:]]
        value = join_rows([value, *got], axis, bits)
    return value


class Sum:
    def __init__(self, parts, groups):
        self.steps = sum_steps(parts, "dp", groups)
        self.result = None
        self.sent, self.got = next(self.steps)

    def take(self, got):
        if self.result is None:
            try:
                self.sent, self.got = self.steps.send(got)
            except StopIteration as end:
                self.result, self.sent, self.got = end.value, [], []


def take_round(sums, *others):
    got, others = lax.optimization_barrier(([s.got for s in sums], others))
    for s, g in zip(sums, got):
        s.take(g)
    return list(others)


def swap_halves(value, lane):
    half = HEAD_DIM // 2
    return jnp.where(
        lane < half, pltpu.roll(value, WIDE - half, 1), pltpu.roll(value, half, 1)
    )


def own_block(values, rows, number):
    block = values[:, -rows:]
    for n in range(values.shape[1] // rows - 1):
        block = jnp.where(number == n, values[:, n * rows : (n + 1) * rows], block)
    return jnp.broadcast_to(block.astype(f32), (WIDE, rows)).T


def table_kernel(me_ref, seg_ref, rate_ref, cos_ref, sin_ref):
    segs = seg_ref[...]
    order = jnp.where(segs < 0, SEGMENTS - 1, segs)
    first_place = jnp.zeros_like(order)
    for s in range(1, SEGMENTS):
        before = jnp.sum((order < s).astype(jnp.int32), axis=1, keepdims=True)
        first_place = jnp.where(order == s, before, first_place)
    places = lax.broadcasted_iota(jnp.int32, segs.shape, 1) - first_place
    angles = own_block(places, cos_ref.shape[0], me_ref[0] ^ pl.program_id(0)) * rate_ref[...]
    lane = lax.broadcasted_iota(jnp.int32, angles.shape, 1)
    sine = jnp.sin(angles)
    cos_ref[...] = jnp.cos(angles)
    sin_ref[...] = jnp.where(lane < HEAD_DIM // 2, -sine, sine)


def rotary_tables(segments, rates, me, block):
    length = segments.shape[1]
    whole = lambda a: pl.BlockSpec(a.shape, lambda i: (0, 0))
    out = jax.ShapeDtypeStruct((length, WIDE), f32)
    return pl.pallas_call(
        table_kernel,
        grid=(length // block,),
        in_specs=[pl.BlockSpec(memory_space=pltpu.SMEM), whole(segments), whole(rates)],
        out_specs=[pl.BlockSpec((block, WIDE), lambda i: (i, 0))] * 2,
        out_shape=[out, out],
        compiler_params=pltpu.CompilerParams(vmem_limit_bytes=VMEM),
        cost_estimate=SMALL_COST,
        name="tables",
    )(me, segments, rates)


def project_kernel(heads, start, count, me_ref, *refs):
    pieces, refs = refs[:count], refs[count:]
    weights, (seg_ref, cos_ref, sin_ref) = refs[:3], refs[3:6]
    x_ref, qa_ref, ka_ref, va_ref = refs[-4:]
    rows = x_ref.shape[0]
    step = pl.program_id(0)
    for n, piece in enumerate(pieces):

        @pl.when(step == n)
        def _(piece=piece):
            x_ref[...] = piece[...]

    x = x_ref[...]
    query, key, value = (dot_nt(x, w[...]) for w in weights)
    seg = own_block(seg_ref[...], rows, me_ref[0] ^ (start + step)).astype(jnp.int32)
    lane = lax.broadcasted_iota(jnp.int32, (rows, WIDE), 1)
    cosine, sine = cos_ref[...], sin_ref[...]
    first = lane < HEAD_DIM
    same = lane == seg + (SEG_AT + 1)
    qf = jnp.where(same, APART, 0.0)
    kf = jnp.where((lane < ROW_AT + 3) & ~same, 1.0, 0.0)
    ones = jnp.where(lane < HEAD_DIM + 3, 1.0, 0.0)

    def part(values, h):
        at = h * HEAD_DIM
        if h % 2:
            return pltpu.roll(values[:, at - HEAD_DIM : at + HEAD_DIM], HEAD_DIM, 1)
        if h + 1 < heads:
            return values[:, at : at + WIDE]
        here = values[:, at : at + HEAD_DIM]
        return jnp.concatenate([here, jnp.zeros_like(here)], axis=1)

    for h in range(heads):
        q, k = part(query, h), part(key, h)
        q = q * cosine + swap_halves(q, lane) * sine
        k = k * cosine + swap_halves(k, lane) * sine
        qa_ref[h] = jnp.where(first, q * (1.0 / math.sqrt(HEAD_DIM)), qf).astype(bf16)
        ka_ref[h] = jnp.where(first, k, kf).astype(bf16)
        va_ref[h] = jnp.where(first, part(value, h), ones).astype(bf16)


def project(pieces, start, weights, segments, cosine, sine, me, heads, done=()):
    block, width = pieces[0].shape
    length = segments.shape[1]
    rows = lambda n: pl.BlockSpec((block, n), lambda i: (start + i, 0))
    whole = lambda a: pl.BlockSpec(a.shape, lambda i: (0, 0))
    out = pl.BlockSpec((heads, block, WIDE), lambda i: (0, start + i, 0))
    given = 1 + len(pieces) + 6
    return pl.pallas_call(
        functools.partial(project_kernel, heads, start, len(pieces)),
        grid=(len(pieces),),
        in_specs=[pl.BlockSpec(memory_space=pltpu.SMEM)]
        + [whole(p) for p in pieces]
        + [whole(w) for w in weights]
        + [whole(segments), rows(WIDE), rows(WIDE)]
        + [pl.BlockSpec(memory_space=pl.ANY)] * len(done),
        out_specs=[rows(width)] + [out] * 3,
        out_shape=[jax.ShapeDtypeStruct((length, width), bf16)]
        + [jax.ShapeDtypeStruct((heads, length, WIDE), bf16)] * 3,
        input_output_aliases={given + n: n for n in range(len(done))},
        compiler_params=pltpu.CompilerParams(vmem_limit_bytes=VMEM),
        cost_estimate=SMALL_COST,
        name="project",
    )(me, *pieces, *weights, segments, cosine, sine, *done)


def split3(value):
    high = value.astype(bf16).astype(f32)
    rest = value - high
    middle = rest.astype(bf16).astype(f32)
    return high, middle, rest - middle


def put_row(wide, at, value):
    lane = lax.broadcasted_iota(jnp.int32, wide.shape, 1)
    for n, part in enumerate(split3(value)):
        wide = jnp.where(lane == at + n, -part, wide)
    return wide


def attend_kernel(heads, qa_ref, ka_ref, va_ref, *refs):
    ctx_ref, qb_ref = refs[-2:]
    parts = []
    for h in range(heads):
        qa = qa_ref[h]
        scores = dot_nt(qa, ka_ref[h])
        peak = jnp.max(scores, axis=1, keepdims=True)
        weights = jnp.exp(scores - peak).astype(bf16)
        summed = dot(weights, va_ref[h])
        total = summed[:, HEAD_DIM : HEAD_DIM + 1]
        parts.append(summed[:, :HEAD_DIM] / total)
        qb_ref[h] = put_row(qa.astype(f32), ROW_AT, peak + jnp.log(total)).astype(bf16)
    ctx_ref[...] = jnp.concatenate(parts, axis=1).astype(bf16)


def attend(qa, ka, va, start, count, done=(), block=256):
    heads, length, _ = qa.shape
    first = start // block
    whole = pl.BlockSpec((heads, length, WIDE), lambda i: (0, 0, 0))
    part = pl.BlockSpec((heads, block, WIDE), lambda i: (0, first + i, 0))
    return pl.pallas_call(
        functools.partial(attend_kernel, heads),
        grid=(count // block,),
        in_specs=[part, whole, whole] + [pl.BlockSpec(memory_space=pl.ANY)] * len(done),
        out_specs=[pl.BlockSpec((block, heads * HEAD_DIM), lambda i: (first + i, 0)), part],
        out_shape=[
            jax.ShapeDtypeStruct((length, heads * HEAD_DIM), bf16),
            jax.ShapeDtypeStruct((heads, length, WIDE), bf16),
        ],
        input_output_aliases={3 + n: n for n in range(len(done))},
        compiler_params=pltpu.CompilerParams(vmem_limit_bytes=VMEM_LESS),
        cost_estimate=SMALL_COST,
        name="attend",
    )(qa, ka, va, *done)


def attend_back_kernel(heads, qb_ref, ka_ref, va_ref, *refs):
    gos, refs = refs[:4], refs[4:]
    ctx_ref, cos_ref, sin_ref, dq_ref, dk_ref, dv_ref, doa, dqt = refs
    j, h = pl.program_id(0), pl.program_id(1)
    length = qb_ref.shape[1]
    block = length // 4
    at = [pl.ds(i * block, block) for i in range(4)]

    for head in range(heads):
        cols = pl.ds(head * HEAD_DIM, HEAD_DIM)

        @pl.when((j == 0) & (h == head))
        def _(cols=cols):
            for i in range(4):
                go = gos[i][:block, cols].astype(f32)
                delta = jnp.sum(go * ctx_ref[at[i], cols].astype(f32), axis=1, keepdims=True)
                wide = jnp.concatenate([go, jnp.zeros_like(go)], axis=1)
                doa[h, at[i], :] = put_row(wide, HEAD_DIM, delta).astype(bf16)

    @pl.when(j == 0)
    def _():
        dqt[h] = jnp.zeros(dqt.shape[1:], f32)

    ka, va = ka_ref[h], va_ref[h]
    kt = ka.astype(f32).T[:HEAD_DIM].astype(bf16)
    dk = dv = None
    for i in range(4):
        qb, do = qb_ref[h, at[i], :], doa[h, at[i], :]
        weights = jnp.exp(dot_nt(ka, qb))
        grads = (weights * dot_nt(va, do)).astype(bf16)
        v_part = dot(weights.astype(bf16), do)
        k_part = dot(grads, qb)
        dk = k_part if i == 0 else dk + k_part
        dv = v_part if i == 0 else dv + v_part
        dqt[h, :, at[i]] += dot(kt, grads)
    lane = lax.broadcasted_iota(jnp.int32, dk.shape, 1)
    rows = pl.ds(pl.multiple_of(j * ka.shape[0], ka.shape[0]), ka.shape[0])
    dk = dk * cos_ref[rows, :] - swap_halves(dk, lane) * sin_ref[rows, :]
    for head in range(heads):
        cols = pl.ds(head * HEAD_DIM, HEAD_DIM)

        @pl.when(h == head)
        def _(cols=cols):
            dk_ref[:, cols] = dk[:, :HEAD_DIM].astype(bf16)
            dv_ref[:, cols] = dv[:, :HEAD_DIM].astype(bf16)

        @pl.when((h == head) & (j == pl.num_programs(0) - 1))
        def _(cols=cols):
            for i in range(4):
                part = dqt[h, :, at[i]]
                dq = jnp.concatenate([part, jnp.zeros_like(part)], axis=0).T
                lanes = lax.broadcasted_iota(jnp.int32, dq.shape, 1)
                dq = dq * cos_ref[at[i], :] - swap_halves(dq, lanes) * sin_ref[at[i], :]
                dq_ref[at[i], cols] = (dq[:, :HEAD_DIM] * (1.0 / math.sqrt(HEAD_DIM))).astype(bf16)


def attend_back(qb, ka, va, gos, ctx, cosine, sine, block_k=512):
    heads, length, _ = qb.shape
    part = pl.BlockSpec((heads, block_k, WIDE), lambda j, h: (0, j, 0))
    full = lambda a: pl.BlockSpec(a.shape, lambda j, h, r=len(a.shape): (0,) * r)
    grad = jax.ShapeDtypeStruct((length, heads * HEAD_DIM), bf16)
    rows = pl.BlockSpec((block_k, heads * HEAD_DIM), lambda j, h: (j, 0))
    return pl.pallas_call(
        functools.partial(attend_back_kernel, heads),
        grid=(length // block_k, heads),
        in_specs=[full(qb), part, part] + [full(a) for a in (*gos, ctx, cosine, sine)],
        out_specs=[full(grad), rows, rows],
        out_shape=[grad] * 3,
        scratch_shapes=[pltpu.VMEM((heads, length, WIDE), bf16), pltpu.VMEM((heads, HEAD_DIM, length), f32)],
        compiler_params=pltpu.CompilerParams(vmem_limit_bytes=VMEM),
        cost_estimate=SMALL_COST,
        name="attend_back",
    )(qb, ka, va, *gos, ctx, cosine, sine)


ANY = pl.BlockSpec(memory_space=pl.ANY)
IN_VMEM = pl.BlockSpec(memory_space=pltpu.VMEM)


def start(source, target, sem):
    copy = pltpu.make_async_copy(source, target, sem)
    copy.start()
    return copy


def norm_parts(row_values):
    centred = row_values - jnp.mean(row_values, axis=-1, keepdims=True)
    inverse = lax.rsqrt(jnp.mean(centred * centred, axis=-1, keepdims=True) + EPSILON)
    return (centred * inverse, inverse)


def norm_back(grad_norm, normalized, inverse):
    return inverse * (
        grad_norm
        - jnp.mean(grad_norm, axis=-1, keepdims=True)
        - normalized * jnp.mean(grad_norm * normalized, axis=-1, keepdims=True)
    )


def sigmoid(value):
    return 0.5 * jnp.tanh(0.5 * value) + 0.5


def feed(low, gate, up):
    gate_pre, up_pre = dot(low, gate), dot(low, up)
    return gate_pre, up_pre


def hidden_of(gate_pre, up_pre):
    return (gate_pre * sigmoid(gate_pre) * up_pre).astype(bf16)


def feed_back(grad_hidden, gate_pre, up_pre):
    part = sigmoid(gate_pre)
    active = gate_pre * part
    grad_gate = grad_hidden * up_pre * (part + active * (1.0 - part))
    return grad_gate.astype(bf16), (grad_hidden * active).astype(bf16)


def shard_copies(n, plan, refs, buffers, sem):
    copies = []
    for buffer, pieces in zip(buffers, plan[n]):
        row, width = 0, buffer.shape[2]
        for at, first in pieces:
            rows = refs[at].shape[0]
            source = refs[at].at[:, pl.ds(first * width, width)]
            copies.append(start(source, buffer.at[n, pl.ds(row, rows), :], sem.at[n, len(copies)]))
            row += rows
    return copies


def shard_plan(shards):
    args, plan = [], []
    for shard in shards:
        plan.append([])
        for pieces in shard:
            plan[-1].append([(len(args) + n, first) for n, (_, first) in enumerate(pieces)])
            args += [a for a, _ in pieces]
    return args, plan


HALVES = 2


def halves(length):
    return [pl.ds(n * (length // HALVES), length // HALVES) for n in range(HALVES)]


def arrays_of(plan):
    return sum(len(pieces) for shard in plan for pieces in shard)


def feed_shards(plan, shards, weights, coming, low, kept, targets, total, sems):
    buffers, (gates, ups), (sem, out_sem) = weights, kept, sems
    gate, up, down = weights
    hidden, going = down.shape[1], []
    for n in range(len(plan)):
        here = coming
        if n + 1 < len(plan):
            coming = shard_copies(n + 1, plan, shards, buffers, sem)
        for copy in here:
            copy.wait()
        for at in halves(low.shape[0]):
            gate_pre, up_pre = feed(low[at, :], gate[n], up[n])
            gates[n, at, :] = gate_pre.astype(bf16)
            ups[n, at, :] = up_pre.astype(bf16)
            part = dot(hidden_of(gate_pre, up_pre), down[n])
            total[at, :] = part if n == 0 else total[at, :] + part
        cols = pl.ds(n * hidden, hidden)
        for k, (buffer, target) in enumerate(zip(kept, targets)):
            going.append(start(buffer.at[n], target.at[:, cols], out_sem.at[n, k]))
    return going


def first_kernel(plan, gain_ref, shift_ref, own_ref, *refs):
    parts, outs, refs = refs[:4], refs[4:8], refs[8:]
    shards, refs = refs[: arrays_of(plan)], refs[arrays_of(plan) :]
    norm_ref, inverse_ref, low_ref, gates_ref, ups_ref, total_ref = refs[:6]
    own, part_in, out_in, norm1, inverse1, low, total, *weights = refs[6:16]
    kept, sems, (in_sem, res_sem) = refs[16:18], refs[18:20], refs[20:]
    coming = [start(own_ref, own, in_sem.at[8])]
    for n in range(4):
        coming.append(start(parts[n], part_in.at[n], in_sem.at[n]))
        coming.append(start(outs[n], out_in.at[n], in_sem.at[4 + n]))
    first = shard_copies(0, plan, shards, weights, sems[0])
    for copy in coming:
        copy.wait()
    summed = own[...].astype(f32)
    for n in range(4):
        summed = summed + dot(part_in[n], out_in[n])
    norm, inverse = norm_parts(summed)
    norm1[...] = norm
    inverse1[...] = jnp.broadcast_to(inverse, inverse1.shape)
    low[...] = (norm * gain_ref[...] + shift_ref[...]).astype(bf16)
    going = [
        start(source, target, res_sem.at[n])
        for n, (source, target) in enumerate([(low, low_ref), (norm1, norm_ref), (inverse1, inverse_ref)])
    ]
    going += feed_shards(plan, shards, weights, first, low, kept, (gates_ref, ups_ref), total, sems)
    going.append(start(total, total_ref, res_sem.at[3]))
    for copy in going:
        copy.wait()


def last_kernel(plan, low_ref, gain_ref, shift_ref, gain2_ref, shift2_ref, before_ref, norm_ref, cot_ref, *refs):
    shards, refs = refs[: arrays_of(plan)], refs[arrays_of(plan) :]
    gates_ref, ups_ref, encoded_ref, second_ref, low2_ref, small_ref = refs[:6]
    before, norm1, cot_in, total, *weights = refs[6:13]
    kept, sems, in_sem = refs[13:15], refs[15:17], refs[17]
    first = shard_copies(0, plan, shards, weights, sems[0])
    late = [
        start(source, target, in_sem.at[n])
        for n, (source, target) in enumerate([(before_ref, before), (norm_ref, norm1), (cot_ref, cot_in)])
    ]
    going = feed_shards(plan, shards, weights, first, low_ref, kept, (gates_ref, ups_ref), total, sems)
    for copy in late:
        copy.wait()
    normed = norm1[...] * gain_ref[...] + shift_ref[...]
    norm, inverse = norm_parts(normed + (before[...] + total[...]))
    cot = cot_in[...].astype(f32)
    encoded_ref[...] = (norm * gain2_ref[...] + shift2_ref[...]).astype(bf16)
    grad = norm_back(cot * gain2_ref[...], norm, inverse)
    second_ref[...] = grad
    low2_ref[...] = grad.astype(bf16)
    small_ref[...] = jnp.concatenate(
        [jnp.sum(cot * norm, axis=0, keepdims=True), jnp.sum(cot, axis=0, keepdims=True)], axis=0
    )
    for copy in going:
        copy.wait()


def shard_scratch(count, length, width, hidden):
    return [
        pltpu.VMEM((count, width, hidden), bf16),
        pltpu.VMEM((count, width, hidden), bf16),
        pltpu.VMEM((count, hidden, width), bf16),
        pltpu.VMEM((count, length, hidden), bf16),
        pltpu.VMEM((count, length, hidden), bf16),
        pltpu.SemaphoreType.DMA((count, 4)),
        pltpu.SemaphoreType.DMA((count, 2)),
    ]


def forward_first(own, parts, outs, shards, gain, shift):
    length, width = own.shape
    count, hidden = len(shards), sum(a.shape[0] for a, _ in shards[0][2])
    args, plan = shard_plan(shards)
    kept = jax.ShapeDtypeStruct((length, hidden * count), bf16)
    norm = jax.ShapeDtypeStruct((length, width), f32)
    inverse = jax.ShapeDtypeStruct((length, WIDE), f32)
    low = jax.ShapeDtypeStruct((length, width), bf16)
    shapes = [norm, inverse, low, kept, kept, norm]
    vmem = lambda a: pltpu.VMEM(a.shape, a.dtype)
    stack = lambda arrays: pltpu.VMEM((len(arrays), *arrays[0].shape), bf16)
    return pl.pallas_call(
        functools.partial(first_kernel, plan),
        in_specs=[IN_VMEM] * 2 + [ANY] * (9 + len(args)),
        out_specs=[ANY] * len(shapes),
        out_shape=shapes,
        scratch_shapes=[vmem(own), stack(parts), stack(outs), vmem(norm), vmem(inverse), vmem(low), vmem(norm)]
        + shard_scratch(count, length, width, hidden)
        + [pltpu.SemaphoreType.DMA((9,)), pltpu.SemaphoreType.DMA((4,))],
        compiler_params=pltpu.CompilerParams(vmem_limit_bytes=VMEM),
        cost_estimate=SMALL_COST,
        name="feed_first",
    )(gain, shift, own, *parts, *outs, *args)


def forward_last(low, shards, before, norm, cot, vectors):
    length, width = low.shape
    count, hidden = len(shards), sum(a.shape[0] for a, _ in shards[0][2])
    args, plan = shard_plan(shards)
    kept = jax.ShapeDtypeStruct((length, hidden * count), bf16)
    wide = jax.ShapeDtypeStruct((length, width), f32)
    rounded = jax.ShapeDtypeStruct((length, width), bf16)
    small = jax.ShapeDtypeStruct((2, width), f32)
    vmem = lambda a: pltpu.VMEM(a.shape, a.dtype)
    return pl.pallas_call(
        functools.partial(last_kernel, plan),
        in_specs=[IN_VMEM] * 5 + [ANY] * (3 + len(args)),
        out_specs=[ANY] * 2 + [IN_VMEM] * 4,
        out_shape=[kept, kept, rounded, wide, rounded, small],
        scratch_shapes=[vmem(a) for a in (wide, wide, cot, wide)]
        + shard_scratch(count, length, width, hidden)
        + [pltpu.SemaphoreType.DMA((3,))],
        compiler_params=pltpu.CompilerParams(vmem_limit_bytes=VMEM),
        cost_estimate=SMALL_COST,
        name="feed_last",
    )(low, *vectors, before, norm, cot, *args)


def backward_kernel(plan, where, low2_ref, *refs):
    count = len(plan)
    shards, refs = refs[: arrays_of(plan)], refs[arrays_of(plan) :]
    pairs = where[-1][0] + 1
    saved, refs = refs[: 2 * pairs], refs[2 * pairs :]
    late_refs, refs = refs[:7], refs[7:]
    gain_ref, small_in_ref, first_ref, low_ref, *ctx_refs = refs[:8]
    gate, up, down, gates, ups, total, second, norm1, inverse, outs, sem, saved_sem, late_sem = refs[8:]
    buffers = (gate, up, down)
    hidden = down.shape[1]

    def fetch(n):
        part, cols = where[n][0], pl.ds(where[n][1] * hidden, hidden)
        return shard_copies(n, plan, shards, buffers, sem) + [
            start(ref.at[:, cols], buffer.at[n], saved_sem.at[n, k])
            for k, (ref, buffer) in enumerate(zip(saved[2 * part : 2 * part + 2], (gates, ups)))
        ]

    coming = [fetch(0)]
    late = []
    for n in range(count):
        if n + 1 < count:
            coming.append(fetch(n + 1))
        else:
            targets = [second, norm1, inverse] + [outs.at[k] for k in range(4)]
            late = [start(ref, target, late_sem.at[k]) for k, (ref, target) in enumerate(zip(late_refs, targets))]
        for copy in coming[n]:
            copy.wait()
        for at in halves(low2_ref.shape[0]):
            grad_hidden = dot_nt(low2_ref[at, :], down[n])
            grad_gate, grad_up = feed_back(grad_hidden, gates[n, at, :].astype(f32), ups[n, at, :].astype(f32))
            part = dot_nt(grad_gate, gate[n]) + dot_nt(grad_up, up[n])
            total[at, :] = part if n == 0 else total[at, :] + part
    for copy in late:
        copy.wait()
    normed_grad, norm = second[...] + total[...], norm1[...]
    first = norm_back(normed_grad * gain_ref[...], norm, inverse[:, :1])
    first_ref[...] = first
    low = first.astype(bf16)
    low_ref[...] = low
    small = jnp.concatenate(
        [
            jnp.sum(normed_grad * norm, axis=0, keepdims=True),
            jnp.sum(normed_grad, axis=0, keepdims=True),
            small_in_ref[...],
        ],
        axis=0,
    )
    width = outs.shape[1]
    small = jnp.concatenate([small[:, k * width : (k + 1) * width] for k in range(4)], axis=0)
    high = small.astype(bf16)
    small = jnp.concatenate([high, (small - high.astype(f32)).astype(bf16)], axis=0)
    length = low.shape[0]
    for k in range(4):
        ctx_refs[k][:length, :] = dot_nt(low, outs[k]).astype(bf16)
        ctx_refs[k][length:, :] = small


SMALL = 32


def backward(low2, shards, saved, second, norm, inverse, outs, gain, small):
    length, width = low2.shape
    count, hidden = len(shards), sum(a.shape[0] for a, _ in shards[0][2])
    args, plan = shard_plan(shards)
    where = [(n, k) for n, (gates, _) in enumerate(saved) for k in range(gates.shape[1] // hidden)]
    saved = [a for pair in saved for a in pair]
    late = [second, norm, inverse, *outs]
    wide = pltpu.VMEM((length, width), f32)
    return pl.pallas_call(
        functools.partial(backward_kernel, plan, where),
        in_specs=[IN_VMEM] + [ANY] * (len(args) + len(saved) + len(late)) + [IN_VMEM] * 2,
        out_specs=[IN_VMEM] * 6,
        out_shape=[
            jax.ShapeDtypeStruct((length, width), f32),
            jax.ShapeDtypeStruct((length, width), bf16),
        ]
        + [jax.ShapeDtypeStruct((length + SMALL, outs[0].shape[0]), bf16)] * 4,
        scratch_shapes=[
            pltpu.VMEM((count, width, hidden), bf16),
            pltpu.VMEM((count, width, hidden), bf16),
            pltpu.VMEM((count, hidden, width), bf16),
            pltpu.VMEM((count, length, hidden), bf16),
            pltpu.VMEM((count, length, hidden), bf16),
            wide,
            wide,
            wide,
            pltpu.VMEM(inverse.shape, f32),
            pltpu.VMEM((4, *outs[0].shape), bf16),
            pltpu.SemaphoreType.DMA((count, 4)),
            pltpu.SemaphoreType.DMA((count, 2)),
            pltpu.SemaphoreType.DMA((len(late),)),
        ],
        compiler_params=pltpu.CompilerParams(vmem_limit_bytes=VMEM),
        cost_estimate=SMALL_COST,
        name="feed_back",
    )(low2, *args, *saved, *late, gain, small)


def weights_kernel(*refs):
    rows, grads, weights, refs = refs[:4], refs[4:8], refs[8:11], refs[11:]
    target, refs = refs[0], refs[1:]
    gate, up, down, low, low_t, low2, dgate, dup, hidden_t, result, sem, out_sem = refs
    block = rows[0].shape[0]
    at = [pl.ds(n * block, block) for n in range(4)]

    def fetch(n):
        return [
            start(rows[n], low.at[at[n], :], sem.at[n, 0]),
            start(grads[n], low2.at[at[n], :], sem.at[n, 1]),
        ]

    coming = [fetch(0)]
    own = [start(w, buffer, sem.at[4 + k, 0]) for k, (w, buffer) in enumerate(zip(weights, (gate, up, down)))]
    coming.append(fetch(1))
    for copy in own:
        copy.wait()
    for n in range(4):
        if n + 2 < 4:
            coming.append(fetch(n + 2))
        for copy in coming[n]:
            copy.wait()
        here = low[at[n], :]
        low_t[:, at[n]] = here.T
        gate_pre, up_pre = feed(here, gate[...], up[...])
        grad_hidden = dot_nt(low2[at[n], :], down[...])
        dgate[at[n], :], dup[at[n], :] = feed_back(grad_hidden, gate_pre, up_pre)
        hidden_t[:, at[n]] = hidden_of(gate_pre, up_pre).T
    going = []
    for k, (left, right) in enumerate([(low_t, dgate), (low_t, dup), (hidden_t, low2)]):
        result[k] = dot(left[...], right[...]).astype(bf16)
        rows_at = pl.ds(k * result.shape[1], result.shape[1])
        going.append(start(result.at[k], target.at[rows_at, :], out_sem.at[k]))
    for copy in going:
        copy.wait()


def weight_grads(rows, grads, gate, up, down):
    block, width = rows[0].shape
    length, hidden = 4 * block, gate.shape[1]
    return pl.pallas_call(
        weights_kernel,
        in_specs=[ANY] * 11,
        out_specs=ANY,
        out_shape=jax.ShapeDtypeStruct((3 * width, hidden), bf16),
        scratch_shapes=[
            pltpu.VMEM((width, hidden), bf16),
            pltpu.VMEM((width, hidden), bf16),
            pltpu.VMEM((hidden, width), bf16),
            pltpu.VMEM((length, width), bf16),
            pltpu.VMEM((width, length), bf16),
            pltpu.VMEM((length, width), bf16),
            pltpu.VMEM((length, hidden), bf16),
            pltpu.VMEM((length, hidden), bf16),
            pltpu.VMEM((hidden, length), bf16),
            pltpu.VMEM((3, width, hidden), bf16),
            pltpu.SemaphoreType.DMA((7, 2)),
            pltpu.SemaphoreType.DMA((3,)),
        ],
        compiler_params=pltpu.CompilerParams(vmem_limit_bytes=VMEM),
        cost_estimate=SMALL_COST,
        name="feed_weights",
    )(*rows, *grads, gate, up, down)


def local(
    tokens,
    segment_ids,
    query_weight,
    key_weight,
    value_weight,
    output_weight,
    attn_gain,
    attn_shift,
    gate_weight,
    up_weight,
    down_weight,
    mlp_gain,
    mlp_shift,
    cotangent,
):
    own = tokens[0]
    head_width = query_weight.shape[1]
    heads = head_width // HEAD_DIM
    group = lax.axis_size("tensor")
    block = own.shape[0]
    dp = lax.axis_size("dp")
    bits = list(range(int(math.log2(dp))))
    groups = [bits[:1]] + [bits[n : n + 2] for n in range(1, len(bits), 2)]

    near = lambda a: swap(a, "tensor", 1)
    far = lambda a: swap(a, "tensor", 2)

    share = gate_weight.shape[0] // dp
    at = lax.axis_index("dp") * share
    mine = jnp.concatenate(
        [lax.dynamic_slice_in_dim(w, at, share, 0) for w in (gate_weight, up_weight)], axis=1
    )
    far_own = far(own)
    near_own = near(own)
    angle_rate = ROPE_BASE ** (-(jnp.arange(HEAD_DIM // 2, dtype=f32) * 2.0 / HEAD_DIM))
    rates = jnp.concatenate([angle_rate, angle_rate, jnp.zeros(HEAD_DIM, f32)])[None, :]
    me = lax.axis_index("tensor").astype(jnp.int32)[None]
    cosine, sine = rotary_tables(segment_ids, rates, me, block)
    inputs = ([w.T for w in (query_weight, key_weight, value_weight)], segment_ids, cosine, sine, me, heads)
    third = down_weight.shape[0] // 3
    downs = [down_weight[:third], down_weight[third:]]
    near_half = project([after(own, mine, *downs), near_own], 0, *inputs)
    far_own = after(far_own, near_half[0])
    both_own = near(far_own)
    mine = after(mine, far_own)
    far_mine = far(mine)
    near_weights = [near(w) for w in all_after([gate_weight, up_weight, down_weight, output_weight], both_own)]
    x_full, qa, ka, va = project([far_own, after(both_own, mine)], 2, *inputs, done=near_half)
    far_mine, *near_weights = all_after([far_mine, *near_weights], qa)
    near_gate, near_up, near_down, near_out = near_weights
    far_mixed = lax.all_gather(far_mine, "dp", axis=0, tiled=True)
    out_sent, downs[0] = all_after([output_weight, downs[0]], far_mine)
    far_out, early_down = far(out_sent), far(downs[0])
    qa = after(qa, out_sent, downs[0], *near_weights)

    def send(value, j):
        return swap(value[j * block : (j + 1) * block], "tensor", j)

    half = attend(qa, ka, va, 2 * block, 2 * block)
    far_out, early_down = all_after([far_out, early_down], half[0])
    slices = [half[0][j * block : (j + 1) * block] for j in (2, 3)]
    ctx_far = [swap(c, "tensor", j) for c, j in zip(slices, (2, 3))]
    both_out = near(far_out)
    ctx, qb = attend(after(qa, far_out, early_down, *slices), ka, va, 0, 2 * block, done=half)
    both_out, *ctx_far = all_after([both_out, *ctx_far], ctx)
    near_ctx = send(ctx, 1)
    down_sent = after(downs[1], *ctx_far)
    far_down = [early_down, far(down_sent)]
    ctx_parts = [ctx[:block], near_ctx, *ctx_far]
    outs = [output_weight, near_out, far_out, both_out]
    row = lambda a: a[None, :]

    near_shards = [
        ([(gate_weight, 0)], [(up_weight, 0)], [(down_weight, 0)]),
        ([(near_gate, 0)], [(near_up, 0)], [(near_down, 0)]),
    ]
    first_norm, inverse, normed_low, *saved_a, half_way = forward_first(
        after(own, down_sent), ctx_parts, outs, near_shards, row(attn_gain), row(attn_shift)
    )
    near_rows = near(normed_low)
    far_mixed, *far_down = all_after([far_mixed, *far_down], half_way)
    both_mixed, both_down = near(far_mixed), [near(d) for d in far_down]
    rows_sent = after(normed_low, *far_down)
    far_rows = far(rows_sent)
    shards = near_shards + [
        ([(mixed, 0)], [(mixed, 1)], [(d, 0) for d in down])
        for mixed, down in ((far_mixed, far_down), (both_mixed, both_down))
    ]
    *saved_b, encoded, grad_second, grad_low, small = forward_last(
        after(normed_low, rows_sent),
        shards[2:],
        half_way,
        first_norm,
        cotangent[0],
        (row(attn_gain), row(attn_shift), row(mlp_gain), row(mlp_shift)),
    )
    near_rows, far_rows = all_after([near_rows, far_rows], grad_low)
    both_rows = near(far_rows)
    near_grads, far_grads = near(grad_low), far(grad_low)
    grad_first, grad_attn_low, own_ctx, *sent_ctx = backward(
        after(grad_low, far_rows),
        shards,
        (saved_a, saved_b),
        grad_second,
        first_norm,
        inverse,
        outs,
        row(attn_gain),
        small,
    )
    near_grads, far_grads, both_rows = all_after([near_grads, far_grads, both_rows], grad_first)
    both_grads = near(far_grads)
    got_ctx = [swap(g, "tensor", j + 1) for j, g in enumerate(sent_ctx)]
    grad_feed = weight_grads(
        [after(normed_low, *sent_ctx), near_rows, far_rows, both_rows],
        [grad_low, near_grads, far_grads, both_grads],
        gate_weight,
        up_weight,
        down_weight,
    )
    grad_ctx = all_after(got_ctx, grad_feed)
    feed_part = lax.psum_scatter(after(grad_feed, *grad_ctx), "dp", scatter_dimension=0, tiled=True)
    grad_ctx = [own_ctx, *grad_ctx]
    grad_attn_low = after(grad_attn_low, grad_feed)
    sent = jnp.concatenate([dot_tn(ctx_parts[j], grad_attn_low) for j in (1, 3)], axis=0).astype(bf16)
    got = near(sent)
    kept = [dot_tn(ctx_parts[j], after(grad_attn_low, sent)) for j in (0, 2)]
    small = sum(g[block:].astype(f32) for g in grad_ctx)
    small = (small[: SMALL // 2] + small[SMALL // 2 :]).reshape(4, 4, head_width)
    small = small.transpose(1, 0, 2).reshape(4, -1).astype(bf16)
    got, *kept = all_after([got, *kept])
    sent = (kept[1] + got[head_width:].astype(f32)).astype(bf16)
    kept = kept[0] + got[:head_width].astype(f32)
    got = far(sent)

    dq, dk, dv = attend_back(qb, ka, va, all_after(grad_ctx, small, sent, kept), ctx, cosine, sine)
    grad_out = (kept + after(got, dq).astype(f32)).astype(bf16)
    joint = [dot_tn(g, x_full).astype(bf16) for g in (dq, dk, dv)]
    joint = jnp.concatenate([*joint, grad_out, small], axis=0)
    joint = jnp.pad(joint, ((0, -len(joint) % (8 * dp)), (0, 0)))
    sums = [Sum(split_rows(joint, "dp", groups[0]), groups)]
    parts = all_after([dq, dk, dv], *[s.sent for s in sums])
    weights = [query_weight, key_weight, value_weight]

    def token_part(j):
        return sum(dot_nt(g[j * block : (j + 1) * block], w) for g, w in zip(parts, weights))

    sent = jnp.concatenate([token_part(j).astype(bf16) for j in (1, 3)], axis=0)
    got = near(sent)
    parts = all_after(parts, sent)
    mine, far_sent = token_part(0), token_part(2)
    got, mine, far_sent, feed_part = take_round(sums, got, mine, far_sent, feed_part)
    grad_feed = lax.all_gather(feed_part, "dp", axis=0, tiled=True)
    far_sent = (far_sent + got[block:].astype(f32)).astype(bf16)
    got_rows = far(far_sent)
    mine = grad_first + mine + got[:block].astype(f32)
    (got_rows,) = take_round(sums, got_rows)
    grad_tokens = mine + got_rows.astype(f32)
    while any(s.result is None for s in sums):
        take_round([s for s in sums if s.result is None])
    joint = sums[0].result.astype(f32)
    grad_gate, grad_up, grad_down = jnp.split(grad_feed.astype(f32), 3, axis=0)
    grad_joint = [joint[n * head_width : (n + 1) * head_width] for n in range(4)]
    grad_out = grad_joint.pop()
    small = joint[4 * head_width : 4 * head_width + 4]
    grad_joint = [g.T for g in grad_joint]
    return (
        encoded[None],
        grad_tokens[None],
        *grad_joint,
        grad_out,
        small[0],
        small[1],
        grad_gate,
        grad_up,
        grad_down,
        small[2],
        small[3],
    )


def solution(mesh):
    rows, cols, lead = P("dp", "tensor", None), P(None, "tensor"), P("tensor", None)
    return jax.shard_map(
        local,
        mesh=mesh,
        in_specs=(
            rows, P("dp", None), cols, cols, cols, lead, P(), P(), cols, cols, lead, P(), P(), rows,
        ),
        out_specs=(
            rows, rows, cols, cols, cols, lead, P(), P(), cols, cols, lead, P(), P(),
        ),
        check_vma=False,
    )
```

```python
import functools
import math

import jax
import jax.numpy as jnp
from jax import lax
from jax.experimental import pallas as pl
from jax.experimental.pallas import tpu as pltpu
from jax.sharding import PartitionSpec as P

HEAD_DIM = 64
EPSILON = 1e-05
ROPE_BASE = 1000.0
APART = -(2.0**30)
WIDE = 128
SEGMENTS = 7
SEG_AT = HEAD_DIM
ROW_AT = HEAD_DIM + 8
VMEM = 60 * 2**20
VMEM_LESS = 44 * 2**20
SMALL_COST = pl.CostEstimate(flops=2**20, bytes_accessed=2**16, transcendentals=0)
bf16 = jnp.bfloat16
f32 = jnp.float32
NT = (((1,), (1,)), ((), ()))
TN = (((0,), (0,)), ((), ()))


def dot(a, b):
    return jnp.dot(a, b, preferred_element_type=f32)


def dot_nt(a, b):
    return lax.dot_general(a, b, NT, preferred_element_type=f32)


def dot_tn(a, b):
    return lax.dot_general(a, b, TN, preferred_element_type=f32)


def swap(value, axis, bit):
    size = lax.axis_size(axis)
    return lax.ppermute(value, axis, [(i, i ^ bit) for i in range(size)])


def after(value, *others):
    return lax.optimization_barrier((value, *others))[0]


def all_after(values, *others):
    return list(lax.optimization_barrier((tuple(values), others))[0])


def scatter_sum(blocks, axis):
    held = dict(enumerate(blocks))
    rows = blocks[0].shape[0]
    step = 1
    while step < len(blocks):
        sent = [k for k in held if k & step]
        got = [held.pop(k).astype(bf16) for k in sent]
        got = swap(got[0] if len(got) == 1 else jnp.concatenate(got, axis=0), axis, step)
        for n, k in enumerate(sent):
            held[k ^ step] = held[k ^ step] + got[n * rows : (n + 1) * rows].astype(f32)
        step *= 2
    return held[0]


def peers(axis, bits):
    me = lax.axis_index(axis)
    mine = sum(((me >> bit) & 1) << n for n, bit in enumerate(bits))
    far = [sum(((j >> n) & 1) << bit for n, bit in enumerate(bits)) for j in range(1 << len(bits))]
    return mine, far


def split_rows(value, axis, bits):
    mine, far = peers(axis, bits)
    rows = value.shape[0] // len(far)
    return [lax.dynamic_slice_in_dim(value, (mine ^ j) * rows, rows, 0) for j in range(len(far))]


def join_rows(parts, axis, bits):
    mine, _ = peers(axis, bits)

    def pick(p):
        value = parts[-1]
        for j in reversed(range(len(parts) - 1)):
            value = jnp.where(mine == p ^ j, parts[j], value)
        return value

    return jnp.concatenate([pick(p) for p in range(len(parts))], axis=0)


def sum_steps(parts, axis, groups):
    for n, bits in enumerate(groups):
        if n:
            parts = split_rows(value, axis, bits)
        _, far = peers(axis, bits)
        got = yield parts[1:], [swap(part, axis, step) for part, step in zip(parts[1:], far[1:])]
        value = sum((g.astype(f32) for g in got), parts[0].astype(f32)).astype(bf16)
    for bits in reversed(groups):
        _, far = peers(axis, bits)
        got = yield [value], [swap(value, axis, step) for step in far[1:]]
        value = join_rows([value, *got], axis, bits)
    return value


class Sum:
    def __init__(self, parts, groups):
        self.steps = sum_steps(parts, "dp", groups)
        self.result = None
        self.sent, self.got = next(self.steps)

    def take(self, got):
        if self.result is None:
            try:
                self.sent, self.got = self.steps.send(got)
            except StopIteration as end:
                self.result, self.sent, self.got = end.value, [], []


def take_round(sums, *others):
    got, others = lax.optimization_barrier(([s.got for s in sums], others))
    for s, g in zip(sums, got):
        s.take(g)
    return list(others)


def swap_halves(value, lane):
    half = HEAD_DIM // 2
    return jnp.where(
        lane < half, pltpu.roll(value, WIDE - half, 1), pltpu.roll(value, half, 1)
    )


def own_block(values, rows, number):
    block = values[:, -rows:]
    for n in range(values.shape[1] // rows - 1):
        block = jnp.where(number == n, values[:, n * rows : (n + 1) * rows], block)
    return jnp.broadcast_to(block.astype(f32), (WIDE, rows)).T


def table_kernel(me_ref, seg_ref, rate_ref, cos_ref, sin_ref):
    segs = seg_ref[...]
    order = jnp.where(segs < 0, SEGMENTS - 1, segs)
    first_place = jnp.zeros_like(order)
    for s in range(1, SEGMENTS):
        before = jnp.sum((order < s).astype(jnp.int32), axis=1, keepdims=True)
        first_place = jnp.where(order == s, before, first_place)
    places = lax.broadcasted_iota(jnp.int32, segs.shape, 1) - first_place
    angles = own_block(places, cos_ref.shape[0], me_ref[0] ^ pl.program_id(0)) * rate_ref[...]
    lane = lax.broadcasted_iota(jnp.int32, angles.shape, 1)
    sine = jnp.sin(angles)
    cos_ref[...] = jnp.cos(angles)
    sin_ref[...] = jnp.where(lane < HEAD_DIM // 2, -sine, sine)


def rotary_tables(segments, rates, me, block):
    length = segments.shape[1]
    whole = lambda a: pl.BlockSpec(a.shape, lambda i: (0, 0))
    out = jax.ShapeDtypeStruct((length, WIDE), f32)
    return pl.pallas_call(
        table_kernel,
        grid=(length // block,),
        in_specs=[pl.BlockSpec(memory_space=pltpu.SMEM), whole(segments), whole(rates)],
        out_specs=[pl.BlockSpec((block, WIDE), lambda i: (i, 0))] * 2,
        out_shape=[out, out],
        compiler_params=pltpu.CompilerParams(vmem_limit_bytes=VMEM),
        cost_estimate=SMALL_COST,
        name="tables",
    )(me, segments, rates)


def project_kernel(heads, start, count, me_ref, *refs):
    pieces, refs = refs[:count], refs[count:]
    weights, (seg_ref, cos_ref, sin_ref) = refs[:3], refs[3:6]
    x_ref, qa_ref, ka_ref, va_ref = refs[-4:]
    rows = x_ref.shape[0]
    step = pl.program_id(0)
    for n, piece in enumerate(pieces):

        @pl.when(step == n)
        def _(piece=piece):
            x_ref[...] = piece[...]

    x = x_ref[...]
    query, key, value = (dot_nt(x, w[...]) for w in weights)
    seg = own_block(seg_ref[...], rows, me_ref[0] ^ (start + step)).astype(jnp.int32)
    lane = lax.broadcasted_iota(jnp.int32, (rows, WIDE), 1)
    cosine, sine = cos_ref[...], sin_ref[...]
    first = lane < HEAD_DIM
    same = lane == seg + (SEG_AT + 1)
    qf = jnp.where(same, APART, 0.0)
    kf = jnp.where((lane < ROW_AT + 3) & ~same, 1.0, 0.0)
    ones = jnp.where(lane < HEAD_DIM + 3, 1.0, 0.0)

    def part(values, h):
        at = h * HEAD_DIM
        if h % 2:
            return pltpu.roll(values[:, at - HEAD_DIM : at + HEAD_DIM], HEAD_DIM, 1)
        if h + 1 < heads:
            return values[:, at : at + WIDE]
        here = values[:, at : at + HEAD_DIM]
        return jnp.concatenate([here, jnp.zeros_like(here)], axis=1)

    for h in range(heads):
        q, k = part(query, h), part(key, h)
        q = q * cosine + swap_halves(q, lane) * sine
        k = k * cosine + swap_halves(k, lane) * sine
        qa_ref[h] = jnp.where(first, q * (1.0 / math.sqrt(HEAD_DIM)), qf).astype(bf16)
        ka_ref[h] = jnp.where(first, k, kf).astype(bf16)
        va_ref[h] = jnp.where(first, part(value, h), ones).astype(bf16)


def project(pieces, start, weights, segments, cosine, sine, me, heads, done=()):
    block, width = pieces[0].shape
    length = segments.shape[1]
    rows = lambda n: pl.BlockSpec((block, n), lambda i: (start + i, 0))
    whole = lambda a: pl.BlockSpec(a.shape, lambda i: (0, 0))
    out = pl.BlockSpec((heads, block, WIDE), lambda i: (0, start + i, 0))
    given = 1 + len(pieces) + 6
    return pl.pallas_call(
        functools.partial(project_kernel, heads, start, len(pieces)),
        grid=(len(pieces),),
        in_specs=[pl.BlockSpec(memory_space=pltpu.SMEM)]
        + [whole(p) for p in pieces]
        + [whole(w) for w in weights]
        + [whole(segments), rows(WIDE), rows(WIDE)]
        + [pl.BlockSpec(memory_space=pl.ANY)] * len(done),
        out_specs=[rows(width)] + [out] * 3,
        out_shape=[jax.ShapeDtypeStruct((length, width), bf16)]
        + [jax.ShapeDtypeStruct((heads, length, WIDE), bf16)] * 3,
        input_output_aliases={given + n: n for n in range(len(done))},
        compiler_params=pltpu.CompilerParams(vmem_limit_bytes=VMEM),
        cost_estimate=SMALL_COST,
        name="project",
    )(me, *pieces, *weights, segments, cosine, sine, *done)


def split3(value):
    high = value.astype(bf16).astype(f32)
    rest = value - high
    middle = rest.astype(bf16).astype(f32)
    return high, middle, rest - middle


def put_row(wide, at, value):
    lane = lax.broadcasted_iota(jnp.int32, wide.shape, 1)
    for n, part in enumerate(split3(value)):
        wide = jnp.where(lane == at + n, -part, wide)
    return wide


def attend_kernel(heads, qa_ref, ka_ref, va_ref, *refs):
    ctx_ref, qb_ref = refs[-2:]
    parts = []
    for h in range(heads):
        qa = qa_ref[h]
        scores = dot_nt(qa, ka_ref[h])
        peak = jnp.max(scores, axis=1, keepdims=True)
        weights = jnp.exp(scores - peak).astype(bf16)
        summed = dot(weights, va_ref[h])
        total = summed[:, HEAD_DIM : HEAD_DIM + 1]
        parts.append(summed[:, :HEAD_DIM] / total)
        qb_ref[h] = put_row(qa.astype(f32), ROW_AT, peak + jnp.log(total)).astype(bf16)
    ctx_ref[...] = jnp.concatenate(parts, axis=1).astype(bf16)


def attend(qa, ka, va, start, count, done=(), block=256):
    heads, length, _ = qa.shape
    first = start // block
    whole = pl.BlockSpec((heads, length, WIDE), lambda i: (0, 0, 0))
    part = pl.BlockSpec((heads, block, WIDE), lambda i: (0, first + i, 0))
    return pl.pallas_call(
        functools.partial(attend_kernel, heads),
        grid=(count // block,),
        in_specs=[part, whole, whole] + [pl.BlockSpec(memory_space=pl.ANY)] * len(done),
        out_specs=[pl.BlockSpec((block, heads * HEAD_DIM), lambda i: (first + i, 0)), part],
        out_shape=[
            jax.ShapeDtypeStruct((length, heads * HEAD_DIM), bf16),
            jax.ShapeDtypeStruct((heads, length, WIDE), bf16),
        ],
        input_output_aliases={3 + n: n for n in range(len(done))},
        compiler_params=pltpu.CompilerParams(vmem_limit_bytes=VMEM_LESS),
        cost_estimate=SMALL_COST,
        name="attend",
    )(qa, ka, va, *done)


def attend_back_kernel(heads, qb_ref, ka_ref, va_ref, *refs):
    gos, refs = refs[:4], refs[4:]
    ctx_ref, cos_ref, sin_ref, dq_ref, dk_ref, dv_ref, doa, dqt = refs
    j, h = pl.program_id(0), pl.program_id(1)
    length = qb_ref.shape[1]
    block = length // 4
    at = [pl.ds(i * block, block) for i in range(4)]

    for head in range(heads):
        cols = pl.ds(head * HEAD_DIM, HEAD_DIM)

        @pl.when((j == 0) & (h == head))
        def _(cols=cols):
            for i in range(4):
                go = gos[i][:block, cols].astype(f32)
                delta = jnp.sum(go * ctx_ref[at[i], cols].astype(f32), axis=1, keepdims=True)
                wide = jnp.concatenate([go, jnp.zeros_like(go)], axis=1)
                doa[h, at[i], :] = put_row(wide, HEAD_DIM, delta).astype(bf16)

    @pl.when(j == 0)
    def _():
        dqt[h] = jnp.zeros(dqt.shape[1:], f32)

    ka, va = ka_ref[h], va_ref[h]
    kt = ka.astype(f32).T[:HEAD_DIM].astype(bf16)
    dk = dv = None
    for i in range(4):
        qb, do = qb_ref[h, at[i], :], doa[h, at[i], :]
        weights = jnp.exp(dot_nt(ka, qb))
        grads = (weights * dot_nt(va, do)).astype(bf16)
        v_part = dot(weights.astype(bf16), do)
        k_part = dot(grads, qb)
        dk = k_part if i == 0 else dk + k_part
        dv = v_part if i == 0 else dv + v_part
        dqt[h, :, at[i]] += dot(kt, grads)
    lane = lax.broadcasted_iota(jnp.int32, dk.shape, 1)
    rows = pl.ds(pl.multiple_of(j * ka.shape[0], ka.shape[0]), ka.shape[0])
    dk = dk * cos_ref[rows, :] - swap_halves(dk, lane) * sin_ref[rows, :]
    for head in range(heads):
        cols = pl.ds(head * HEAD_DIM, HEAD_DIM)

        @pl.when(h == head)
        def _(cols=cols):
            dk_ref[:, cols] = dk[:, :HEAD_DIM].astype(bf16)
            dv_ref[:, cols] = dv[:, :HEAD_DIM].astype(bf16)

        @pl.when((h == head) & (j == pl.num_programs(0) - 1))
        def _(cols=cols):
            for i in range(4):
                part = dqt[h, :, at[i]]
                dq = jnp.concatenate([part, jnp.zeros_like(part)], axis=0).T
                lanes = lax.broadcasted_iota(jnp.int32, dq.shape, 1)
                dq = dq * cos_ref[at[i], :] - swap_halves(dq, lanes) * sin_ref[at[i], :]
                dq_ref[at[i], cols] = (dq[:, :HEAD_DIM] * (1.0 / math.sqrt(HEAD_DIM))).astype(bf16)


def attend_back(qb, ka, va, gos, ctx, cosine, sine, block_k=512):
    heads, length, _ = qb.shape
    part = pl.BlockSpec((heads, block_k, WIDE), lambda j, h: (0, j, 0))
    full = lambda a: pl.BlockSpec(a.shape, lambda j, h, r=len(a.shape): (0,) * r)
    grad = jax.ShapeDtypeStruct((length, heads * HEAD_DIM), bf16)
    rows = pl.BlockSpec((block_k, heads * HEAD_DIM), lambda j, h: (j, 0))
    return pl.pallas_call(
        functools.partial(attend_back_kernel, heads),
        grid=(length // block_k, heads),
        in_specs=[full(qb), part, part] + [full(a) for a in (*gos, ctx, cosine, sine)],
        out_specs=[full(grad), rows, rows],
        out_shape=[grad] * 3,
        scratch_shapes=[pltpu.VMEM((heads, length, WIDE), bf16), pltpu.VMEM((heads, HEAD_DIM, length), f32)],
        compiler_params=pltpu.CompilerParams(vmem_limit_bytes=VMEM),
        cost_estimate=SMALL_COST,
        name="attend_back",
    )(qb, ka, va, *gos, ctx, cosine, sine)


ANY = pl.BlockSpec(memory_space=pl.ANY)
IN_VMEM = pl.BlockSpec(memory_space=pltpu.VMEM)


def start(source, target, sem):
    copy = pltpu.make_async_copy(source, target, sem)
    copy.start()
    return copy


def norm_parts(row_values):
    centred = row_values - jnp.mean(row_values, axis=-1, keepdims=True)
    inverse = lax.rsqrt(jnp.mean(centred * centred, axis=-1, keepdims=True) + EPSILON)
    return (centred * inverse, inverse)


def norm_back(grad_norm, normalized, inverse):
    return inverse * (
        grad_norm
        - jnp.mean(grad_norm, axis=-1, keepdims=True)
        - normalized * jnp.mean(grad_norm * normalized, axis=-1, keepdims=True)
    )


def sigmoid(value):
    return 0.5 * jnp.tanh(0.5 * value) + 0.5


def feed(low, gate, up):
    gate_pre, up_pre = dot(low, gate), dot(low, up)
    return gate_pre, up_pre


def hidden_of(gate_pre, up_pre):
    return (gate_pre * sigmoid(gate_pre) * up_pre).astype(bf16)


def feed_back(grad_hidden, gate_pre, up_pre):
    part = sigmoid(gate_pre)
    active = gate_pre * part
    grad_gate = grad_hidden * up_pre * (part + active * (1.0 - part))
    return grad_gate.astype(bf16), (grad_hidden * active).astype(bf16)


def shard_copies(n, plan, refs, buffers, sem):
    copies = []
    for buffer, pieces in zip(buffers, plan[n]):
        row, width = 0, buffer.shape[2]
        for at, first in pieces:
            rows = refs[at].shape[0]
            source = refs[at].at[:, pl.ds(first * width, width)]
            copies.append(start(source, buffer.at[n, pl.ds(row, rows), :], sem.at[n, len(copies)]))
            row += rows
    return copies


def shard_plan(shards):
    args, plan = [], []
    for shard in shards:
        plan.append([])
        for pieces in shard:
            plan[-1].append([(len(args) + n, first) for n, (_, first) in enumerate(pieces)])
            args += [a for a, _ in pieces]
    return args, plan


HALVES = 2


def halves(length):
    return [pl.ds(n * (length // HALVES), length // HALVES) for n in range(HALVES)]


def arrays_of(plan):
    return sum(len(pieces) for shard in plan for pieces in shard)


def feed_shards(plan, shards, weights, coming, low, kept, targets, total, sems):
    buffers, (gates, ups), (sem, out_sem) = weights, kept, sems
    gate, up, down = weights
    hidden, going = down.shape[1], []
    for n in range(len(plan)):
        here = coming
        if n + 1 < len(plan):
            coming = shard_copies(n + 1, plan, shards, buffers, sem)
        for copy in here:
            copy.wait()
        for at in halves(low.shape[0]):
            gate_pre, up_pre = feed(low[at, :], gate[n], up[n])
            gates[n, at, :] = gate_pre.astype(bf16)
            ups[n, at, :] = up_pre.astype(bf16)
            part = dot(hidden_of(gate_pre, up_pre), down[n])
            total[at, :] = part if n == 0 else total[at, :] + part
        cols = pl.ds(n * hidden, hidden)
        for k, (buffer, target) in enumerate(zip(kept, targets)):
            going.append(start(buffer.at[n], target.at[:, cols], out_sem.at[n, k]))
    return going


def first_kernel(plan, gain_ref, shift_ref, own_ref, *refs):
    parts, outs, refs = refs[:4], refs[4:8], refs[8:]
    shards, refs = refs[: arrays_of(plan)], refs[arrays_of(plan) :]
    norm_ref, inverse_ref, low_ref, gates_ref, ups_ref, total_ref = refs[:6]
    own, part_in, out_in, norm1, inverse1, low, total, *weights = refs[6:16]
    kept, sems, (in_sem, res_sem) = refs[16:18], refs[18:20], refs[20:]
    coming = [start(own_ref, own, in_sem.at[8])]
    for n in range(4):
        coming.append(start(parts[n], part_in.at[n], in_sem.at[n]))
        coming.append(start(outs[n], out_in.at[n], in_sem.at[4 + n]))
    first = shard_copies(0, plan, shards, weights, sems[0])
    for copy in coming:
        copy.wait()
    summed = own[...].astype(f32)
    for n in range(4):
        summed = summed + dot(part_in[n], out_in[n])
    norm, inverse = norm_parts(summed)
    norm1[...] = norm
    inverse1[...] = jnp.broadcast_to(inverse, inverse1.shape)
    low[...] = (norm * gain_ref[...] + shift_ref[...]).astype(bf16)
    going = [
        start(source, target, res_sem.at[n])
        for n, (source, target) in enumerate([(low, low_ref), (norm1, norm_ref), (inverse1, inverse_ref)])
    ]
    going += feed_shards(plan, shards, weights, first, low, kept, (gates_ref, ups_ref), total, sems)
    going.append(start(total, total_ref, res_sem.at[3]))
    for copy in going:
        copy.wait()


def last_kernel(plan, low_ref, gain_ref, shift_ref, gain2_ref, shift2_ref, before_ref, norm_ref, cot_ref, *refs):
    shards, refs = refs[: arrays_of(plan)], refs[arrays_of(plan) :]
    gates_ref, ups_ref, encoded_ref, second_ref, low2_ref, small_ref = refs[:6]
    before, norm1, cot_in, total, *weights = refs[6:13]
    kept, sems, in_sem = refs[13:15], refs[15:17], refs[17]
    first = shard_copies(0, plan, shards, weights, sems[0])
    late = [
        start(source, target, in_sem.at[n])
        for n, (source, target) in enumerate([(before_ref, before), (norm_ref, norm1), (cot_ref, cot_in)])
    ]
    going = feed_shards(plan, shards, weights, first, low_ref, kept, (gates_ref, ups_ref), total, sems)
    for copy in late:
        copy.wait()
    normed = norm1[...] * gain_ref[...] + shift_ref[...]
    norm, inverse = norm_parts(normed + (before[...] + total[...]))
    cot = cot_in[...].astype(f32)
    encoded_ref[...] = (norm * gain2_ref[...] + shift2_ref[...]).astype(bf16)
    grad = norm_back(cot * gain2_ref[...], norm, inverse)
    second_ref[...] = grad
    low2_ref[...] = grad.astype(bf16)
    small_ref[...] = jnp.concatenate(
        [jnp.sum(cot * norm, axis=0, keepdims=True), jnp.sum(cot, axis=0, keepdims=True)], axis=0
    )
    for copy in going:
        copy.wait()


def shard_scratch(count, length, width, hidden):
    return [
        pltpu.VMEM((count, width, hidden), bf16),
        pltpu.VMEM((count, width, hidden), bf16),
        pltpu.VMEM((count, hidden, width), bf16),
        pltpu.VMEM((count, length, hidden), bf16),
        pltpu.VMEM((count, length, hidden), bf16),
        pltpu.SemaphoreType.DMA((count, 4)),
        pltpu.SemaphoreType.DMA((count, 2)),
    ]


def forward_first(own, parts, outs, shards, gain, shift):
    length, width = own.shape
    count, hidden = len(shards), sum(a.shape[0] for a, _ in shards[0][2])
    args, plan = shard_plan(shards)
    kept = jax.ShapeDtypeStruct((length, hidden * count), bf16)
    norm = jax.ShapeDtypeStruct((length, width), f32)
    inverse = jax.ShapeDtypeStruct((length, WIDE), f32)
    low = jax.ShapeDtypeStruct((length, width), bf16)
    shapes = [norm, inverse, low, kept, kept, norm]
    vmem = lambda a: pltpu.VMEM(a.shape, a.dtype)
    stack = lambda arrays: pltpu.VMEM((len(arrays), *arrays[0].shape), bf16)
    return pl.pallas_call(
        functools.partial(first_kernel, plan),
        in_specs=[IN_VMEM] * 2 + [ANY] * (9 + len(args)),
        out_specs=[ANY] * len(shapes),
        out_shape=shapes,
        scratch_shapes=[vmem(own), stack(parts), stack(outs), vmem(norm), vmem(inverse), vmem(low), vmem(norm)]
        + shard_scratch(count, length, width, hidden)
        + [pltpu.SemaphoreType.DMA((9,)), pltpu.SemaphoreType.DMA((4,))],
        compiler_params=pltpu.CompilerParams(vmem_limit_bytes=VMEM),
        cost_estimate=SMALL_COST,
        name="feed_first",
    )(gain, shift, own, *parts, *outs, *args)


def forward_last(low, shards, before, norm, cot, vectors):
    length, width = low.shape
    count, hidden = len(shards), sum(a.shape[0] for a, _ in shards[0][2])
    args, plan = shard_plan(shards)
    kept = jax.ShapeDtypeStruct((length, hidden * count), bf16)
    wide = jax.ShapeDtypeStruct((length, width), f32)
    rounded = jax.ShapeDtypeStruct((length, width), bf16)
    small = jax.ShapeDtypeStruct((2, width), f32)
    vmem = lambda a: pltpu.VMEM(a.shape, a.dtype)
    return pl.pallas_call(
        functools.partial(last_kernel, plan),
        in_specs=[IN_VMEM] * 5 + [ANY] * (3 + len(args)),
        out_specs=[ANY] * 2 + [IN_VMEM] * 4,
        out_shape=[kept, kept, rounded, wide, rounded, small],
        scratch_shapes=[vmem(a) for a in (wide, wide, cot, wide)]
        + shard_scratch(count, length, width, hidden)
        + [pltpu.SemaphoreType.DMA((3,))],
        compiler_params=pltpu.CompilerParams(vmem_limit_bytes=VMEM),
        cost_estimate=SMALL_COST,
        name="feed_last",
    )(low, *vectors, before, norm, cot, *args)


def backward_kernel(plan, where, low2_ref, *refs):
    count = len(plan)
    shards, refs = refs[: arrays_of(plan)], refs[arrays_of(plan) :]
    pairs = where[-1][0] + 1
    saved, refs = refs[: 2 * pairs], refs[2 * pairs :]
    late_refs, refs = refs[:7], refs[7:]
    gain_ref, small_in_ref, first_ref, low_ref, *ctx_refs = refs[:8]
    gate, up, down, gates, ups, total, second, norm1, inverse, outs, sem, saved_sem, late_sem = refs[8:]
    buffers = (gate, up, down)
    hidden = down.shape[1]

    def fetch(n):
        part, cols = where[n][0], pl.ds(where[n][1] * hidden, hidden)
        return shard_copies(n, plan, shards, buffers, sem) + [
            start(ref.at[:, cols], buffer.at[n], saved_sem.at[n, k])
            for k, (ref, buffer) in enumerate(zip(saved[2 * part : 2 * part + 2], (gates, ups)))
        ]

    coming = [fetch(0)]
    late = []
    for n in range(count):
        if n + 1 < count:
            coming.append(fetch(n + 1))
        else:
            targets = [second, norm1, inverse] + [outs.at[k] for k in range(4)]
            late = [start(ref, target, late_sem.at[k]) for k, (ref, target) in enumerate(zip(late_refs, targets))]
        for copy in coming[n]:
            copy.wait()
        for at in halves(low2_ref.shape[0]):
            grad_hidden = dot_nt(low2_ref[at, :], down[n])
            grad_gate, grad_up = feed_back(grad_hidden, gates[n, at, :].astype(f32), ups[n, at, :].astype(f32))
            part = dot_nt(grad_gate, gate[n]) + dot_nt(grad_up, up[n])
            total[at, :] = part if n == 0 else total[at, :] + part
    for copy in late:
        copy.wait()
    normed_grad, norm = second[...] + total[...], norm1[...]
    first = norm_back(normed_grad * gain_ref[...], norm, inverse[:, :1])
    first_ref[...] = first
    low = first.astype(bf16)
    low_ref[...] = low
    small = jnp.concatenate(
        [
            jnp.sum(normed_grad * norm, axis=0, keepdims=True),
            jnp.sum(normed_grad, axis=0, keepdims=True),
            small_in_ref[...],
        ],
        axis=0,
    )
    width = outs.shape[1]
    small = jnp.concatenate([small[:, k * width : (k + 1) * width] for k in range(4)], axis=0)
    high = small.astype(bf16)
    small = jnp.concatenate([high, (small - high.astype(f32)).astype(bf16)], axis=0)
    length = low.shape[0]
    for k in range(4):
        ctx_refs[k][:length, :] = dot_nt(low, outs[k]).astype(bf16)
        ctx_refs[k][length:, :] = small


SMALL = 32


def backward(low2, shards, saved, second, norm, inverse, outs, gain, small):
    length, width = low2.shape
    count, hidden = len(shards), sum(a.shape[0] for a, _ in shards[0][2])
    args, plan = shard_plan(shards)
    where = [(n, k) for n, (gates, _) in enumerate(saved) for k in range(gates.shape[1] // hidden)]
    saved = [a for pair in saved for a in pair]
    late = [second, norm, inverse, *outs]
    wide = pltpu.VMEM((length, width), f32)
    return pl.pallas_call(
        functools.partial(backward_kernel, plan, where),
        in_specs=[IN_VMEM] + [ANY] * (len(args) + len(saved) + len(late)) + [IN_VMEM] * 2,
        out_specs=[IN_VMEM] * 6,
        out_shape=[
            jax.ShapeDtypeStruct((length, width), f32),
            jax.ShapeDtypeStruct((length, width), bf16),
        ]
        + [jax.ShapeDtypeStruct((length + SMALL, outs[0].shape[0]), bf16)] * 4,
        scratch_shapes=[
            pltpu.VMEM((count, width, hidden), bf16),
            pltpu.VMEM((count, width, hidden), bf16),
            pltpu.VMEM((count, hidden, width), bf16),
            pltpu.VMEM((count, length, hidden), bf16),
            pltpu.VMEM((count, length, hidden), bf16),
            wide,
            wide,
            wide,
            pltpu.VMEM(inverse.shape, f32),
            pltpu.VMEM((4, *outs[0].shape), bf16),
            pltpu.SemaphoreType.DMA((count, 4)),
            pltpu.SemaphoreType.DMA((count, 2)),
            pltpu.SemaphoreType.DMA((len(late),)),
        ],
        compiler_params=pltpu.CompilerParams(vmem_limit_bytes=VMEM),
        cost_estimate=SMALL_COST,
        name="feed_back",
    )(low2, *args, *saved, *late, gain, small)


def weights_kernel(*refs):
    rows, grads, weights, refs = refs[:4], refs[4:8], refs[8:11], refs[11:]
    target, refs = refs[0], refs[1:]
    gate, up, down, low, low_t, low2, dgate, dup, hidden_t, result, sem, out_sem = refs
    block = rows[0].shape[0]
    at = [pl.ds(n * block, block) for n in range(4)]

    def fetch(n):
        return [
            start(rows[n], low.at[at[n], :], sem.at[n, 0]),
            start(grads[n], low2.at[at[n], :], sem.at[n, 1]),
        ]

    own = [start(weights[0], gate, sem.at[4, 0])]
    coming = [fetch(0)]
    own += [start(weights[k], buffer, sem.at[4 + k, 0]) for k, buffer in ((1, up), (2, down))]
    coming.append(fetch(1))
    for copy in own:
        copy.wait()
    for n in range(4):
        if n + 2 < 4:
            coming.append(fetch(n + 2))
        for copy in coming[n]:
            copy.wait()
        low_t[:, at[n]] = low[at[n], :].T
        for m in range(HALVES):
            part = pl.ds(n * block + m * (block // HALVES), block // HALVES)
            gate_pre, up_pre = feed(low[part, :], gate[...], up[...])
            grad_hidden = dot_nt(low2[part, :], down[...])
            dgate[part, :], dup[part, :] = feed_back(grad_hidden, gate_pre, up_pre)
            hidden_t[:, part] = hidden_of(gate_pre, up_pre).T
    going = []
    for k, (left, right) in enumerate([(low_t, dgate), (low_t, dup), (hidden_t, low2)]):
        result[k] = dot(left[...], right[...]).astype(bf16)
        rows_at = pl.ds(k * result.shape[1], result.shape[1])
        going.append(start(result.at[k], target.at[rows_at, :], out_sem.at[k]))
    for copy in going:
        copy.wait()


def weight_grads(rows, grads, gate, up, down):
    block, width = rows[0].shape
    length, hidden = 4 * block, gate.shape[1]
    return pl.pallas_call(
        weights_kernel,
        in_specs=[ANY] * 11,
        out_specs=ANY,
        out_shape=jax.ShapeDtypeStruct((3 * width, hidden), bf16),
        scratch_shapes=[
            pltpu.VMEM((width, hidden), bf16),
            pltpu.VMEM((width, hidden), bf16),
            pltpu.VMEM((hidden, width), bf16),
            pltpu.VMEM((length, width), bf16),
            pltpu.VMEM((width, length), bf16),
            pltpu.VMEM((length, width), bf16),
            pltpu.VMEM((length, hidden), bf16),
            pltpu.VMEM((length, hidden), bf16),
            pltpu.VMEM((hidden, length), bf16),
            pltpu.VMEM((3, width, hidden), bf16),
            pltpu.SemaphoreType.DMA((7, 2)),
            pltpu.SemaphoreType.DMA((3,)),
        ],
        compiler_params=pltpu.CompilerParams(vmem_limit_bytes=VMEM),
        cost_estimate=SMALL_COST,
        name="feed_weights",
    )(*rows, *grads, gate, up, down)


def local(
    tokens,
    segment_ids,
    query_weight,
    key_weight,
    value_weight,
    output_weight,
    attn_gain,
    attn_shift,
    gate_weight,
    up_weight,
    down_weight,
    mlp_gain,
    mlp_shift,
    cotangent,
):
    own = tokens[0]
    head_width = query_weight.shape[1]
    heads = head_width // HEAD_DIM
    group = lax.axis_size("tensor")
    block = own.shape[0]
    dp = lax.axis_size("dp")
    bits = list(range(int(math.log2(dp))))
    groups = [bits[:1]] + [bits[n : n + 2] for n in range(1, len(bits), 2)]

    near = lambda a: swap(a, "tensor", 1)
    far = lambda a: swap(a, "tensor", 2)

    share = gate_weight.shape[0] // dp
    at = lax.axis_index("dp") * share
    mine = jnp.concatenate(
        [lax.dynamic_slice_in_dim(w, at, share, 0) for w in (gate_weight, up_weight)], axis=1
    )
    far_own = far(own)
    near_own = near(own)
    angle_rate = ROPE_BASE ** (-(jnp.arange(HEAD_DIM // 2, dtype=f32) * 2.0 / HEAD_DIM))
    rates = jnp.concatenate([angle_rate, angle_rate, jnp.zeros(HEAD_DIM, f32)])[None, :]
    me = lax.axis_index("tensor").astype(jnp.int32)[None]
    cosine, sine = rotary_tables(segment_ids, rates, me, block)
    inputs = ([w.T for w in (query_weight, key_weight, value_weight)], segment_ids, cosine, sine, me, heads)
    third = down_weight.shape[0] // 3
    downs = [down_weight[:third], down_weight[third:]]
    near_half = project([after(own, mine, *downs), near_own], 0, *inputs)
    far_own = after(far_own, near_half[0])
    both_own = near(far_own)
    mine = after(mine, far_own)
    far_mine = far(mine)
    near_weights = [near(w) for w in all_after([gate_weight, up_weight, down_weight, output_weight], both_own)]
    x_full, qa, ka, va = project([far_own, after(both_own, mine)], 2, *inputs, done=near_half)
    far_mine, *near_weights = all_after([far_mine, *near_weights], qa)
    near_gate, near_up, near_down, near_out = near_weights
    far_mixed = lax.all_gather(far_mine, "dp", axis=0, tiled=True)
    out_sent, downs[0] = all_after([output_weight, downs[0]], far_mine)
    far_out, early_down = far(out_sent), far(downs[0])
    qa = after(qa, out_sent, downs[0], *near_weights)

    def send(value, j):
        return swap(value[j * block : (j + 1) * block], "tensor", j)

    half = attend(qa, ka, va, 2 * block, 2 * block)
    far_out, early_down = all_after([far_out, early_down], half[0])
    slices = [half[0][j * block : (j + 1) * block] for j in (2, 3)]
    ctx_far = [swap(c, "tensor", j) for c, j in zip(slices, (2, 3))]
    both_out, both_early = near(far_out), near(early_down)
    ctx, qb = attend(after(qa, far_out, early_down, *slices), ka, va, 0, 2 * block, done=half)
    both_out, both_early, *ctx_far = all_after([both_out, both_early, *ctx_far], ctx)
    near_ctx = send(ctx, 1)
    down_sent = after(downs[1], *ctx_far)
    far_down = [early_down, far(down_sent)]
    ctx_parts = [ctx[:block], near_ctx, *ctx_far]
    outs = [output_weight, near_out, far_out, both_out]
    row = lambda a: a[None, :]

    near_shards = [
        ([(gate_weight, 0)], [(up_weight, 0)], [(down_weight, 0)]),
        ([(near_gate, 0)], [(near_up, 0)], [(near_down, 0)]),
    ]
    first_norm, inverse, normed_low, *saved_a, half_way = forward_first(
        after(own, down_sent), ctx_parts, outs, near_shards, row(attn_gain), row(attn_shift)
    )
    near_rows = near(normed_low)
    far_mixed, *far_down = all_after([far_mixed, *far_down], half_way)
    both_mixed, both_down = near(far_mixed), [both_early, near(far_down[1])]
    rows_sent = after(normed_low, half_way)
    far_rows = far(rows_sent)
    shards = near_shards + [
        ([(mixed, 0)], [(mixed, 1)], [(d, 0) for d in down])
        for mixed, down in ((far_mixed, far_down), (both_mixed, both_down))
    ]
    *saved_b, encoded, grad_second, grad_low, small = forward_last(
        after(normed_low, rows_sent),
        shards[2:],
        half_way,
        first_norm,
        cotangent[0],
        (row(attn_gain), row(attn_shift), row(mlp_gain), row(mlp_shift)),
    )
    near_rows, far_rows = all_after([near_rows, far_rows], grad_low)
    both_rows = near(far_rows)
    near_grads, far_grads = near(grad_low), far(grad_low)
    grad_first, grad_attn_low, own_ctx, *sent_ctx = backward(
        after(grad_low, far_rows),
        shards,
        (saved_a, saved_b),
        grad_second,
        first_norm,
        inverse,
        outs,
        row(attn_gain),
        small,
    )
    near_grads, far_grads, both_rows = all_after([near_grads, far_grads, both_rows], grad_first)
    both_grads = near(far_grads)
    got_ctx = [swap(g, "tensor", j + 1) for j, g in enumerate(sent_ctx)]
    grad_feed = weight_grads(
        [after(normed_low, *sent_ctx), near_rows, far_rows, both_rows],
        [grad_low, near_grads, far_grads, both_grads],
        gate_weight,
        up_weight,
        down_weight,
    )
    grad_ctx = all_after(got_ctx, grad_feed)
    feed_part = lax.psum_scatter(after(grad_feed, *grad_ctx), "dp", scatter_dimension=0, tiled=True)
    grad_ctx = [own_ctx, *grad_ctx]
    grad_attn_low = after(grad_attn_low, grad_feed)
    sent = jnp.concatenate([dot_tn(ctx_parts[j], grad_attn_low) for j in (1, 3)], axis=0).astype(bf16)
    got = near(sent)
    kept = [dot_tn(ctx_parts[j], after(grad_attn_low, sent)) for j in (0, 2)]
    small = sum(g[block:].astype(f32) for g in grad_ctx)
    small = (small[: SMALL // 2] + small[SMALL // 2 :]).reshape(4, 4, head_width)
    small = small.transpose(1, 0, 2).reshape(4, -1).astype(bf16)
    got, *kept = all_after([got, *kept])
    sent = (kept[1] + got[head_width:].astype(f32)).astype(bf16)
    kept = kept[0] + got[:head_width].astype(f32)
    got = far(sent)

    dq, dk, dv = attend_back(qb, ka, va, all_after(grad_ctx, small, sent, kept), ctx, cosine, sine)
    grad_out = (kept + after(got, dq).astype(f32)).astype(bf16)
    joint = [dot_tn(g, x_full).astype(bf16) for g in (dq, dk, dv)]
    joint = jnp.concatenate([*joint, grad_out, small], axis=0)
    joint = jnp.pad(joint, ((0, -len(joint) % (8 * dp)), (0, 0)))
    sums = [Sum(split_rows(joint, "dp", groups[0]), groups)]
    parts = all_after([dq, dk, dv], *[s.sent for s in sums])
    weights = [query_weight, key_weight, value_weight]

    def token_part(j):
        return sum(dot_nt(g[j * block : (j + 1) * block], w) for g, w in zip(parts, weights))

    sent = jnp.concatenate([token_part(j).astype(bf16) for j in (1, 3)], axis=0)
    got = near(sent)
    parts = all_after(parts, sent)
    mine, far_sent = token_part(0), token_part(2)
    got, mine, far_sent, feed_part = take_round(sums, got, mine, far_sent, feed_part)
    grad_feed = lax.all_gather(feed_part, "dp", axis=0, tiled=True)
    far_sent = (far_sent + got[block:].astype(f32)).astype(bf16)
    got_rows = far(far_sent)
    mine = grad_first + mine + got[:block].astype(f32)
    (got_rows,) = take_round(sums, got_rows)
    grad_tokens = mine + got_rows.astype(f32)
    while any(s.result is None for s in sums):
        take_round([s for s in sums if s.result is None])
    joint = sums[0].result.astype(f32)
    grad_gate, grad_up, grad_down = jnp.split(grad_feed.astype(f32), 3, axis=0)
    grad_joint = [joint[n * head_width : (n + 1) * head_width] for n in range(4)]
    grad_out = grad_joint.pop()
    small = joint[4 * head_width : 4 * head_width + 4]
    grad_joint = [g.T for g in grad_joint]
    return (
        encoded[None],
        grad_tokens[None],
        *grad_joint,
        grad_out,
        small[0],
        small[1],
        grad_gate,
        grad_up,
        grad_down,
        small[2],
        small[3],
    )


def solution(mesh):
    rows, cols, lead = P("dp", "tensor", None), P(None, "tensor"), P("tensor", None)
    return jax.shard_map(
        local,
        mesh=mesh,
        in_specs=(
            rows, P("dp", None), cols, cols, cols, lead, P(), P(), cols, cols, lead, P(), P(), rows,
        ),
        out_specs=(
            rows, rows, cols, cols, cols, lead, P(), P(), cols, cols, lead, P(), P(),
        ),
        check_vma=False,
    )
```

```python
import functools
import math

import jax
import jax.numpy as jnp
from jax import lax
from jax.experimental import pallas as pl
from jax.experimental.pallas import tpu as pltpu
from jax.sharding import PartitionSpec as P

HEAD_DIM = 64
EPSILON = 1e-05
ROPE_BASE = 1000.0
APART = -(2.0**30)
WIDE = 128
SEGMENTS = 7
SEG_AT = HEAD_DIM
ROW_AT = HEAD_DIM + 8
VMEM = 60 * 2**20
VMEM_LESS = 44 * 2**20
SMALL_COST = pl.CostEstimate(flops=2**20, bytes_accessed=2**16, transcendentals=0)
bf16 = jnp.bfloat16
f32 = jnp.float32
NT = (((1,), (1,)), ((), ()))
TN = (((0,), (0,)), ((), ()))


def dot(a, b):
    return jnp.dot(a, b, preferred_element_type=f32)


def dot_nt(a, b):
    return lax.dot_general(a, b, NT, preferred_element_type=f32)


def dot_tn(a, b):
    return lax.dot_general(a, b, TN, preferred_element_type=f32)


def swap(value, axis, bit):
    size = lax.axis_size(axis)
    return lax.ppermute(value, axis, [(i, i ^ bit) for i in range(size)])


def after(value, *others):
    return lax.optimization_barrier((value, *others))[0]


def all_after(values, *others):
    return list(lax.optimization_barrier((tuple(values), others))[0])


def scatter_sum(blocks, axis):
    held = dict(enumerate(blocks))
    rows = blocks[0].shape[0]
    step = 1
    while step < len(blocks):
        sent = [k for k in held if k & step]
        got = [held.pop(k).astype(bf16) for k in sent]
        got = swap(got[0] if len(got) == 1 else jnp.concatenate(got, axis=0), axis, step)
        for n, k in enumerate(sent):
            held[k ^ step] = held[k ^ step] + got[n * rows : (n + 1) * rows].astype(f32)
        step *= 2
    return held[0]


def peers(axis, bits):
    me = lax.axis_index(axis)
    mine = sum(((me >> bit) & 1) << n for n, bit in enumerate(bits))
    far = [sum(((j >> n) & 1) << bit for n, bit in enumerate(bits)) for j in range(1 << len(bits))]
    return mine, far


def split_rows(value, axis, bits):
    mine, far = peers(axis, bits)
    rows = value.shape[0] // len(far)
    return [lax.dynamic_slice_in_dim(value, (mine ^ j) * rows, rows, 0) for j in range(len(far))]


def join_rows(parts, axis, bits):
    mine, _ = peers(axis, bits)

    def pick(p):
        value = parts[-1]
        for j in reversed(range(len(parts) - 1)):
            value = jnp.where(mine == p ^ j, parts[j], value)
        return value

    return jnp.concatenate([pick(p) for p in range(len(parts))], axis=0)


def sum_steps(parts, axis, groups):
    for n, bits in enumerate(groups):
        if n:
            parts = split_rows(value, axis, bits)
        _, far = peers(axis, bits)
        got = yield parts[1:], [swap(part, axis, step) for part, step in zip(parts[1:], far[1:])]
        value = sum((g.astype(f32) for g in got), parts[0].astype(f32)).astype(bf16)
    for bits in reversed(groups):
        _, far = peers(axis, bits)
        got = yield [value], [swap(value, axis, step) for step in far[1:]]
        value = join_rows([value, *got], axis, bits)
    return value


class Sum:
    def __init__(self, parts, groups):
        self.steps = sum_steps(parts, "dp", groups)
        self.result = None
        self.sent, self.got = next(self.steps)

    def take(self, got):
        if self.result is None:
            try:
                self.sent, self.got = self.steps.send(got)
            except StopIteration as end:
                self.result, self.sent, self.got = end.value, [], []


def take_round(sums, *others):
    got, others = lax.optimization_barrier(([s.got for s in sums], others))
    for s, g in zip(sums, got):
        s.take(g)
    return list(others)


def swap_halves(value, lane):
    half = HEAD_DIM // 2
    return jnp.where(
        lane < half, pltpu.roll(value, WIDE - half, 1), pltpu.roll(value, half, 1)
    )


def own_block(values, rows, number):
    block = values[:, -rows:]
    for n in range(values.shape[1] // rows - 1):
        block = jnp.where(number == n, values[:, n * rows : (n + 1) * rows], block)
    return jnp.broadcast_to(block.astype(f32), (WIDE, rows)).T


def table_kernel(me_ref, seg_ref, rate_ref, cos_ref, sin_ref):
    segs = seg_ref[...]
    order = jnp.where(segs < 0, SEGMENTS - 1, segs)
    first_place = jnp.zeros_like(order)
    for s in range(1, SEGMENTS):
        before = jnp.sum((order < s).astype(jnp.int32), axis=1, keepdims=True)
        first_place = jnp.where(order == s, before, first_place)
    places = lax.broadcasted_iota(jnp.int32, segs.shape, 1) - first_place
    angles = own_block(places, cos_ref.shape[0], me_ref[0] ^ pl.program_id(0)) * rate_ref[...]
    lane = lax.broadcasted_iota(jnp.int32, angles.shape, 1)
    sine = jnp.sin(angles)
    cos_ref[...] = jnp.cos(angles)
    sin_ref[...] = jnp.where(lane < HEAD_DIM // 2, -sine, sine)


def rotary_tables(segments, rates, me, block):
    length = segments.shape[1]
    whole = lambda a: pl.BlockSpec(a.shape, lambda i: (0, 0))
    out = jax.ShapeDtypeStruct((length, WIDE), f32)
    return pl.pallas_call(
        table_kernel,
        grid=(length // block,),
        in_specs=[pl.BlockSpec(memory_space=pltpu.SMEM), whole(segments), whole(rates)],
        out_specs=[pl.BlockSpec((block, WIDE), lambda i: (i, 0))] * 2,
        out_shape=[out, out],
        compiler_params=pltpu.CompilerParams(vmem_limit_bytes=VMEM),
        cost_estimate=SMALL_COST,
        name="tables",
    )(me, segments, rates)


def project_kernel(heads, start, count, me_ref, *refs):
    pieces, refs = refs[:count], refs[count:]
    weights, (seg_ref, cos_ref, sin_ref) = refs[:3], refs[3:6]
    x_ref, qa_ref, ka_ref, va_ref = refs[-4:]
    rows = x_ref.shape[0]
    step = pl.program_id(0)
    for n, piece in enumerate(pieces):

        @pl.when(step == n)
        def _(piece=piece):
            x_ref[...] = piece[...]

    x = x_ref[...]
    query, key, value = (dot_nt(x, w[...]) for w in weights)
    seg = own_block(seg_ref[...], rows, me_ref[0] ^ (start + step)).astype(jnp.int32)
    lane = lax.broadcasted_iota(jnp.int32, (rows, WIDE), 1)
    cosine, sine = cos_ref[...], sin_ref[...]
    first = lane < HEAD_DIM
    same = lane == seg + (SEG_AT + 1)
    qf = jnp.where(same, APART, 0.0)
    kf = jnp.where((lane < ROW_AT + 3) & ~same, 1.0, 0.0)
    ones = jnp.where(lane < HEAD_DIM + 3, 1.0, 0.0)

    def part(values, h):
        at = h * HEAD_DIM
        if h % 2:
            return pltpu.roll(values[:, at - HEAD_DIM : at + HEAD_DIM], HEAD_DIM, 1)
        if h + 1 < heads:
            return values[:, at : at + WIDE]
        here = values[:, at : at + HEAD_DIM]
        return jnp.concatenate([here, jnp.zeros_like(here)], axis=1)

    for h in range(heads):
        q, k = part(query, h), part(key, h)
        q = q * cosine + swap_halves(q, lane) * sine
        k = k * cosine + swap_halves(k, lane) * sine
        qa_ref[h] = jnp.where(first, q * (1.0 / math.sqrt(HEAD_DIM)), qf).astype(bf16)
        ka_ref[h] = jnp.where(first, k, kf).astype(bf16)
        va_ref[h] = jnp.where(first, part(value, h), ones).astype(bf16)


def project(pieces, start, weights, segments, cosine, sine, me, heads, done=()):
    block, width = pieces[0].shape
    length = segments.shape[1]
    rows = lambda n: pl.BlockSpec((block, n), lambda i: (start + i, 0))
    whole = lambda a: pl.BlockSpec(a.shape, lambda i: (0, 0))
    out = pl.BlockSpec((heads, block, WIDE), lambda i: (0, start + i, 0))
    given = 1 + len(pieces) + 6
    return pl.pallas_call(
        functools.partial(project_kernel, heads, start, len(pieces)),
        grid=(len(pieces),),
        in_specs=[pl.BlockSpec(memory_space=pltpu.SMEM)]
        + [whole(p) for p in pieces]
        + [whole(w) for w in weights]
        + [whole(segments), rows(WIDE), rows(WIDE)]
        + [pl.BlockSpec(memory_space=pl.ANY)] * len(done),
        out_specs=[rows(width)] + [out] * 3,
        out_shape=[jax.ShapeDtypeStruct((length, width), bf16)]
        + [jax.ShapeDtypeStruct((heads, length, WIDE), bf16)] * 3,
        input_output_aliases={given + n: n for n in range(len(done))},
        compiler_params=pltpu.CompilerParams(vmem_limit_bytes=VMEM),
        cost_estimate=SMALL_COST,
        name="project",
    )(me, *pieces, *weights, segments, cosine, sine, *done)


def split3(value):
    high = value.astype(bf16).astype(f32)
    rest = value - high
    middle = rest.astype(bf16).astype(f32)
    return high, middle, rest - middle


def put_row(wide, at, value):
    lane = lax.broadcasted_iota(jnp.int32, wide.shape, 1)
    for n, part in enumerate(split3(value)):
        wide = jnp.where(lane == at + n, -part, wide)
    return wide


def attend_kernel(heads, qa_ref, ka_ref, va_ref, *refs):
    ctx_ref, qb_ref = refs[-2:]
    parts = []
    for h in range(heads):
        qa = qa_ref[h]
        scores = dot_nt(qa, ka_ref[h])
        peak = jnp.max(scores, axis=1, keepdims=True)
        weights = jnp.exp(scores - peak).astype(bf16)
        summed = dot(weights, va_ref[h])
        total = summed[:, HEAD_DIM : HEAD_DIM + 1]
        parts.append(summed[:, :HEAD_DIM] / total)
        qb_ref[h] = put_row(qa.astype(f32), ROW_AT, peak + jnp.log(total)).astype(bf16)
    ctx_ref[...] = jnp.concatenate(parts, axis=1).astype(bf16)


def attend(qa, ka, va, start, count, done=(), block=256):
    heads, length, _ = qa.shape
    first = start // block
    whole = pl.BlockSpec((heads, length, WIDE), lambda i: (0, 0, 0))
    part = pl.BlockSpec((heads, block, WIDE), lambda i: (0, first + i, 0))
    return pl.pallas_call(
        functools.partial(attend_kernel, heads),
        grid=(count // block,),
        in_specs=[part, whole, whole] + [pl.BlockSpec(memory_space=pl.ANY)] * len(done),
        out_specs=[pl.BlockSpec((block, heads * HEAD_DIM), lambda i: (first + i, 0)), part],
        out_shape=[
            jax.ShapeDtypeStruct((length, heads * HEAD_DIM), bf16),
            jax.ShapeDtypeStruct((heads, length, WIDE), bf16),
        ],
        input_output_aliases={3 + n: n for n in range(len(done))},
        compiler_params=pltpu.CompilerParams(vmem_limit_bytes=VMEM_LESS),
        cost_estimate=SMALL_COST,
        name="attend",
    )(qa, ka, va, *done)


def attend_back_kernel(heads, qb_ref, ka_ref, va_ref, *refs):
    gos, refs = refs[:4], refs[4:]
    ctx_ref, cos_ref, sin_ref, dq_ref, dk_ref, dv_ref, doa, dqt = refs
    j, h = pl.program_id(0), pl.program_id(1)
    length = qb_ref.shape[1]
    block = length // 4
    at = [pl.ds(i * block, block) for i in range(4)]

    for head in range(heads):
        cols = pl.ds(head * HEAD_DIM, HEAD_DIM)

        @pl.when((j == 0) & (h == head))
        def _(cols=cols):
            for i in range(4):
                go = gos[i][:block, cols].astype(f32)
                delta = jnp.sum(go * ctx_ref[at[i], cols].astype(f32), axis=1, keepdims=True)
                wide = jnp.concatenate([go, jnp.zeros_like(go)], axis=1)
                doa[h, at[i], :] = put_row(wide, HEAD_DIM, delta).astype(bf16)

    @pl.when(j == 0)
    def _():
        dqt[h] = jnp.zeros(dqt.shape[1:], f32)

    ka, va = ka_ref[h], va_ref[h]
    kt = ka.astype(f32).T[:HEAD_DIM].astype(bf16)
    dk = dv = None
    for i in range(4):
        qb, do = qb_ref[h, at[i], :], doa[h, at[i], :]
        weights = jnp.exp(dot_nt(ka, qb))
        grads = (weights * dot_nt(va, do)).astype(bf16)
        v_part = dot(weights.astype(bf16), do)
        k_part = dot(grads, qb)
        dk = k_part if i == 0 else dk + k_part
        dv = v_part if i == 0 else dv + v_part
        dqt[h, :, at[i]] += dot(kt, grads)
    lane = lax.broadcasted_iota(jnp.int32, dk.shape, 1)
    rows = pl.ds(pl.multiple_of(j * ka.shape[0], ka.shape[0]), ka.shape[0])
    dk = dk * cos_ref[rows, :] - swap_halves(dk, lane) * sin_ref[rows, :]
    for head in range(heads):
        cols = pl.ds(head * HEAD_DIM, HEAD_DIM)

        @pl.when(h == head)
        def _(cols=cols):
            dk_ref[:, cols] = dk[:, :HEAD_DIM].astype(bf16)
            dv_ref[:, cols] = dv[:, :HEAD_DIM].astype(bf16)

        @pl.when((h == head) & (j == pl.num_programs(0) - 1))
        def _(cols=cols):
            for i in range(4):
                part = dqt[h, :, at[i]]
                dq = jnp.concatenate([part, jnp.zeros_like(part)], axis=0).T
                lanes = lax.broadcasted_iota(jnp.int32, dq.shape, 1)
                dq = dq * cos_ref[at[i], :] - swap_halves(dq, lanes) * sin_ref[at[i], :]
                dq_ref[at[i], cols] = (dq[:, :HEAD_DIM] * (1.0 / math.sqrt(HEAD_DIM))).astype(bf16)


def attend_back(qb, ka, va, gos, ctx, cosine, sine, block_k=512):
    heads, length, _ = qb.shape
    part = pl.BlockSpec((heads, block_k, WIDE), lambda j, h: (0, j, 0))
    full = lambda a: pl.BlockSpec(a.shape, lambda j, h, r=len(a.shape): (0,) * r)
    grad = jax.ShapeDtypeStruct((length, heads * HEAD_DIM), bf16)
    rows = pl.BlockSpec((block_k, heads * HEAD_DIM), lambda j, h: (j, 0))
    return pl.pallas_call(
        functools.partial(attend_back_kernel, heads),
        grid=(length // block_k, heads),
        in_specs=[full(qb), part, part] + [full(a) for a in (*gos, ctx, cosine, sine)],
        out_specs=[full(grad), rows, rows],
        out_shape=[grad] * 3,
        scratch_shapes=[pltpu.VMEM((heads, length, WIDE), bf16), pltpu.VMEM((heads, HEAD_DIM, length), f32)],
        compiler_params=pltpu.CompilerParams(vmem_limit_bytes=VMEM),
        cost_estimate=SMALL_COST,
        name="attend_back",
    )(qb, ka, va, *gos, ctx, cosine, sine)


ANY = pl.BlockSpec(memory_space=pl.ANY)
IN_VMEM = pl.BlockSpec(memory_space=pltpu.VMEM)


def start(source, target, sem):
    copy = pltpu.make_async_copy(source, target, sem)
    copy.start()
    return copy


def norm_parts(row_values):
    centred = row_values - jnp.mean(row_values, axis=-1, keepdims=True)
    inverse = lax.rsqrt(jnp.mean(centred * centred, axis=-1, keepdims=True) + EPSILON)
    return (centred * inverse, inverse)


def norm_back(grad_norm, normalized, inverse):
    return inverse * (
        grad_norm
        - jnp.mean(grad_norm, axis=-1, keepdims=True)
        - normalized * jnp.mean(grad_norm * normalized, axis=-1, keepdims=True)
    )


def sigmoid(value):
    return 0.5 * jnp.tanh(0.5 * value) + 0.5


def feed(low, gate, up):
    gate_pre, up_pre = dot(low, gate), dot(low, up)
    return gate_pre, up_pre


def hidden_of(gate_pre, up_pre):
    return (gate_pre * sigmoid(gate_pre) * up_pre).astype(bf16)


def feed_back(grad_hidden, gate_pre, up_pre):
    part = sigmoid(gate_pre)
    active = gate_pre * part
    grad_gate = grad_hidden * up_pre * (part + active * (1.0 - part))
    return grad_gate.astype(bf16), (grad_hidden * active).astype(bf16)


def shard_copies(n, plan, refs, buffers, sem):
    copies = []
    for buffer, pieces in zip(buffers, plan[n]):
        row, width = 0, buffer.shape[2]
        for at, first in pieces:
            rows = refs[at].shape[0]
            source = refs[at].at[:, pl.ds(first * width, width)]
            copies.append(start(source, buffer.at[n, pl.ds(row, rows), :], sem.at[n, len(copies)]))
            row += rows
    return copies


def shard_plan(shards):
    args, plan = [], []
    for shard in shards:
        plan.append([])
        for pieces in shard:
            plan[-1].append([(len(args) + n, first) for n, (_, first) in enumerate(pieces)])
            args += [a for a, _ in pieces]
    return args, plan


HALVES = 2


def halves(length):
    return [pl.ds(n * (length // HALVES), length // HALVES) for n in range(HALVES)]


def arrays_of(plan):
    return sum(len(pieces) for shard in plan for pieces in shard)


def feed_shards(plan, shards, weights, coming, low, kept, targets, total, sems):
    buffers, (gates, ups), (sem, out_sem) = weights, kept, sems
    gate, up, down = weights
    hidden, going = down.shape[1], []
    for n in range(len(plan)):
        here = coming
        if n + 1 < len(plan):
            coming = shard_copies(n + 1, plan, shards, buffers, sem)
        for copy in here:
            copy.wait()
        for at in halves(low.shape[0]):
            gate_pre, up_pre = feed(low[at, :], gate[n], up[n])
            gates[n, at, :] = gate_pre.astype(bf16)
            ups[n, at, :] = up_pre.astype(bf16)
            part = dot(hidden_of(gate_pre, up_pre), down[n])
            total[at, :] = part if n == 0 else total[at, :] + part
        cols = pl.ds(n * hidden, hidden)
        for k, (buffer, target) in enumerate(zip(kept, targets)):
            going.append(start(buffer.at[n], target.at[:, cols], out_sem.at[n, k]))
    return going


def first_kernel(plan, gain_ref, shift_ref, own_ref, *refs):
    parts, outs, refs = refs[:4], refs[4:8], refs[8:]
    shards, refs = refs[: arrays_of(plan)], refs[arrays_of(plan) :]
    norm_ref, inverse_ref, low_ref, gates_ref, ups_ref, total_ref = refs[:6]
    own, part_in, out_in, norm1, inverse1, low, total, *weights = refs[6:16]
    kept, sems, (in_sem, res_sem) = refs[16:18], refs[18:20], refs[20:]
    coming = [start(own_ref, own, in_sem.at[8])]
    for n in range(4):
        coming.append(start(parts[n], part_in.at[n], in_sem.at[n]))
        coming.append(start(outs[n], out_in.at[n], in_sem.at[4 + n]))
    first = shard_copies(0, plan, shards, weights, sems[0])
    for copy in coming:
        copy.wait()
    summed = own[...].astype(f32)
    for n in range(4):
        summed = summed + dot(part_in[n], out_in[n])
    norm, inverse = norm_parts(summed)
    norm1[...] = norm
    inverse1[...] = jnp.broadcast_to(inverse, inverse1.shape)
    low[...] = (norm * gain_ref[...] + shift_ref[...]).astype(bf16)
    going = [
        start(source, target, res_sem.at[n])
        for n, (source, target) in enumerate([(low, low_ref), (norm1, norm_ref), (inverse1, inverse_ref)])
    ]
    going += feed_shards(plan, shards, weights, first, low, kept, (gates_ref, ups_ref), total, sems)
    going.append(start(total, total_ref, res_sem.at[3]))
    for copy in going:
        copy.wait()


def last_kernel(plan, low_ref, gain_ref, shift_ref, gain2_ref, shift2_ref, before_ref, norm_ref, cot_ref, *refs):
    shards, refs = refs[: arrays_of(plan)], refs[arrays_of(plan) :]
    gates_ref, ups_ref, encoded_ref, second_ref, low2_ref, small_ref = refs[:6]
    before, norm1, cot_in, total, *weights = refs[6:13]
    kept, sems, in_sem = refs[13:15], refs[15:17], refs[17]
    first = shard_copies(0, plan, shards, weights, sems[0])
    late = [
        start(source, target, in_sem.at[n])
        for n, (source, target) in enumerate([(before_ref, before), (norm_ref, norm1), (cot_ref, cot_in)])
    ]
    going = feed_shards(plan, shards, weights, first, low_ref, kept, (gates_ref, ups_ref), total, sems)
    for copy in late:
        copy.wait()
    normed = norm1[...] * gain_ref[...] + shift_ref[...]
    norm, inverse = norm_parts(normed + (before[...] + total[...]))
    cot = cot_in[...].astype(f32)
    encoded_ref[...] = (norm * gain2_ref[...] + shift2_ref[...]).astype(bf16)
    grad = norm_back(cot * gain2_ref[...], norm, inverse)
    second_ref[...] = grad
    low2_ref[...] = grad.astype(bf16)
    small_ref[...] = jnp.concatenate(
        [jnp.sum(cot * norm, axis=0, keepdims=True), jnp.sum(cot, axis=0, keepdims=True)], axis=0
    )
    for copy in going:
        copy.wait()


def shard_scratch(count, length, width, hidden):
    return [
        pltpu.VMEM((count, width, hidden), bf16),
        pltpu.VMEM((count, width, hidden), bf16),
        pltpu.VMEM((count, hidden, width), bf16),
        pltpu.VMEM((count, length, hidden), bf16),
        pltpu.VMEM((count, length, hidden), bf16),
        pltpu.SemaphoreType.DMA((count, 4)),
        pltpu.SemaphoreType.DMA((count, 2)),
    ]


def forward_first(own, parts, outs, shards, gain, shift):
    length, width = own.shape
    count, hidden = len(shards), sum(a.shape[0] for a, _ in shards[0][2])
    args, plan = shard_plan(shards)
    kept = jax.ShapeDtypeStruct((length, hidden * count), bf16)
    norm = jax.ShapeDtypeStruct((length, width), f32)
    inverse = jax.ShapeDtypeStruct((length, WIDE), f32)
    low = jax.ShapeDtypeStruct((length, width), bf16)
    shapes = [norm, inverse, low, kept, kept, norm]
    vmem = lambda a: pltpu.VMEM(a.shape, a.dtype)
    stack = lambda arrays: pltpu.VMEM((len(arrays), *arrays[0].shape), bf16)
    return pl.pallas_call(
        functools.partial(first_kernel, plan),
        in_specs=[IN_VMEM] * 2 + [ANY] * (9 + len(args)),
        out_specs=[ANY] * len(shapes),
        out_shape=shapes,
        scratch_shapes=[vmem(own), stack(parts), stack(outs), vmem(norm), vmem(inverse), vmem(low), vmem(norm)]
        + shard_scratch(count, length, width, hidden)
        + [pltpu.SemaphoreType.DMA((9,)), pltpu.SemaphoreType.DMA((4,))],
        compiler_params=pltpu.CompilerParams(vmem_limit_bytes=VMEM),
        cost_estimate=SMALL_COST,
        name="feed_first",
    )(gain, shift, own, *parts, *outs, *args)


def forward_last(low, shards, before, norm, cot, vectors):
    length, width = low.shape
    count, hidden = len(shards), sum(a.shape[0] for a, _ in shards[0][2])
    args, plan = shard_plan(shards)
    kept = jax.ShapeDtypeStruct((length, hidden * count), bf16)
    wide = jax.ShapeDtypeStruct((length, width), f32)
    rounded = jax.ShapeDtypeStruct((length, width), bf16)
    small = jax.ShapeDtypeStruct((2, width), f32)
    vmem = lambda a: pltpu.VMEM(a.shape, a.dtype)
    return pl.pallas_call(
        functools.partial(last_kernel, plan),
        in_specs=[IN_VMEM] * 5 + [ANY] * (3 + len(args)),
        out_specs=[ANY] * 2 + [IN_VMEM] * 4,
        out_shape=[kept, kept, rounded, wide, rounded, small],
        scratch_shapes=[vmem(a) for a in (wide, wide, cot, wide)]
        + shard_scratch(count, length, width, hidden)
        + [pltpu.SemaphoreType.DMA((3,))],
        compiler_params=pltpu.CompilerParams(vmem_limit_bytes=VMEM),
        cost_estimate=SMALL_COST,
        name="feed_last",
    )(low, *vectors, before, norm, cot, *args)


def backward_kernel(plan, where, low2_ref, *refs):
    count = len(plan)
    shards, refs = refs[: arrays_of(plan)], refs[arrays_of(plan) :]
    pairs = where[-1][0] + 1
    saved, refs = refs[: 2 * pairs], refs[2 * pairs :]
    late_refs, refs = refs[:7], refs[7:]
    gain_ref, small_in_ref, first_ref, low_ref, *ctx_refs = refs[:8]
    gate, up, down, gates, ups, total, second, norm1, inverse, outs, sem, saved_sem, late_sem = refs[8:]
    buffers = (gate, up, down)
    hidden = down.shape[1]

    def fetch(n):
        part, cols = where[n][0], pl.ds(where[n][1] * hidden, hidden)
        return shard_copies(n, plan, shards, buffers, sem) + [
            start(ref.at[:, cols], buffer.at[n], saved_sem.at[n, k])
            for k, (ref, buffer) in enumerate(zip(saved[2 * part : 2 * part + 2], (gates, ups)))
        ]

    coming = [fetch(0)]
    late = []
    for n in range(count):
        if n + 1 < count:
            coming.append(fetch(n + 1))
        else:
            targets = [second, norm1, inverse] + [outs.at[k] for k in range(4)]
            late = [start(ref, target, late_sem.at[k]) for k, (ref, target) in enumerate(zip(late_refs, targets))]
        for copy in coming[n]:
            copy.wait()
        for at in halves(low2_ref.shape[0]):
            grad_hidden = dot_nt(low2_ref[at, :], down[n])
            grad_gate, grad_up = feed_back(grad_hidden, gates[n, at, :].astype(f32), ups[n, at, :].astype(f32))
            part = dot_nt(grad_gate, gate[n]) + dot_nt(grad_up, up[n])
            total[at, :] = part if n == 0 else total[at, :] + part
    for copy in late:
        copy.wait()
    normed_grad, norm = second[...] + total[...], norm1[...]
    first = norm_back(normed_grad * gain_ref[...], norm, inverse[:, :1])
    first_ref[...] = first
    low = first.astype(bf16)
    low_ref[...] = low
    small = jnp.concatenate(
        [
            jnp.sum(normed_grad * norm, axis=0, keepdims=True),
            jnp.sum(normed_grad, axis=0, keepdims=True),
            small_in_ref[...],
        ],
        axis=0,
    )
    width = outs.shape[1]
    small = jnp.concatenate([small[:, k * width : (k + 1) * width] for k in range(4)], axis=0)
    high = small.astype(bf16)
    small = jnp.concatenate([high, (small - high.astype(f32)).astype(bf16)], axis=0)
    length = low.shape[0]
    for k in range(4):
        ctx_refs[k][:length, :] = dot_nt(low, outs[k]).astype(bf16)
        ctx_refs[k][length:, :] = small


SMALL = 32


def backward(low2, shards, saved, second, norm, inverse, outs, gain, small):
    length, width = low2.shape
    count, hidden = len(shards), sum(a.shape[0] for a, _ in shards[0][2])
    args, plan = shard_plan(shards)
    where = [(n, k) for n, (gates, _) in enumerate(saved) for k in range(gates.shape[1] // hidden)]
    saved = [a for pair in saved for a in pair]
    late = [second, norm, inverse, *outs]
    wide = pltpu.VMEM((length, width), f32)
    return pl.pallas_call(
        functools.partial(backward_kernel, plan, where),
        in_specs=[IN_VMEM] + [ANY] * (len(args) + len(saved) + len(late)) + [IN_VMEM] * 2,
        out_specs=[IN_VMEM] * 6,
        out_shape=[
            jax.ShapeDtypeStruct((length, width), f32),
            jax.ShapeDtypeStruct((length, width), bf16),
        ]
        + [jax.ShapeDtypeStruct((length + SMALL, outs[0].shape[0]), bf16)] * 4,
        scratch_shapes=[
            pltpu.VMEM((count, width, hidden), bf16),
            pltpu.VMEM((count, width, hidden), bf16),
            pltpu.VMEM((count, hidden, width), bf16),
            pltpu.VMEM((count, length, hidden), bf16),
            pltpu.VMEM((count, length, hidden), bf16),
            wide,
            wide,
            wide,
            pltpu.VMEM(inverse.shape, f32),
            pltpu.VMEM((4, *outs[0].shape), bf16),
            pltpu.SemaphoreType.DMA((count, 4)),
            pltpu.SemaphoreType.DMA((count, 2)),
            pltpu.SemaphoreType.DMA((len(late),)),
        ],
        compiler_params=pltpu.CompilerParams(vmem_limit_bytes=VMEM),
        cost_estimate=SMALL_COST,
        name="feed_back",
    )(low2, *args, *saved, *late, gain, small)


def weights_kernel(*refs):
    rows, grads, weights, refs = refs[:4], refs[4:8], refs[8:11], refs[11:]
    target, refs = refs[0], refs[1:]
    gate, up, down, low, low_t, low2, dgate, dup, hidden_t, result, sem, out_sem = refs
    block = rows[0].shape[0]
    at = [pl.ds(n * block, block) for n in range(4)]

    def fetch(n):
        return [
            start(rows[n], low.at[at[n], :], sem.at[n, 0]),
            start(grads[n], low2.at[at[n], :], sem.at[n, 1]),
        ]

    own = [start(weights[0], gate, sem.at[4, 0])]
    coming = [fetch(0)]
    own += [start(weights[k], buffer, sem.at[4 + k, 0]) for k, buffer in ((1, up), (2, down))]
    coming.append(fetch(1))
    for copy in own:
        copy.wait()
    for n in range(4):
        if n + 2 < 4:
            coming.append(fetch(n + 2))
        for copy in coming[n]:
            copy.wait()
        low_t[:, at[n]] = low[at[n], :].T
        for m in range(HALVES):
            part = pl.ds(n * block + m * (block // HALVES), block // HALVES)
            gate_pre, up_pre = feed(low[part, :], gate[...], up[...])
            grad_hidden = dot_nt(low2[part, :], down[...])
            dgate[part, :], dup[part, :] = feed_back(grad_hidden, gate_pre, up_pre)
            hidden_t[:, part] = hidden_of(gate_pre, up_pre).T
    going = []
    for k, (left, right) in enumerate([(low_t, dgate), (low_t, dup), (hidden_t, low2)]):
        result[k] = dot(left[...], right[...]).astype(bf16)
        rows_at = pl.ds(k * result.shape[1], result.shape[1])
        going.append(start(result.at[k], target.at[rows_at, :], out_sem.at[k]))
    for copy in going:
        copy.wait()


def weight_grads(rows, grads, gate, up, down):
    block, width = rows[0].shape
    length, hidden = 4 * block, gate.shape[1]
    return pl.pallas_call(
        weights_kernel,
        in_specs=[ANY] * 11,
        out_specs=ANY,
        out_shape=jax.ShapeDtypeStruct((3 * width, hidden), bf16),
        scratch_shapes=[
            pltpu.VMEM((width, hidden), bf16),
            pltpu.VMEM((width, hidden), bf16),
            pltpu.VMEM((hidden, width), bf16),
            pltpu.VMEM((length, width), bf16),
            pltpu.VMEM((width, length), bf16),
            pltpu.VMEM((length, width), bf16),
            pltpu.VMEM((length, hidden), bf16),
            pltpu.VMEM((length, hidden), bf16),
            pltpu.VMEM((hidden, length), bf16),
            pltpu.VMEM((3, width, hidden), bf16),
            pltpu.SemaphoreType.DMA((7, 2)),
            pltpu.SemaphoreType.DMA((3,)),
        ],
        compiler_params=pltpu.CompilerParams(vmem_limit_bytes=VMEM),
        cost_estimate=SMALL_COST,
        name="feed_weights",
    )(*rows, *grads, gate, up, down)


def local(
    tokens,
    segment_ids,
    query_weight,
    key_weight,
    value_weight,
    output_weight,
    attn_gain,
    attn_shift,
    gate_weight,
    up_weight,
    down_weight,
    mlp_gain,
    mlp_shift,
    cotangent,
):
    own = tokens[0]
    head_width = query_weight.shape[1]
    heads = head_width // HEAD_DIM
    group = lax.axis_size("tensor")
    block = own.shape[0]
    dp = lax.axis_size("dp")
    bits = list(range(int(math.log2(dp))))
    groups = [bits[:1]] + [bits[n : n + 2] for n in range(1, len(bits), 2)]

    near = lambda a: swap(a, "tensor", 1)
    far = lambda a: swap(a, "tensor", 2)

    share = gate_weight.shape[0] // dp
    at = lax.axis_index("dp") * share
    mine = jnp.concatenate(
        [lax.dynamic_slice_in_dim(w, at, share, 0) for w in (gate_weight, up_weight)], axis=1
    )
    far_own = far(own)
    near_own = near(own)
    angle_rate = ROPE_BASE ** (-(jnp.arange(HEAD_DIM // 2, dtype=f32) * 2.0 / HEAD_DIM))
    rates = jnp.concatenate([angle_rate, angle_rate, jnp.zeros(HEAD_DIM, f32)])[None, :]
    me = lax.axis_index("tensor").astype(jnp.int32)[None]
    cosine, sine = rotary_tables(segment_ids, rates, me, block)
    inputs = ([w.T for w in (query_weight, key_weight, value_weight)], segment_ids, cosine, sine, me, heads)
    third = down_weight.shape[0] // 3
    downs = [down_weight[:third], down_weight[third:]]
    near_half = project([after(own, mine, *downs), near_own], 0, *inputs)
    far_own = after(far_own, near_half[0])
    both_own = near(far_own)
    mine = after(mine, far_own)
    far_mine = far(mine)
    near_weights = [near(w) for w in all_after([gate_weight, up_weight, down_weight, output_weight], both_own)]
    most = project([far_own], 2, *inputs, done=near_half)
    x_full, qa, ka, va = project([after(both_own, mine)], 3, *inputs, done=most)
    far_mine, *near_weights = all_after([far_mine, *near_weights], qa)
    near_gate, near_up, near_down, near_out = near_weights
    far_mixed = lax.all_gather(far_mine, "dp", axis=0, tiled=True)
    out_sent, downs[0] = all_after([output_weight, downs[0]], far_mine)
    far_out, early_down = far(out_sent), far(downs[0])
    qa = after(qa, out_sent, downs[0], *near_weights)

    def send(value, j):
        return swap(value[j * block : (j + 1) * block], "tensor", j)

    half = attend(qa, ka, va, 2 * block, 2 * block)
    far_out, early_down = all_after([far_out, early_down], half[0])
    slices = [half[0][j * block : (j + 1) * block] for j in (2, 3)]
    ctx_far = [swap(c, "tensor", j) for c, j in zip(slices, (2, 3))]
    both_out, both_early = near(far_out), near(early_down)
    ctx, qb = attend(after(qa, far_out, early_down, *slices), ka, va, 0, 2 * block, done=half)
    both_out, both_early, *ctx_far = all_after([both_out, both_early, *ctx_far], ctx)
    near_ctx = send(ctx, 1)
    down_sent = after(downs[1], *ctx_far)
    far_down = [early_down, far(down_sent)]
    ctx_parts = [ctx[:block], near_ctx, *ctx_far]
    outs = [output_weight, near_out, far_out, both_out]
    row = lambda a: a[None, :]

    near_shards = [
        ([(gate_weight, 0)], [(up_weight, 0)], [(down_weight, 0)]),
        ([(near_gate, 0)], [(near_up, 0)], [(near_down, 0)]),
    ]
    first_norm, inverse, normed_low, *saved_a, half_way = forward_first(
        after(own, down_sent), ctx_parts, outs, near_shards, row(attn_gain), row(attn_shift)
    )
    near_rows = near(normed_low)
    far_mixed, *far_down = all_after([far_mixed, *far_down], half_way)
    both_mixed, both_down = near(far_mixed), [both_early, near(far_down[1])]
    rows_sent = after(normed_low, half_way)
    far_rows = far(rows_sent)
    shards = near_shards + [
        ([(mixed, 0)], [(mixed, 1)], [(d, 0) for d in down])
        for mixed, down in ((far_mixed, far_down), (both_mixed, both_down))
    ]
    *saved_b, encoded, grad_second, grad_low, small = forward_last(
        after(normed_low, rows_sent),
        shards[2:],
        half_way,
        first_norm,
        cotangent[0],
        (row(attn_gain), row(attn_shift), row(mlp_gain), row(mlp_shift)),
    )
    near_rows, far_rows = all_after([near_rows, far_rows], grad_low)
    both_rows = near(far_rows)
    near_grads, far_grads = near(grad_low), far(grad_low)
    grad_first, grad_attn_low, own_ctx, *sent_ctx = backward(
        after(grad_low, far_rows),
        shards,
        (saved_a, saved_b),
        grad_second,
        first_norm,
        inverse,
        outs,
        row(attn_gain),
        small,
    )
    near_grads, far_grads, both_rows = all_after([near_grads, far_grads, both_rows], grad_first)
    both_grads = near(far_grads)
    got_ctx = [swap(g, "tensor", j + 1) for j, g in enumerate(sent_ctx)]
    grad_feed = weight_grads(
        [after(normed_low, *sent_ctx), near_rows, far_rows, both_rows],
        [grad_low, near_grads, far_grads, both_grads],
        gate_weight,
        up_weight,
        down_weight,
    )
    grad_ctx = all_after(got_ctx, grad_feed)
    feed_part = lax.psum_scatter(after(grad_feed, *grad_ctx), "dp", scatter_dimension=0, tiled=True)
    grad_ctx = [own_ctx, *grad_ctx]
    grad_attn_low = after(grad_attn_low, grad_feed)
    sent = jnp.concatenate([dot_tn(ctx_parts[j], grad_attn_low) for j in (1, 3)], axis=0).astype(bf16)
    got = near(sent)
    kept = [dot_tn(ctx_parts[j], after(grad_attn_low, sent)) for j in (0, 2)]
    small = sum(g[block:].astype(f32) for g in grad_ctx)
    small = (small[: SMALL // 2] + small[SMALL // 2 :]).reshape(4, 4, head_width)
    small = small.transpose(1, 0, 2).reshape(4, -1).astype(bf16)
    got, *kept = all_after([got, *kept])
    sent = (kept[1] + got[head_width:].astype(f32)).astype(bf16)
    kept = kept[0] + got[:head_width].astype(f32)
    got = far(sent)

    dq, dk, dv = attend_back(qb, ka, va, all_after(grad_ctx, small, sent, kept), ctx, cosine, sine)
    grad_out = (kept + after(got, dq).astype(f32)).astype(bf16)
    joint = [dot_tn(g, x_full).astype(bf16) for g in (dq, dk, dv)]
    joint = jnp.concatenate([*joint, grad_out, small], axis=0)
    joint = jnp.pad(joint, ((0, -len(joint) % (8 * dp)), (0, 0)))
    sums = [Sum(split_rows(joint, "dp", groups[0]), groups)]
    parts = all_after([dq, dk, dv], *[s.sent for s in sums])
    weights = [query_weight, key_weight, value_weight]

    def token_part(j):
        return sum(dot_nt(g[j * block : (j + 1) * block], w) for g, w in zip(parts, weights))

    sent = jnp.concatenate([token_part(j).astype(bf16) for j in (1, 3)], axis=0)
    got = near(sent)
    parts = all_after(parts, sent)
    mine, far_sent = token_part(0), token_part(2)
    got, mine, far_sent, feed_part = take_round(sums, got, mine, far_sent, feed_part)
    grad_feed = lax.all_gather(feed_part, "dp", axis=0, tiled=True)
    far_sent = (far_sent + got[block:].astype(f32)).astype(bf16)
    got_rows = far(far_sent)
    mine = grad_first + mine + got[:block].astype(f32)
    (got_rows,) = take_round(sums, got_rows)
    grad_tokens = mine + got_rows.astype(f32)
    while any(s.result is None for s in sums):
        take_round([s for s in sums if s.result is None])
    joint = sums[0].result.astype(f32)
    grad_gate, grad_up, grad_down = jnp.split(grad_feed.astype(f32), 3, axis=0)
    grad_joint = [joint[n * head_width : (n + 1) * head_width] for n in range(4)]
    grad_out = grad_joint.pop()
    small = joint[4 * head_width : 4 * head_width + 4]
    grad_joint = [g.T for g in grad_joint]
    return (
        encoded[None],
        grad_tokens[None],
        *grad_joint,
        grad_out,
        small[0],
        small[1],
        grad_gate,
        grad_up,
        grad_down,
        small[2],
        small[3],
    )


def solution(mesh):
    rows, cols, lead = P("dp", "tensor", None), P(None, "tensor"), P("tensor", None)
    return jax.shard_map(
        local,
        mesh=mesh,
        in_specs=(
            rows, P("dp", None), cols, cols, cols, lead, P(), P(), cols, cols, lead, P(), P(), rows,
        ),
        out_specs=(
            rows, rows, cols, cols, cols, lead, P(), P(), cols, cols, lead, P(), P(),
        ),
        check_vma=False,
    )
```
